32 devices in a mesh: comp: 4 (over x, core), feat: 8 (over z, y).
Axes of the slice: x: 2, y: 2, z: 4, core: 2. Of those that a mesh axis runs over, the one named last changes fastest.
Arguments:
- samples: float32 [1, 192, 28672], P(None, None, 'feat'), may hold values from -20 to 20, as said below
- start_vectors: float32 [256, 28672], P('comp', 'feat'), may hold values from -8 to 8
Outputs:
- vectors: float32 [256, 28672], P('comp', 'feat')
The draws below stay inside these ranges and needn't reach their ends.
Inputs may be any that keep to these rules, and one draw needn't show every extreme that they name: `samples`: activation rows with feature scales that differ over a factor of ten.
All inputs are finite; a program needn't handle non-finite values.
Results may differ from the reference program's by a relative error of at most 0.0001.
Values sent between devices are 32-bit elements; how exact they have to be, the bound alone decides.
No kernel may reach another device: no remote copies, remote signals or barrier semaphores. Data moves between devices by JAX's collectives and lax.ppermute only.
A program may use at most 64 MiB of HBM per device.

```python
import math
import jax
import jax.numpy as jnp
from jax import lax

D = 28672
ROWS = 192
STEPS = 1
COMPONENTS = 256


def draw_samples(key, part):
    key_base, key_rough = jax.random.split(jax.random.fold_in(key, 11), 2)
    position = jnp.arange(D, dtype=jnp.float32) / D
    rough = jax.random.uniform(key_rough, (D,), jnp.float32, 0.6, 1.4)
    scales = 10.0 ** (position - 0.5) * rough
    values = jax.random.normal(key_base, (STEPS, ROWS, D), jnp.float32) * scales
    return jnp.clip(values, -20.0, 20.0)


def draw_start_vectors(key, part):
    key_base, key_rough = jax.random.split(jax.random.fold_in(key, 23), 2)
    position = jnp.arange(D, dtype=jnp.float32) / D
    rough = jax.random.uniform(key_rough, (D,), jnp.float32, 0.5, 1.5)
    values = jax.random.normal(key_base, (COMPONENTS, D), jnp.float32) * 3.0 ** (2.0 * position - 1.0) * rough
    return jnp.clip(values, -8.0, 8.0)


def setup_inputs(seed: int = 0) -> dict:
    streams_of = jax.random.split(jax.random.key(seed), 3)
    return {
        "samples": draw_samples(jax.random.fold_in(streams_of[2], 71), 0),
        "start_vectors": draw_start_vectors(jax.random.fold_in(streams_of[2], 71), 0),
    }


step_rate = 0.1
epsilon = 1e-06
highest = lax.Precision.HIGHEST

def normalize(updated):
    return updated * lax.rsqrt(lax.optimization_barrier(jnp.mean(updated * updated, axis=1, keepdims=True)) + epsilon)

def reference(samples, start_vectors):
    root_width = math.sqrt(D)
    earlier = jnp.arange(COMPONENTS, dtype=jnp.int32)[:, None] < jnp.arange(COMPONENTS, dtype=jnp.int32)[None, :]
    vector = normalize(start_vectors)
    for turn_index in range(STEPS):
        sample = samples[turn_index]
        images = jnp.einsum('rd,kd->rk', sample, vector, precision=highest) / root_width
        intersection = jnp.einsum('rj,ri->ji', images, images, precision=highest) / ROWS
        coupling = jnp.where(earlier, intersection, jnp.float32(0.0))
        penalty = jnp.einsum('ji,jd->id', coupling, vector, precision=highest)
        gradient = root_width * jnp.einsum('rk,rd->kd', images, sample, precision=highest) / ROWS - penalty
        vector = normalize(vector + step_rate * gradient)
    return vector
```

```python
import math

import jax
import jax.numpy as jnp
from jax import lax
from jax.sharding import PartitionSpec as P

step_rate = 0.1
epsilon = 1e-06
high = lax.Precision.HIGH


def earlier_blocks(own, comp):
    cores = 2 if comp % 2 == 0 else 1
    chips = comp // cores
    group = lax.axis_index("comp")
    blocks = [(own, group)]
    if cores == 2:
        swap = [(i, i ^ 1) for i in range(comp)]
    travelling = own
    for step in range(chips):
        if step > 0:
            travelling = lax.ppermute(travelling, "comp", [(i, i + cores) for i in range(comp - cores)])
            blocks.append((travelling, group - step * cores))
        if cores == 2:
            other = lax.ppermute(travelling, "comp", swap)
            blocks.append((other, (group ^ 1) - step * cores))
    return blocks


def shards(samples, start_vectors):
    comp = lax.axis_size("comp")
    feat = lax.axis_size("feat")
    per_group = start_vectors.shape[0]
    sample = samples[0]
    rows = sample.shape[0]
    features = sample.shape[1] * feat
    total = per_group * comp
    root_width = math.sqrt(features)
    group = lax.axis_index("comp")

    blocks = earlier_blocks(start_vectors, comp)

    raw = jnp.einsum("kd,rd->kr", start_vectors, sample, precision=high)
    squares = jnp.sum(start_vectors * start_vectors, axis=1, keepdims=True)
    partial = jnp.concatenate([raw, squares], axis=1)
    share = -(-per_group // feat)
    partial = jnp.pad(partial, ((0, share * feat - per_group), (0, 0)))
    pieces = lax.all_to_all(partial, "feat", split_axis=0, concat_axis=0, tiled=True)
    summed = jnp.sum(pieces.reshape(feat, share, rows + 1), axis=0)
    everything = lax.all_gather(summed, ("comp", "feat"), axis=0, tiled=True)
    everything = everything.reshape(comp, share * feat, rows + 1)[:, :per_group].reshape(total, rows + 1)

    scale = lax.rsqrt(everything[:, rows:] / features + epsilon)
    images = everything[:, :rows] * (scale / root_width)
    own_images = lax.dynamic_slice_in_dim(images, group * per_group, per_group, 0)
    own_scale = lax.dynamic_slice_in_dim(scale, group * per_group, per_group, 0)
    intersection = jnp.einsum("ir,jr->ij", own_images, images, precision=lax.Precision.HIGHEST) / rows
    own_rows = group * per_group + jnp.arange(per_group, dtype=jnp.int32)
    coupling = jnp.where(
        jnp.arange(total, dtype=jnp.int32)[None, :] < own_rows[:, None], intersection * scale[:, 0][None, :], 0.0
    )

    updated = own_scale * start_vectors + (step_rate * root_width / rows) * jnp.einsum(
        "kr,rd->kd", own_images, sample, precision=high
    )
    for block, owner in blocks:
        part = lax.dynamic_slice_in_dim(coupling, jnp.maximum(owner, 0) * per_group, per_group, 1)
        part = jnp.where(owner >= 0, part, 0.0)
        updated = updated - step_rate * jnp.einsum("ij,jd->id", part, block, precision=high)

    norms = jnp.broadcast_to(jnp.sum(updated * updated, axis=1), (feat, per_group))
    sums = lax.all_to_all(norms, "feat", split_axis=0, concat_axis=0, tiled=True)
    return updated * lax.rsqrt(jnp.sum(sums, axis=0) / features + epsilon)[:, None]


def solution(mesh):
    in_specs = (P(None, None, "feat"), P("comp", "feat"))
    out_specs = P("comp", "feat")
    return jax.shard_map(shards, mesh=mesh, in_specs=in_specs, out_specs=out_specs, check_vma=False)
```

```python
import math

import jax
import jax.numpy as jnp
from jax import lax
from jax.sharding import PartitionSpec as P

step_rate = 0.1
epsilon = 1e-06
high = lax.Precision.HIGH


def partner(index, step, size):
    if size & (size - 1) == 0:
        return index ^ step
    return (index + step) % size


def source(index, step, size):
    if size & (size - 1) == 0:
        return index ^ step
    return (index - step) % size


def swap_all(pieces, axis):
    size = lax.axis_size(axis)
    return [pieces[0]] + [
        lax.ppermute(pieces[step], axis, [(i, partner(i, step, size)) for i in range(size)]) for step in range(1, size)
    ]


def earlier_blocks(own, comp):
    cores = 2 if comp % 2 == 0 else 1
    chips = comp // cores
    group = lax.axis_index("comp")
    blocks = [(own, group)]
    if cores == 2:
        swap = [(i, i ^ 1) for i in range(comp)]
    travelling = own
    for step in range(chips):
        if step > 0:
            travelling = lax.ppermute(travelling, "comp", [(i, i + cores) for i in range(comp - cores)])
            blocks.append((travelling, group - step * cores))
        if cores == 2:
            other = lax.ppermute(travelling, "comp", swap)
            blocks.append((other, (group ^ 1) - step * cores))
    return blocks


def shards(samples, start_vectors):
    comp = lax.axis_size("comp")
    feat = lax.axis_size("feat")
    per_group = start_vectors.shape[0]
    sample = samples[0]
    rows = sample.shape[0]
    features = sample.shape[1] * feat
    root_width = math.sqrt(features)
    group = lax.axis_index("comp")
    place = lax.axis_index("feat")

    blocks = earlier_blocks(start_vectors, comp)

    raw = jnp.einsum("kd,rd->kr", start_vectors, sample, precision=high)
    squares = jnp.sum(start_vectors * start_vectors, axis=1, keepdims=True)
    partial = jnp.concatenate([raw, squares], axis=1)
    share = -(-per_group // feat)
    partial = jnp.pad(partial, ((0, share * feat - per_group), (0, 0)))
    pieces = [
        lax.dynamic_slice_in_dim(partial, partner(place, step, feat) * share, share, 0) for step in range(feat)
    ]
    summed = sum(swap_all(pieces, "feat"))
    gathered = jnp.zeros((share * feat, rows + 1), jnp.float32)
    for step, piece in enumerate(swap_all([summed] * feat, "feat")):
        gathered = lax.dynamic_update_slice_in_dim(gathered, piece, source(place, step, feat) * share, 0)
    gathered = gathered[:per_group]

    def scaled(block):
        scale = lax.rsqrt(block[:, rows:] / features + epsilon)
        return block[:, :rows] * (scale / root_width), scale

    own_images, own_scale = scaled(gathered)
    updated = own_scale * start_vectors + (step_rate * root_width / rows) * jnp.einsum(
        "kr,rd->kd", own_images, sample, precision=high
    )
    own_rows = jnp.arange(per_group, dtype=jnp.int32)[:, None]
    other_rows = jnp.arange(per_group, dtype=jnp.int32)[None, :]
    for (projected, owner), (block, _) in zip(earlier_blocks(gathered, comp), blocks):
        images, scale = scaled(projected)
        intersection = jnp.einsum("ir,jr->ij", own_images, images, precision=lax.Precision.HIGHEST) / rows
        earlier = (owner >= 0) & (owner * per_group + other_rows < group * per_group + own_rows)
        coupling = jnp.where(earlier, intersection * scale[:, 0][None, :], 0.0)
        updated = updated - step_rate * jnp.einsum("ij,jd->id", coupling, block, precision=high)

    sums = swap_all([jnp.sum(updated * updated, axis=1)] * feat, "feat")
    return updated * lax.rsqrt(sum(sums) / features + epsilon)[:, None]


def solution(mesh):
    in_specs = (P(None, None, "feat"), P("comp", "feat"))
    out_specs = P("comp", "feat")
    return jax.shard_map(shards, mesh=mesh, in_specs=in_specs, out_specs=out_specs, check_vma=False)
```

```python
import functools

import jax
import jax.numpy as jnp
from jax import lax
from jax.experimental import pallas as pl
from jax.experimental.pallas import tpu as pltpu
from jax.sharding import PartitionSpec as P

step_rate = 0.1
epsilon = 1e-06
lanes = 128


def tile_of(columns):
    if columns % lanes:
        return columns
    units = columns // lanes
    return lanes * max(u for u in range(1, 8) if units % u == 0)


def halves(array):
    top = array.astype(jnp.bfloat16)
    return top, (array - top.astype(jnp.float32)).astype(jnp.bfloat16)


def product(left, right, transposed=False):
    dims = (((1,), (1 if transposed else 0,)), ((), ()))
    dot = functools.partial(lax.dot_general, dimension_numbers=dims, preferred_element_type=jnp.float32)
    left_top, left_rest = halves(left)
    right_top, right_rest = halves(right)
    return dot(left_top, right_top) + (dot(left_top, right_rest) + dot(left_rest, right_top))


def project_kernel(x_ref, s_ref, out_ref):
    x, s = x_ref[...], s_ref[...]
    rows = s.shape[0]
    projected = product(x, s, transposed=True)
    squares = jnp.broadcast_to(jnp.sum(x * x, axis=1, keepdims=True), (x.shape[0], out_ref.shape[1] - rows))

    @pl.when(pl.program_id(0) == 0)
    def _():
        out_ref[:, :rows] = projected
        out_ref[:, rows:] = squares

    @pl.when(pl.program_id(0) > 0)
    def _():
        out_ref[:, :rows] += projected
        out_ref[:, rows:] += squares


def project(x, sample):
    per_group, columns = x.shape
    rows = sample.shape[0]
    width = -(-(rows + 1) // lanes) * lanes
    tile = tile_of(columns)
    return pl.pallas_call(
        project_kernel,
        grid=(columns // tile,),
        in_specs=[pl.BlockSpec((per_group, tile), lambda i: (0, i)), pl.BlockSpec((rows, tile), lambda i: (0, i))],
        out_specs=pl.BlockSpec((per_group, width), lambda i: (0, 0)),
        out_shape=jax.ShapeDtypeStruct((per_group, width), jnp.float32),
        name="project",
    )(x, sample)


def scale_of(block, rows, features):
    return lax.rsqrt(block[:, rows : rows + 1] / features + epsilon)


def own_kernel(features, p_ref, x_ref, s_ref, out_ref):
    rows = s_ref.shape[0]
    per_group = x_ref.shape[0]
    scale = scale_of(p_ref[...], rows, features)
    images = p_ref[:, :rows] * scale
    shared = product(images, images * scale, transposed=True)
    later = lax.broadcasted_iota(jnp.int32, shared.shape, 0)
    earlier = lax.broadcasted_iota(jnp.int32, shared.shape, 1)
    coupling = jnp.where(earlier < later, shared * (-step_rate / (features * rows)), 0.0)
    x = x_ref[...]
    out_ref[...] = scale * x + (product(images * (step_rate / rows), s_ref[...]) + product(coupling, x))


def own_part(projected, x, sample, features):
    per_group, columns = x.shape
    rows = sample.shape[0]
    tile = tile_of(columns)
    return pl.pallas_call(
        functools.partial(own_kernel, features),
        grid=(columns // tile,),
        in_specs=[
            pl.BlockSpec(projected.shape, lambda i: (0, 0)),
            pl.BlockSpec((per_group, tile), lambda i: (0, i)),
            pl.BlockSpec((rows, tile), lambda i: (0, i)),
        ],
        out_specs=pl.BlockSpec((per_group, tile), lambda i: (0, i)),
        out_shape=jax.ShapeDtypeStruct(x.shape, jnp.float32),
        name="own_part",
    )(projected, x, sample)


def others_kernel(features, rows, count, flags_ref, t_ref, p_ref, *refs):
    projected_refs, x_refs, out_ref, squares_ref, total = (*[refs[: count], refs[count : 2 * count]], *refs[2 * count :])
    per_group = t_ref.shape[0]
    images = p_ref[:, :rows] * (scale_of(p_ref[...], rows, features) * (-step_rate / (features * rows)))
    updated = t_ref[...]
    others = []
    for k in range(count):
        scale = scale_of(projected_refs[k][...], rows, features)
        others.append(projected_refs[k][:, :rows] * (scale * scale * flags_ref[k]))
    coupling = product(images, jnp.concatenate(others, axis=0), transposed=True)
    updated += product(coupling, jnp.concatenate([x_ref[...] for x_ref in x_refs], axis=0))
    out_ref[...] = updated
    squares = jnp.sum(updated * updated, axis=1, keepdims=True)

    @pl.when(pl.program_id(0) == 0)
    def _():
        total[...] = squares

    @pl.when(pl.program_id(0) > 0)
    def _():
        total[...] += squares

    @pl.when(pl.program_id(0) == pl.num_programs(0) - 1)
    def _():
        down = lax.broadcasted_iota(jnp.int32, (per_group, per_group), 0)
        across = lax.broadcasted_iota(jnp.int32, (per_group, per_group), 1)
        spread = jnp.broadcast_to(total[...], (per_group, per_group))
        squares_ref[...] = jnp.sum(jnp.where(down == across, spread, 0.0), axis=0, keepdims=True)


def others_part(flags, partly, projected, others, blocks, rows, features):
    per_group, columns = partly.shape
    count = len(blocks)
    tile = tile_of(columns)
    whole = pl.BlockSpec(projected.shape, lambda i: (0, 0))
    tiled = pl.BlockSpec((per_group, tile), lambda i: (0, i))
    return pl.pallas_call(
        functools.partial(others_kernel, features, rows, count),
        grid=(columns // tile,),
        in_specs=[pl.BlockSpec(memory_space=pltpu.SMEM), tiled, whole] + [whole] * count + [tiled] * count,
        out_specs=[tiled, pl.BlockSpec((1, per_group), lambda i: (0, 0))],
        out_shape=[
            jax.ShapeDtypeStruct(partly.shape, jnp.float32),
            jax.ShapeDtypeStruct((1, per_group), jnp.float32),
        ],
        scratch_shapes=[pltpu.VMEM((per_group, 1), jnp.float32)],
        name="others_part",
    )(flags, partly, projected, *others, *blocks)


def exchange(array, axis, step):
    return lax.ppermute(array, axis, [(i, i ^ step) for i in range(lax.axis_size(axis))])


def add_up(array, axis):
    size = lax.axis_size(axis)
    if size & (size - 1):
        return lax.psum(array, axis)
    step = 1
    while step < size:
        array = array + exchange(array, axis, step)
        step *= 2
    return array


def gather(own, size):
    if size & (size - 1):
        arrays = lax.all_gather(own, "comp")
        group = lax.axis_index("comp")
        return [arrays[(group + k) % size] for k in range(1, size)]
    across = [own] + [exchange(own, "comp", step) for step in range(2, size, 2)]
    beside = [exchange(array, "comp", 1) for array in across] if size > 1 else []
    return across[1:] + beside


def owners(size):
    group = lax.axis_index("comp")
    if size & (size - 1):
        return [(group + k) % size for k in range(1, size)]
    return [group ^ step for step in range(2, size, 2)] + [group ^ (step + 1) for step in range(0, size, 2)]


def shards(samples, start_vectors):
    comp = lax.axis_size("comp")
    feat = lax.axis_size("feat")
    sample = samples[0]
    rows = sample.shape[0]
    features = sample.shape[1] * feat
    group = lax.axis_index("comp")

    blocks = gather(start_vectors, comp)
    projected = add_up(project(start_vectors, sample), "feat")
    others = gather(projected, comp)
    partly = own_part(projected, start_vectors, sample, features)
    flags = (jnp.stack(owners(comp)) < group).astype(jnp.float32)
    updated, squares = others_part(flags, partly, projected, others, blocks, rows, features)
    squares = add_up(squares, "feat")[0]
    return updated * lax.rsqrt(squares / features + epsilon)[:, None]


def solution(mesh):
    in_specs = (P(None, None, "feat"), P("comp", "feat"))
    out_specs = P("comp", "feat")
    return jax.shard_map(shards, mesh=mesh, in_specs=in_specs, out_specs=out_specs, check_vma=False)
```

```python
import functools

import jax
import jax.numpy as jnp
from jax import lax
from jax.experimental import pallas as pl
from jax.experimental.pallas import tpu as pltpu
from jax.sharding import PartitionSpec as P

step_rate = 0.1
epsilon = 1e-06
lanes = 128
in_vmem = pl.BlockSpec(memory_space=pltpu.VMEM)


def tile_of(columns, most):
    if columns % lanes:
        return columns
    units = columns // lanes
    return lanes * max(u for u in range(1, most + 1) if units % u == 0)


def halves(array):
    top = array.astype(jnp.bfloat16)
    return top, (array - top.astype(jnp.float32)).astype(jnp.bfloat16)


def product(left, right, transposed=False):
    dims = (((1,), (1 if transposed else 0,)), ((), ()))
    dot = functools.partial(lax.dot_general, dimension_numbers=dims, preferred_element_type=jnp.float32)
    left_top, left_rest = left if isinstance(left, tuple) else halves(left)
    right_top, right_rest = halves(right)
    rows = left_top.shape[0]
    both = dot(jnp.concatenate([left_top, left_rest], axis=0), right_top)
    return both[:rows] + (both[rows:] + dot(left_top, right_rest))


def scale_of(squares, features):
    return lax.rsqrt(squares / features + epsilon)


def loop(columns, most, body, init):
    tile = tile_of(columns, most)
    return lax.fori_loop(0, columns // tile, lambda i, c: body(pl.ds(pl.multiple_of(i * tile, tile), tile), c), init)


def project_kernel(x_ref, s_ref, out_ref):
    per_group, columns = x_ref.shape
    rows = s_ref.shape[0]

    def body(here, carry):
        x = x_ref[:, here]
        projected, squares = carry
        projected += product(x, s_ref[:, here], transposed=True)
        return projected, squares + jnp.sum(x * x, axis=1, keepdims=True)

    zeros = jnp.zeros((per_group, rows), jnp.float32), jnp.zeros((per_group, 1), jnp.float32)
    projected, squares = loop(columns, 4, body, zeros)
    out_ref[:, :rows] = projected
    out_ref[:, rows:] = jnp.broadcast_to(squares, (per_group, out_ref.shape[1] - rows))


def project(x, sample):
    per_group = x.shape[0]
    rows = sample.shape[0]
    width = -(-(rows + 1) // lanes) * lanes
    return pl.pallas_call(
        project_kernel,
        in_specs=[in_vmem, in_vmem],
        out_specs=in_vmem,
        out_shape=jax.ShapeDtypeStruct((per_group, width), jnp.float32),
        name="project",
    )(x, sample)


def own_kernel(features, p_ref, x_ref, s_ref, out_ref):
    rows = s_ref.shape[0]
    scale = scale_of(p_ref[:, rows : rows + 1], features)
    images = p_ref[:, :rows] * scale
    shared = product(images, images * scale, transposed=True)
    later = lax.broadcasted_iota(jnp.int32, shared.shape, 0)
    earlier = lax.broadcasted_iota(jnp.int32, shared.shape, 1)
    coupling = halves(jnp.where(earlier < later, shared * (-step_rate / (features * rows)), 0.0))
    images = halves(images * (step_rate / rows))

    def body(here, carry):
        x = x_ref[:, here]
        out_ref[:, here] = scale * x + (product(images, s_ref[:, here]) + product(coupling, x))
        return carry

    loop(x_ref.shape[1], 4, body, 0)


def own_part(projected, x, sample, features):
    return pl.pallas_call(
        functools.partial(own_kernel, features),
        in_specs=[in_vmem] * 3,
        out_specs=in_vmem,
        out_shape=jax.ShapeDtypeStruct(x.shape, jnp.float32),
        name="own_part",
    )(projected, x, sample)


def diagonal(count):
    down = lax.broadcasted_iota(jnp.int32, (count, count), 0)
    across = lax.broadcasted_iota(jnp.int32, (count, count), 1)
    return down == across


def others_kernel(features, rows, count, flags_ref, t_ref, p_ref, *refs):
    projected_refs, x_refs = refs[:count], refs[count : 2 * count]
    out_ref, squares_ref = refs[2 * count :]
    per_group, columns = t_ref.shape
    images = p_ref[:, :rows] * (scale_of(p_ref[:, rows : rows + 1], features) * (-step_rate / (features * rows)))
    others = []
    for k in range(count):
        scale = scale_of(projected_refs[k][:, rows : rows + 1], features)
        others.append(projected_refs[k][:, :rows] * (scale * scale * flags_ref[k]))
    coupling = halves(product(images, jnp.concatenate(others, axis=0), transposed=True))

    def body(here, squares):
        updated = t_ref[:, here] + product(coupling, jnp.concatenate([x_ref[:, here] for x_ref in x_refs], axis=0))
        out_ref[:, here] = updated
        return squares + jnp.sum(updated * updated, axis=1, keepdims=True)

    squares = loop(columns, 4, body, jnp.zeros((per_group, 1), jnp.float32))
    spread = jnp.broadcast_to(squares, (per_group, per_group))
    squares_ref[...] = jnp.sum(jnp.where(diagonal(per_group), spread, 0.0), axis=0, keepdims=True)


def others_part(flags, partly, projected, others, blocks, rows, features):
    count = len(blocks)
    return pl.pallas_call(
        functools.partial(others_kernel, features, rows, count),
        in_specs=[pl.BlockSpec(memory_space=pltpu.SMEM)] + [in_vmem] * (2 + 2 * count),
        out_specs=[in_vmem, in_vmem],
        out_shape=[
            jax.ShapeDtypeStruct(partly.shape, jnp.float32),
            jax.ShapeDtypeStruct((1, partly.shape[0]), jnp.float32),
        ],
        name="others_part",
    )(flags, partly, projected, *others, *blocks)


def finish_kernel(features, count, updated_ref, *refs):
    squares_refs, (out_ref, scaled, sems) = refs[:count], refs[count:]
    per_group, columns = updated_ref.shape
    squares = squares_refs[0][...]
    for ref in squares_refs[1:]:
        squares += ref[...]
    spread = jnp.broadcast_to(scale_of(squares, features), (per_group, per_group))
    scale = jnp.sum(jnp.where(diagonal(per_group), spread, 0.0), axis=1, keepdims=True)
    tile = tile_of(columns, 7)
    copies = []
    for i in range(columns // tile):
        here = pl.ds(i * tile, tile)
        scaled[:, here] = updated_ref[:, here] * scale
        copies.append(pltpu.make_async_copy(scaled.at[:, here], out_ref.at[:, here], sems.at[i]))
        copies[-1].start()
    for copy in copies:
        copy.wait()


def finish(updated, squares, features):
    count = len(squares)
    return pl.pallas_call(
        functools.partial(finish_kernel, features, count),
        in_specs=[in_vmem] * (1 + count),
        out_specs=pl.BlockSpec(memory_space=pl.ANY),
        out_shape=jax.ShapeDtypeStruct(updated.shape, jnp.float32),
        scratch_shapes=[
            pltpu.VMEM(updated.shape, jnp.float32),
            pltpu.SemaphoreType.DMA((updated.shape[1] // tile_of(updated.shape[1], 7),)),
        ],
        name="finish",
    )(updated, *squares)


def exchange(array, axis, step):
    return lax.ppermute(array, axis, [(i, i ^ step) for i in range(lax.axis_size(axis))])


def terms(array, axis, together):
    size = lax.axis_size(axis)
    if size & (size - 1):
        return [lax.psum(array, axis)]
    parts, step, bits = [array], 1, (size.bit_length() - 1) % together or together
    while step < size:
        array = sum(parts[1:], parts[0])
        parts = [array] + [exchange(array, axis, step * k) for k in range(1, 1 << bits)]
        step <<= bits
        bits = together
    return parts


def gather(own, size):
    if size & (size - 1):
        arrays = lax.all_gather(own, "comp")
        group = lax.axis_index("comp")
        return [arrays[(group + step) % size] for step in range(1, size)]
    return [exchange(own, "comp", step) for step in range(1, size)]


def owners(size):
    group = lax.axis_index("comp")
    steps = jnp.arange(1, size, dtype=jnp.int32)
    return (group + steps) % size if size & (size - 1) else group ^ steps


def shards(samples, start_vectors):
    comp = lax.axis_size("comp")
    feat = lax.axis_size("feat")
    sample = samples[0]
    rows = sample.shape[0]
    features = sample.shape[1] * feat
    flags = (owners(comp) < lax.axis_index("comp")).astype(jnp.float32)

    straight = {step: exchange(start_vectors, "comp", step) for step in range(1, comp) if step % 2 == 0 or step == 1}
    parts = terms(project(start_vectors, sample), "feat", 1)
    projected = sum(parts[1:], parts[0])
    others = gather(projected, comp)
    partly = own_part(projected, start_vectors, sample, features)
    blocks = []
    for step in range(1, comp):
        if step in straight:
            blocks.append(straight[step])
        else:
            arrived, partly, others = lax.optimization_barrier((straight[step - 1], partly, others))
            blocks.append(exchange(arrived, "comp", 1))
    updated, squares = others_part(flags, partly, projected, others, blocks, rows, features)
    return finish(updated, terms(squares, "feat", 2), features)


def solution(mesh):
    in_specs = (P(None, None, "feat"), P("comp", "feat"))
    out_specs = P("comp", "feat")
    return jax.shard_map(shards, mesh=mesh, in_specs=in_specs, out_specs=out_specs, check_vma=False)
```

```python
import functools

import jax
import jax.numpy as jnp
from jax import lax
from jax.experimental import pallas as pl
from jax.experimental.pallas import tpu as pltpu
from jax.sharding import PartitionSpec as P

step_rate = 0.1
epsilon = 1e-06
lanes = 128
in_vmem = pl.BlockSpec(memory_space=pltpu.VMEM)
params = pltpu.CompilerParams(vmem_limit_bytes=16 << 20)


def tile_of(columns, most):
    if columns % lanes:
        return columns
    units = columns // lanes
    return lanes * max(u for u in range(1, most + 1) if units % u == 0)


def halves(array):
    top = array.astype(jnp.bfloat16)
    return top, (array - top.astype(jnp.float32)).astype(jnp.bfloat16)


def product(left, right, transposed=False):
    dims = (((1,), (1 if transposed else 0,)), ((), ()))
    dot = functools.partial(lax.dot_general, dimension_numbers=dims, preferred_element_type=jnp.float32)
    left_top, left_rest = left if isinstance(left, tuple) else halves(left)
    right_top, right_rest = halves(right)
    rows = left_top.shape[0]
    both = dot(jnp.concatenate([left_top, left_rest], axis=0), right_top)
    return both[:rows] + (both[rows:] + dot(left_top, right_rest))


def scale_of(squares, features):
    return lax.rsqrt(squares / features + epsilon)


def loop(columns, most, body, init):
    tile = tile_of(columns, most)
    return lax.fori_loop(0, columns // tile, lambda i, c: body(pl.ds(pl.multiple_of(i * tile, tile), tile), c), init)


def project_kernel(x_ref, s_ref, out_ref):
    per_group, columns = x_ref.shape
    rows = s_ref.shape[0]

    def body(here, carry):
        x = x_ref[:, here]
        projected, squares = carry
        projected += product(x, s_ref[:, here], transposed=True)
        return projected, squares + jnp.sum(x * x, axis=1, keepdims=True)

    zeros = jnp.zeros((per_group, rows), jnp.float32), jnp.zeros((per_group, 1), jnp.float32)
    projected, squares = loop(columns, 4, body, zeros)
    out_ref[:, :rows] = projected
    out_ref[:, rows:] = jnp.broadcast_to(squares, (per_group, out_ref.shape[1] - rows))


def project(x, sample):
    per_group = x.shape[0]
    rows = sample.shape[0]
    width = -(-(rows + 1) // lanes) * lanes
    return pl.pallas_call(
        project_kernel,
        in_specs=[in_vmem, in_vmem],
        out_specs=in_vmem,
        out_shape=jax.ShapeDtypeStruct((per_group, width), jnp.float32),
        compiler_params=params,
        cost_estimate=pl.CostEstimate(flops=1024, bytes_accessed=1024, transcendentals=0),
        name="project",
    )(x, sample)


def own_kernel(features, p_ref, x_ref, s_ref, out_ref):
    rows = s_ref.shape[0]
    scale = scale_of(p_ref[:, rows : rows + 1], features)
    images = p_ref[:, :rows] * scale
    shared = product(images, images * scale, transposed=True)
    later = lax.broadcasted_iota(jnp.int32, shared.shape, 0)
    earlier = lax.broadcasted_iota(jnp.int32, shared.shape, 1)
    coupling = jnp.where(earlier < later, shared * (-step_rate / (features * rows)), 0.0)
    weights = halves(jnp.concatenate([images * (step_rate / rows), coupling], axis=1))

    def body(here, carry):
        x = x_ref[:, here]
        out_ref[:, here] = scale * x + product(weights, jnp.concatenate([s_ref[:, here], x], axis=0))
        return carry

    loop(x_ref.shape[1], 4, body, 0)


def own_part(projected, x, sample, features):
    return pl.pallas_call(
        functools.partial(own_kernel, features),
        in_specs=[in_vmem] * 3,
        out_specs=in_vmem,
        out_shape=jax.ShapeDtypeStruct(x.shape, jnp.float32),
        compiler_params=params,
        cost_estimate=pl.CostEstimate(flops=1024, bytes_accessed=1024, transcendentals=0),
        name="own_part",
    )(projected, x, sample)


def diagonal(count):
    down = lax.broadcasted_iota(jnp.int32, (count, count), 0)
    across = lax.broadcasted_iota(jnp.int32, (count, count), 1)
    return down == across


def owner(group, step, size):
    return (group + step) % size if size & (size - 1) else group ^ step


def others_kernel(features, rows, count, t_ref, p_ref, *refs):
    projected_refs, x_refs = refs[:count], refs[count : 2 * count]
    out_ref, squares_ref = refs[2 * count :]
    per_group, columns = t_ref.shape
    images = p_ref[:, :rows] * (scale_of(p_ref[:, rows : rows + 1], features) * (-step_rate / (features * rows)))
    group = lax.axis_index("comp")
    others = []
    for k in range(count):
        earlier = (owner(group, k + 1, count + 1) < group).astype(jnp.float32)
        scale = scale_of(projected_refs[k][:, rows : rows + 1], features)
        others.append(projected_refs[k][:, :rows] * (scale * scale * earlier))
    coupling = halves(product(images, jnp.concatenate(others, axis=0), transposed=True))

    def body(here, squares):
        updated = t_ref[:, here] + product(coupling, jnp.concatenate([x_ref[:, here] for x_ref in x_refs], axis=0))
        out_ref[:, here] = updated
        return squares + jnp.sum(updated * updated, axis=1, keepdims=True)

    squares = loop(columns, 4, body, jnp.zeros((per_group, 1), jnp.float32))
    spread = jnp.broadcast_to(squares, (per_group, per_group))
    squares_ref[...] = jnp.sum(jnp.where(diagonal(per_group), spread, 0.0), axis=0, keepdims=True)


def others_part(partly, projected, others, blocks, rows, features):
    count = len(blocks)
    return pl.pallas_call(
        functools.partial(others_kernel, features, rows, count),
        in_specs=[in_vmem] * (2 + 2 * count),
        out_specs=[in_vmem, in_vmem],
        out_shape=[
            jax.ShapeDtypeStruct(partly.shape, jnp.float32),
            jax.ShapeDtypeStruct((1, partly.shape[0]), jnp.float32),
        ],
        compiler_params=params,
        cost_estimate=pl.CostEstimate(flops=1024, bytes_accessed=1024, transcendentals=0),
        name="others_part",
    )(partly, projected, *others, *blocks)


def finish_kernel(features, count, updated_ref, *refs):
    squares_refs, (out_ref, scaled, sems) = refs[:count], refs[count:]
    per_group, columns = updated_ref.shape
    squares = squares_refs[0][...]
    for ref in squares_refs[1:]:
        squares += ref[...]
    spread = jnp.broadcast_to(scale_of(squares, features), (per_group, per_group))
    scale = jnp.sum(jnp.where(diagonal(per_group), spread, 0.0), axis=1, keepdims=True)
    tile = tile_of(columns, 7)
    copies = []
    for i in range(columns // tile):
        here = pl.ds(i * tile, tile)
        scaled[:, here] = updated_ref[:, here] * scale
        copies.append(pltpu.make_async_copy(scaled.at[:, here], out_ref.at[:, here], sems.at[i]))
        copies[-1].start()
    for copy in copies:
        copy.wait()


def finish(updated, squares, features):
    count = len(squares)
    return pl.pallas_call(
        functools.partial(finish_kernel, features, count),
        in_specs=[in_vmem] * (1 + count),
        out_specs=pl.BlockSpec(memory_space=pl.ANY),
        out_shape=jax.ShapeDtypeStruct(updated.shape, jnp.float32),
        scratch_shapes=[
            pltpu.VMEM(updated.shape, jnp.float32),
            pltpu.SemaphoreType.DMA((updated.shape[1] // tile_of(updated.shape[1], 7),)),
        ],
        compiler_params=params,
        cost_estimate=pl.CostEstimate(flops=1024, bytes_accessed=1024, transcendentals=0),
        name="finish",
    )(updated, *squares)


def exchange(array, axis, step):
    return lax.ppermute(array, axis, [(i, i ^ step) for i in range(lax.axis_size(axis))])


def terms(array, axis, together):
    size = lax.axis_size(axis)
    if size & (size - 1):
        return [lax.psum(array, axis)]
    parts, step, bits = [array], 1, (size.bit_length() - 1) % together or together
    while step < size:
        array = sum(parts[1:], parts[0])
        parts = [array] + [exchange(array, axis, step * k) for k in range(1, 1 << bits)]
        step <<= bits
        bits = together
    return parts


def gather(own, size):
    if size & (size - 1):
        arrays = lax.all_gather(own, "comp")
        group = lax.axis_index("comp")
        return [arrays[owner(group, step, size)] for step in range(1, size)]
    return [exchange(own, "comp", step) for step in range(1, size)]


def shards(samples, start_vectors):
    comp = lax.axis_size("comp")
    feat = lax.axis_size("feat")
    sample = samples[0]
    rows = sample.shape[0]
    features = sample.shape[1] * feat
    even = comp & (comp - 1) == 0
    straight = {}
    for step in range(1, comp):
        if even and (step == 1 or step % 2 == 0):
            straight[step] = exchange(start_vectors, "comp", step)
    parts = terms(project(start_vectors, sample), "feat", 1)
    projected = sum(parts[1:], parts[0])
    others = gather(projected, comp)
    blocks = [] if even else gather(start_vectors, comp)
    own = projected
    for step in range(1, comp if even else 1):
        if step in straight:
            blocks.append(straight[step])
        else:
            arrived, others[0], own = lax.optimization_barrier((straight[step - 1], others[0], own))
            blocks.append(exchange(arrived, "comp", 1))
    partly = own_part(own, start_vectors, sample, features)
    updated, squares = others_part(partly, projected, others, blocks, rows, features)
    return finish(updated, terms(squares, "feat", 2), features)


def solution(mesh):
    in_specs = (P(None, None, "feat"), P("comp", "feat"))
    out_specs = P("comp", "feat")
    return jax.shard_map(shards, mesh=mesh, in_specs=in_specs, out_specs=out_specs, check_vma=False)
```

```python
import functools

import jax
import jax.numpy as jnp
from jax import lax
from jax.experimental import pallas as pl
from jax.experimental.pallas import tpu as pltpu
from jax.sharding import PartitionSpec as P

step_rate = 0.1
epsilon = 1e-06
lanes = 128
in_vmem = pl.BlockSpec(memory_space=pltpu.VMEM)
anywhere = pl.BlockSpec(memory_space=pl.ANY)
params = pltpu.CompilerParams(vmem_limit_bytes=16 << 20)


def tile_of(columns, most):
    if columns % lanes:
        return columns
    units = columns // lanes
    return lanes * max(u for u in range(1, most + 1) if units % u == 0)


def halves(array):
    top = array.astype(jnp.bfloat16)
    return top, (array - top.astype(jnp.float32)).astype(jnp.bfloat16)


def product(left, right, transposed=False):
    dims = (((1,), (1 if transposed else 0,)), ((), ()))
    dot = functools.partial(lax.dot_general, dimension_numbers=dims, preferred_element_type=jnp.float32)
    left_top, left_rest = left if isinstance(left, tuple) else halves(left)
    right_top, right_rest = halves(right)
    rows = left_top.shape[0]
    both = dot(jnp.concatenate([left_top, left_rest], axis=0), right_top)
    return both[:rows] + (both[rows:] + dot(left_top, right_rest))


def scale_of(squares, features):
    return lax.rsqrt(squares / features + epsilon)


def loop(columns, most, body, init):
    tile = tile_of(columns, most)
    return lax.fori_loop(0, columns // tile, lambda i, c: body(i, pl.ds(pl.multiple_of(i * tile, tile), tile), c), init)


def place_of(cores):
    group = lax.axis_index("comp")
    return group // cores, group % cores


def diagonal(count):
    down = lax.broadcasted_iota(jnp.int32, (count, count), 0)
    across = lax.broadcasted_iota(jnp.int32, (count, count), 1)
    return down == across


def as_row(column):
    count = column.shape[0]
    return jnp.sum(jnp.where(diagonal(count), jnp.broadcast_to(column, (count, count)), 0.0), axis=0, keepdims=True)


def as_column(row):
    count = row.shape[1]
    return jnp.sum(jnp.where(diagonal(count), jnp.broadcast_to(row, (count, count)), 0.0), axis=1, keepdims=True)


def packing(per_group, rows):
    whole, rest = divmod(rows, lanes)
    folded = rest * 2 == lanes and per_group % 16 == 0
    short = per_group <= lanes
    height = whole * per_group + (per_group // 2 if folded else per_group if rest else 0) + (8 if short else per_group)
    return whole, rest, folded, short, height


def pack(projected, squares, out_ref):
    per_group, rows = projected.shape
    whole, rest, folded, short, height = packing(per_group, rows)
    for k in range(whole):
        out_ref[k * per_group : (k + 1) * per_group, :] = projected[:, k * lanes : (k + 1) * lanes]
    base, half, last = whole * per_group, per_group // 2, projected[:, whole * lanes :]
    if folded:
        out_ref[base : base + half, :] = jnp.concatenate([last[:half], last[half:]], axis=1)
        base += half
    elif rest:
        out_ref[base : base + per_group, :] = jnp.concatenate([last, jnp.zeros((per_group, lanes - rest))], axis=1)
        base += per_group
    if short:
        row = as_row(squares)
        if per_group < lanes:
            row = jnp.concatenate([row, jnp.zeros((1, lanes - per_group), jnp.float32)], axis=1)
        out_ref[base:, :] = jnp.broadcast_to(row, (8, lanes))
    else:
        out_ref[base:, :] = jnp.broadcast_to(squares, (per_group, lanes))


def unpack(p_ref, core, per_group, rows):
    whole, rest, folded, short, height = packing(per_group, rows)
    start = core * height

    def part(first, count):
        return p_ref[pl.ds(pl.multiple_of(start + first, 8), count), :]

    blocks = [part(k * per_group, per_group) for k in range(whole)]
    base, half = whole * per_group, per_group // 2
    if folded:
        last = part(base, half)
        blocks.append(jnp.concatenate([last[:, :rest], last[:, rest:]], axis=0))
        base += half
    elif rest:
        blocks.append(part(base, per_group)[:, :rest])
        base += per_group
    squares = as_column(part(base, 8)[:1, :per_group]) if short else part(base, per_group)[:, :1]
    return jnp.concatenate(blocks, axis=1), squares


def project_kernel(x_hbm, s_hbm, out_ref, x_ref, s_ref, sems):
    per_group, columns = x_ref.shape
    rows = s_ref.shape[0]

    def copies(i, here):
        return (
            pltpu.make_async_copy(x_hbm.at[:, here], x_ref.at[:, here], sems.at[0, i]),
            pltpu.make_async_copy(s_hbm.at[:, here], s_ref.at[:, here], sems.at[1, i]),
        )

    def begin(i, here, carry):
        for copy in copies(i, here):
            copy.start()
        return carry

    def body(i, here, carry):
        for copy in copies(i, here):
            copy.wait()
        x = x_ref[:, here]
        projected, squares = carry
        projected += product(x, s_ref[:, here], transposed=True)
        return projected, squares + jnp.sum(x * x, axis=1, keepdims=True)

    loop(columns, 4, begin, 0)
    zeros = jnp.zeros((per_group, rows), jnp.float32), jnp.zeros((per_group, 1), jnp.float32)
    projected, squares = loop(columns, 4, body, zeros)
    pack(projected, squares, out_ref)


def project(x, sample):
    per_group, columns = x.shape
    rows = sample.shape[0]
    height = packing(per_group, rows)[-1]
    return pl.pallas_call(
        project_kernel,
        in_specs=[anywhere] * 2,
        out_specs=[in_vmem] * 3,
        out_shape=[
            jax.ShapeDtypeStruct((height, lanes), jnp.float32),
            jax.ShapeDtypeStruct(x.shape, jnp.float32),
            jax.ShapeDtypeStruct(sample.shape, jnp.float32),
        ],
        scratch_shapes=[pltpu.SemaphoreType.DMA((2, columns // tile_of(columns, 4)))],
        compiler_params=params,
        name="project",
    )(x, sample)


def images_of(p_ref, core, rows, per_group, features):
    projected, squares = unpack(p_ref, core, per_group, rows)
    scale = scale_of(squares, features)
    return projected * scale, scale


def chip_kernel(features, cores, p_ref, s_ref, *refs):
    x_refs, out_ref = refs[:cores], refs[cores]
    rows = s_ref.shape[0]
    per_group = out_ref.shape[0]
    core = place_of(cores)[1]
    images, scale = images_of(p_ref, core, rows, per_group, features)
    shared = product(images, images * scale, transposed=True)
    later = lax.broadcasted_iota(jnp.int32, shared.shape, 0)
    earlier = lax.broadcasted_iota(jnp.int32, shared.shape, 1)
    weights = [images * (step_rate / rows), jnp.where(earlier < later, shared * (-step_rate / (features * rows)), 0.0)]
    for step in range(1, cores):
        other = (core + step) % cores
        others, others_scale = images_of(p_ref, other, rows, per_group, features)
        factor = jnp.where(other < core, -step_rate / (features * rows), 0.0)
        weights.append(product(images, others * (others_scale * factor), transposed=True))
    weights = halves(jnp.concatenate(weights, axis=1))

    def body(i, here, carry):
        x = x_refs[0][:, here]
        others = [x_ref[:, here] for x_ref in x_refs[1:]]
        out_ref[:, here] = scale * x + product(weights, jnp.concatenate([s_ref[:, here], x, *others], axis=0))
        return carry

    loop(out_ref.shape[1], 4, body, 0)


def chip_part(projected, sample, blocks, features):
    return pl.pallas_call(
        functools.partial(chip_kernel, features, len(blocks)),
        in_specs=[in_vmem] * (2 + len(blocks)),
        out_specs=in_vmem,
        out_shape=jax.ShapeDtypeStruct(blocks[0].shape, jnp.float32),
        compiler_params=params,
        name="chip_part",
    )(projected, sample, *blocks)


def others_kernel(features, rows, cores, chips, t_ref, p_ref, *refs):
    projected_refs, x_refs = refs[: chips - 1], refs[chips - 1 : (chips - 1) * (cores + 1)]
    out_ref, squares_ref = refs[(chips - 1) * (cores + 1) :]
    per_group, columns = t_ref.shape
    chip, core = place_of(cores)
    images = images_of(p_ref, core, rows, per_group, features)[0]
    others = []
    for k, projected_ref in enumerate(projected_refs):
        factor = jnp.where(partner(chip, k + 1, chips) < chip, -step_rate / (features * rows), 0.0)
        for step in range(cores):
            other, scale = images_of(projected_ref, (core + step) % cores, rows, per_group, features)
            others.append(other * (scale * factor))
    coupling = halves(product(images, jnp.concatenate(others, axis=0), transposed=True)) if others else None

    def body(i, here, squares):
        updated = t_ref[:, here]
        if others:
            updated += product(coupling, jnp.concatenate([x_ref[:, here] for x_ref in x_refs], axis=0))
        out_ref[:, here] = updated
        return squares + jnp.sum(updated * updated, axis=1, keepdims=True)

    squares = loop(columns, 4, body, jnp.zeros((per_group, 1), jnp.float32))
    squares_ref[...] = as_row(squares)


def others_part(partly, projected, others, blocks, rows, features):
    chips = len(others) + 1
    cores = len(blocks) // len(others) if others else 1
    return pl.pallas_call(
        functools.partial(others_kernel, features, rows, cores, chips),
        in_specs=[in_vmem] * (2 + len(others) + len(blocks)),
        out_specs=[in_vmem, in_vmem],
        out_shape=[
            jax.ShapeDtypeStruct(partly.shape, jnp.float32),
            jax.ShapeDtypeStruct((1, partly.shape[0]), jnp.float32),
        ],
        compiler_params=params,
        name="others_part",
    )(partly, projected, *others, *blocks)


def finish_kernel(features, cores, count, updated_ref, *refs):
    squares_refs, (out_ref, scaled, sems) = refs[:-3], refs[-3:]
    per_group, columns = updated_ref.shape
    core = place_of(cores)[1]
    squares = sum((ref[cores - 1 : cores, :] for ref in squares_refs[1:count]), squares_refs[0][cores - 1 : cores, :])
    if cores > 1:
        squares = jnp.where(core == 0, squares_refs[count][0:1, :], squares)
    scale = as_column(scale_of(squares, features))
    tile = tile_of(columns, 7)
    copies = []
    for i in range(columns // tile):
        here = pl.ds(i * tile, tile)
        scaled[:, here] = updated_ref[:, here] * scale
        copies.append(pltpu.make_async_copy(scaled.at[:, here], out_ref.at[:, here], sems.at[i]))
        copies[-1].start()
    for copy in copies:
        copy.wait()


def finish(updated, squares, count, cores, features):
    columns = updated.shape[1]
    return pl.pallas_call(
        functools.partial(finish_kernel, features, cores, count),
        in_specs=[in_vmem] * (1 + len(squares)),
        out_specs=anywhere,
        out_shape=jax.ShapeDtypeStruct(updated.shape, jnp.float32),
        scratch_shapes=[
            pltpu.VMEM(updated.shape, jnp.float32),
            pltpu.SemaphoreType.DMA((columns // tile_of(columns, 7),)),
        ],
        compiler_params=params,
        name="finish",
    )(updated, *squares)


def partner(place, step, size):
    return (place + step) % size if size & (size - 1) else place ^ step


def swap_cores(array, cores):
    return lax.ppermute(array, "comp", [(i, i ^ 1) for i in range(lax.axis_size("comp"))])


def from_chip(array, step, cores, carrying=False):
    size = lax.axis_size("comp")
    chips = size // cores
    pairs = []
    for i in range(size):
        moves = not carrying or i % cores == cores - 1
        pairs.append(((partner(i // cores, step, chips) * cores + i % cores) if moves else i, i))
    return lax.ppermute(array, "comp", pairs)


def along_feat(array, step, cores):
    comp, feat = lax.axis_size("comp"), lax.axis_size("feat")
    pairs = []
    for i in range(comp):
        for j in range(feat):
            source = partner(j, step, feat) if i % cores == cores - 1 else j
            pairs.append((i * feat + source, i * feat + j))
    return lax.ppermute(array, ("comp", "feat"), pairs)


def terms(array, cores, together):
    size = lax.axis_size("feat")
    if size & (size - 1):
        return [array] + [along_feat(array, step, cores) for step in range(1, size)]
    parts, step, bits = [array], 1, (size.bit_length() - 1) % together or together
    while step < size:
        array = sum(parts[1:], parts[0])
        parts = [array] + [along_feat(array, step * k, cores) for k in range(1, 1 << bits)]
        step <<= bits
        bits = together
    return parts


def hand_over(array, cores):
    if cores == 1:
        return array
    return jnp.where(place_of(cores)[1] == 0, swap_cores(array, cores), array)


def shards(samples, start_vectors):
    comp = lax.axis_size("comp")
    feat = lax.axis_size("feat")
    cores = 2 if comp % 2 == 0 else 1
    chips = comp // cores
    sample = samples[0]
    rows = sample.shape[0]
    features = sample.shape[1] * feat

    across = [from_chip(start_vectors, step, cores) for step in range(1, chips)]
    beside = [swap_cores(start_vectors, cores)] if cores > 1 else []

    sources = [pltpu.with_memory_space_constraint(array, pltpu.HBM) for array in (start_vectors, sample)]
    projected, vectors, sample = project(*sources)
    if cores > 1:
        projected = jnp.concatenate([swap_cores(projected, cores), projected], axis=0)
    parts = terms(projected, cores, 1)
    carried = sum(parts[1:], parts[0])
    projected = hand_over(carried, cores)
    received = [from_chip(carried, step, cores, True) for step in range(1, chips)]
    partly = chip_part(projected, sample, [vectors] + beside, features)
    blocks = []
    for k, arrived in enumerate(across):
        arrived, received[k], projected = lax.optimization_barrier((arrived, received[k], projected))
        blocks += [arrived] + ([swap_cores(arrived, cores)] if cores > 1 else [])
    others = [hand_over(array, cores) for array in received]
    updated, squares = others_part(partly, projected, others, blocks, rows, features)

    if cores > 1:
        squares = jnp.concatenate([swap_cores(squares, cores), squares], axis=0)
    squares = terms(squares, cores, 2)
    count = len(squares)
    if cores > 1:
        squares = squares + [swap_cores(sum(squares[1:], squares[0]), cores)]
    return finish(updated, squares, count, cores, features)


def solution(mesh):
    in_specs = (P(None, None, "feat"), P("comp", "feat"))
    out_specs = P("comp", "feat")
    return jax.shard_map(shards, mesh=mesh, in_specs=in_specs, out_specs=out_specs, check_vma=False)
```

```python
import functools

import jax
import jax.numpy as jnp
from jax import lax
from jax.experimental import pallas as pl
from jax.experimental.pallas import tpu as pltpu
from jax.sharding import PartitionSpec as P

step_rate = 0.1
epsilon = 1e-06
lanes = 128
in_vmem = pl.BlockSpec(memory_space=pltpu.VMEM)
anywhere = pl.BlockSpec(memory_space=pl.ANY)
params = pltpu.CompilerParams(vmem_limit_bytes=16 << 20)


def tile_of(columns, most):
    if columns % lanes:
        return columns
    units = columns // lanes
    return lanes * max(u for u in range(1, most + 1) if units % u == 0)


def halves(array):
    top = array.astype(jnp.bfloat16)
    return top, (array - top.astype(jnp.float32)).astype(jnp.bfloat16)


def product(left, right, transposed=False):
    dims = (((1,), (1 if transposed else 0,)), ((), ()))
    dot = functools.partial(lax.dot_general, dimension_numbers=dims, preferred_element_type=jnp.float32)
    left_top, left_rest = left if isinstance(left, tuple) else halves(left)
    right_top, right_rest = halves(right)
    rows = left_top.shape[0]
    both = dot(jnp.concatenate([left_top, left_rest], axis=0), right_top)
    return both[:rows] + (both[rows:] + dot(left_top, right_rest))


def scale_of(squares, features):
    return lax.rsqrt(squares / features + epsilon)


def loop(columns, most, body, init):
    tile = tile_of(columns, most)
    return lax.fori_loop(0, columns // tile, lambda i, c: body(i, pl.ds(pl.multiple_of(i * tile, tile), tile), c), init)


def project_kernel(x_hbm, s_hbm, out_ref, x_ref, s_ref, sems):
    per_group, columns = x_ref.shape
    rows = s_ref.shape[0]

    def copies(i, here):
        return (
            pltpu.make_async_copy(x_hbm.at[:, here], x_ref.at[:, here], sems.at[0, i]),
            pltpu.make_async_copy(s_hbm.at[:, here], s_ref.at[:, here], sems.at[1, i]),
        )

    def begin(i, here, carry):
        for copy in copies(i, here):
            copy.start()
        return carry

    def body(i, here, carry):
        for copy in copies(i, here):
            copy.wait()
        x = x_ref[:, here]
        projected, squares = carry
        projected += product(x, s_ref[:, here], transposed=True)
        return projected, squares + jnp.sum(x * x, axis=1, keepdims=True)

    loop(columns, 4, begin, 0)
    zeros = jnp.zeros((per_group, rows), jnp.float32), jnp.zeros((per_group, 1), jnp.float32)
    projected, squares = loop(columns, 4, body, zeros)
    out_ref[:, :rows] = projected
    out_ref[:, rows:] = jnp.broadcast_to(squares, (per_group, out_ref.shape[1] - rows))


def project(x, sample):
    per_group, columns = x.shape
    rows = sample.shape[0]
    width = -(-(rows + 1) // lanes) * lanes
    return pl.pallas_call(
        project_kernel,
        in_specs=[anywhere] * 2,
        out_specs=[in_vmem] * 3,
        out_shape=[
            jax.ShapeDtypeStruct((per_group, width), jnp.float32),
            jax.ShapeDtypeStruct(x.shape, jnp.float32),
            jax.ShapeDtypeStruct(sample.shape, jnp.float32),
        ],
        scratch_shapes=[pltpu.SemaphoreType.DMA((2, columns // tile_of(columns, 4)))],
        compiler_params=params,
        name="project",
    )(x, sample)


def images_of(p_ref, rows, features):
    scale = scale_of(p_ref[:, rows : rows + 1], features)
    return p_ref[:, :rows] * scale, scale


def owner(group, step, size):
    return (group + step) % size if size & (size - 1) else group ^ step


def couplings(images, steps, projected_refs, features):
    group, size = lax.axis_index("comp"), lax.axis_size("comp")
    rows = images.shape[1]
    others = []
    for step, p_ref in zip(steps, projected_refs):
        other, scale = images_of(p_ref, rows, features)
        others.append(other * (scale * jnp.where(owner(group, step, size) < group, -step_rate / (features * rows), 0.0)))
    return product(images, jnp.concatenate(others, axis=0), transposed=True)


def first_kernel(features, steps, p_ref, s_ref, x_ref, *refs):
    count = len(steps)
    projected_refs, x_refs, out_ref = refs[:count], refs[count : 2 * count], refs[2 * count]
    rows = s_ref.shape[0]
    images, scale = images_of(p_ref, rows, features)
    shared = product(images, images * scale, transposed=True)
    later = lax.broadcasted_iota(jnp.int32, shared.shape, 0)
    earlier = lax.broadcasted_iota(jnp.int32, shared.shape, 1)
    weights = [images * (step_rate / rows), jnp.where(earlier < later, shared * (-step_rate / (features * rows)), 0.0)]
    if count:
        weights.append(couplings(images, steps, projected_refs, features))
    weights = halves(jnp.concatenate(weights, axis=1))

    def body(i, here, carry):
        x = x_ref[:, here]
        others = [ref[:, here] for ref in x_refs]
        out_ref[:, here] = scale * x + product(weights, jnp.concatenate([s_ref[:, here], x, *others], axis=0))
        return carry

    loop(x_ref.shape[1], 4, body, 0)


def first_part(projected, sample, x, steps, others, blocks, features):
    return pl.pallas_call(
        functools.partial(first_kernel, features, steps),
        in_specs=[in_vmem] * (3 + 2 * len(steps)),
        out_specs=in_vmem,
        out_shape=jax.ShapeDtypeStruct(x.shape, jnp.float32),
        compiler_params=params,
        name="first_part",
    )(projected, sample, x, *others, *blocks)


def rest_kernel(features, rows, steps, t_ref, p_ref, *refs):
    count = len(steps)
    projected_refs, x_refs, (out_ref, squares_ref) = refs[:count], refs[count : 2 * count], refs[2 * count :]
    per_group, columns = t_ref.shape
    if count:
        weights = halves(couplings(images_of(p_ref, rows, features)[0], steps, projected_refs, features))

    def body(i, here, squares):
        updated = t_ref[:, here]
        if count:
            updated += product(weights, jnp.concatenate([ref[:, here] for ref in x_refs], axis=0))
        out_ref[:, here] = updated
        return squares + jnp.sum(updated * updated, axis=1, keepdims=True)

    squares = loop(columns, 4, body, jnp.zeros((per_group, 1), jnp.float32))
    spread = jnp.broadcast_to(squares, (per_group, per_group))
    squares_ref[...] = jnp.sum(jnp.where(diagonal(per_group), spread, 0.0), axis=0, keepdims=True)


def rest_part(partly, projected, steps, others, blocks, rows, features):
    return pl.pallas_call(
        functools.partial(rest_kernel, features, rows, steps),
        in_specs=[in_vmem] * (2 + 2 * len(steps)),
        out_specs=[in_vmem, in_vmem],
        out_shape=[
            jax.ShapeDtypeStruct(partly.shape, jnp.float32),
            jax.ShapeDtypeStruct((1, partly.shape[0]), jnp.float32),
        ],
        compiler_params=params,
        name="rest_part",
    )(partly, projected, *others, *blocks)


def diagonal(count):
    down = lax.broadcasted_iota(jnp.int32, (count, count), 0)
    across = lax.broadcasted_iota(jnp.int32, (count, count), 1)
    return down == across


def finish_kernel(features, count, updated_ref, *refs):
    squares_refs, (out_ref, scaled, sems) = refs[:count], refs[count:]
    per_group, columns = updated_ref.shape
    squares = squares_refs[0][...]
    for ref in squares_refs[1:]:
        squares += ref[...]
    spread = jnp.broadcast_to(scale_of(squares, features), (per_group, per_group))
    scale = jnp.sum(jnp.where(diagonal(per_group), spread, 0.0), axis=1, keepdims=True)
    tile = tile_of(columns, 7)
    copies = []
    for i in range(columns // tile):
        here = pl.ds(i * tile, tile)
        scaled[:, here] = updated_ref[:, here] * scale
        copies.append(pltpu.make_async_copy(scaled.at[:, here], out_ref.at[:, here], sems.at[i]))
        copies[-1].start()
    for copy in copies:
        copy.wait()


def finish(updated, squares, features):
    count = len(squares)
    return pl.pallas_call(
        functools.partial(finish_kernel, features, count),
        in_specs=[in_vmem] * (1 + count),
        out_specs=anywhere,
        out_shape=jax.ShapeDtypeStruct(updated.shape, jnp.float32),
        scratch_shapes=[
            pltpu.VMEM(updated.shape, jnp.float32),
            pltpu.SemaphoreType.DMA((updated.shape[1] // tile_of(updated.shape[1], 7),)),
        ],
        compiler_params=params,
        name="finish",
    )(updated, *squares)


def exchange(array, axis, step):
    return lax.ppermute(array, axis, [(i, i ^ step) for i in range(lax.axis_size(axis))])


def terms(array, axis, together):
    size = lax.axis_size(axis)
    if size & (size - 1):
        return [lax.psum(array, axis)]
    parts, step, bits = [array], 1, (size.bit_length() - 1) % together or together
    while step < size:
        array = sum(parts[1:], parts[0])
        parts = [array] + [exchange(array, axis, step * k) for k in range(1, 1 << bits)]
        step <<= bits
        bits = together
    return parts


def gather(own):
    size = lax.axis_size("comp")
    if size & (size - 1):
        arrays, group = lax.all_gather(own, "comp"), lax.axis_index("comp")
        return {step: arrays[owner(group, step, size)] for step in range(1, size)}
    return {step: exchange(own, "comp", step) for step in range(1, size)}


def shards(samples, start_vectors):
    comp = lax.axis_size("comp")
    feat = lax.axis_size("feat")
    sample = samples[0]
    rows = sample.shape[0]
    features = sample.shape[1] * feat
    even = comp & (comp - 1) == 0

    blocks = {step: exchange(start_vectors, "comp", step) for step in range(2, comp, 2)} if even else gather(start_vectors)
    projected, vectors, sample = project(
        *(pltpu.with_memory_space_constraint(array, pltpu.HBM) for array in (start_vectors, sample))
    )
    if even and comp > 1:
        blocks[1] = exchange(vectors, "comp", 1)
    parts = terms(projected, "feat", 1)
    projected = sum(parts[1:], parts[0])
    if even:
        others = {step: exchange(projected, "comp", step) for step in range(1, comp) if step == 1 or step % 2 == 0}
    else:
        others = gather(projected)
    near = [1][: comp - 1]
    far = list(range(2, comp))

    def of(arrays, steps):
        return [arrays[step] for step in steps]

    partly = first_part(projected, sample, vectors, near, of(others, near), of(blocks, near), features)
    if even:
        for step in range(2, comp, 2):
            blocks[step], others[step], others[1] = lax.optimization_barrier((blocks[step], others[step], others[1]))
            blocks[step + 1] = exchange(blocks[step], "comp", 1)
            others[step + 1] = exchange(others[step], "comp", 1)
    updated, squares = rest_part(partly, projected, far, of(others, far), of(blocks, far), rows, features)
    return finish(updated, terms(squares, "feat", 2), features)


def solution(mesh):
    in_specs = (P(None, None, "feat"), P("comp", "feat"))
    out_specs = P("comp", "feat")
    return jax.shard_map(shards, mesh=mesh, in_specs=in_specs, out_specs=out_specs, check_vma=False)
```

```python
import functools

import jax
import jax.numpy as jnp
from jax import lax
from jax.experimental import pallas as pl
from jax.experimental.pallas import tpu as pltpu
from jax.sharding import PartitionSpec as P

step_rate = 0.1
epsilon = 1e-06
lanes = 128
in_vmem = pl.BlockSpec(memory_space=pltpu.VMEM)
anywhere = pl.BlockSpec(memory_space=pl.ANY)
params = pltpu.CompilerParams(vmem_limit_bytes=16 << 20)


def tile_of(columns, most):
    if columns % lanes:
        return columns
    units = columns // lanes
    return lanes * max(u for u in range(1, most + 1) if units % u == 0)


def halves(array):
    top = array.astype(jnp.bfloat16)
    return top, (array - top.astype(jnp.float32)).astype(jnp.bfloat16)


def product(left, right, transposed=False):
    dims = (((1,), (1 if transposed else 0,)), ((), ()))
    dot = functools.partial(lax.dot_general, dimension_numbers=dims, preferred_element_type=jnp.float32)
    left_top, left_rest = left if isinstance(left, tuple) else halves(left)
    right_top, right_rest = halves(right)
    rows = left_top.shape[0]
    both = dot(jnp.concatenate([left_top, left_rest], axis=0), right_top)
    return both[:rows] + (both[rows:] + dot(left_top, right_rest))


def scale_of(squares, features):
    return lax.rsqrt(squares / features + epsilon)


def loop(columns, most, body, init):
    tile = tile_of(columns, most)
    return lax.fori_loop(0, columns // tile, lambda i, c: body(i, pl.ds(pl.multiple_of(i * tile, tile), tile), c), init, unroll=True)


def project_kernel(x_hbm, s_hbm, out_ref, x_ref, s_ref, sems):
    per_group, columns = x_ref.shape
    rows = s_ref.shape[0]

    def copies(i, here):
        return (
            pltpu.make_async_copy(x_hbm.at[:, here], x_ref.at[:, here], sems.at[0, i]),
            pltpu.make_async_copy(s_hbm.at[:, here], s_ref.at[:, here], sems.at[1, i]),
        )

    def begin(i, here, carry):
        for copy in copies(i, here):
            copy.start()
        return carry

    def body(i, here, carry):
        for copy in copies(i, here):
            copy.wait()
        x = x_ref[:, here]
        projected, squares = carry
        projected += product(x, s_ref[:, here], transposed=True)
        return projected, squares + jnp.sum(x * x, axis=1, keepdims=True)

    loop(columns, 4, begin, 0)
    zeros = jnp.zeros((per_group, rows), jnp.float32), jnp.zeros((per_group, 1), jnp.float32)
    projected, squares = loop(columns, 4, body, zeros)
    out_ref[:, :rows] = projected
    out_ref[:, rows:] = jnp.broadcast_to(squares, (per_group, out_ref.shape[1] - rows))


def project(x, sample):
    per_group, columns = x.shape
    rows = sample.shape[0]
    width = -(-(rows + 1) // lanes) * lanes
    return pl.pallas_call(
        project_kernel,
        in_specs=[anywhere] * 2,
        out_specs=[in_vmem] * 3,
        out_shape=[
            jax.ShapeDtypeStruct((per_group, width), jnp.float32),
            jax.ShapeDtypeStruct(x.shape, jnp.float32),
            jax.ShapeDtypeStruct(sample.shape, jnp.float32),
        ],
        scratch_shapes=[pltpu.SemaphoreType.DMA((2, columns // tile_of(columns, 4)))],
        compiler_params=params,
        name="project",
    )(x, sample)


def images_of(p_ref, rows, features):
    scale = scale_of(p_ref[:, rows : rows + 1], features)
    return p_ref[:, :rows] * scale, scale


def owner(group, step, size):
    return (group + step) % size if size & (size - 1) else group ^ step


def couplings(images, steps, projected_refs, features):
    group, size = lax.axis_index("comp"), lax.axis_size("comp")
    rows = images.shape[1]
    others = []
    for step, p_ref in zip(steps, projected_refs):
        other, scale = images_of(p_ref, rows, features)
        others.append(other * (scale * jnp.where(owner(group, step, size) < group, -step_rate / (features * rows), 0.0)))
    return product(images, jnp.concatenate(others, axis=0), transposed=True)


def first_kernel(features, steps, p_ref, s_ref, x_ref, *refs):
    count = len(steps)
    projected_refs, x_refs, out_ref = refs[:count], refs[count : 2 * count], refs[2 * count]
    rows = s_ref.shape[0]
    images, scale = images_of(p_ref, rows, features)
    shared = product(images, images * scale, transposed=True)
    later = lax.broadcasted_iota(jnp.int32, shared.shape, 0)
    earlier = lax.broadcasted_iota(jnp.int32, shared.shape, 1)
    weights = [images * (step_rate / rows), jnp.where(earlier < later, shared * (-step_rate / (features * rows)), 0.0)]
    if count:
        weights.append(couplings(images, steps, projected_refs, features))
    weights = halves(jnp.concatenate(weights, axis=1))

    def body(i, here, carry):
        x = x_ref[:, here]
        others = [ref[:, here] for ref in x_refs]
        out_ref[:, here] = scale * x + product(weights, jnp.concatenate([s_ref[:, here], x, *others], axis=0))
        return carry

    loop(x_ref.shape[1], 4, body, 0)


def first_part(projected, sample, x, steps, others, blocks, features):
    return pl.pallas_call(
        functools.partial(first_kernel, features, steps),
        in_specs=[in_vmem] * (3 + 2 * len(steps)),
        out_specs=in_vmem,
        out_shape=jax.ShapeDtypeStruct(x.shape, jnp.float32),
        compiler_params=params,
        name="first_part",
    )(projected, sample, x, *others, *blocks)


def rest_kernel(features, rows, steps, t_ref, p_ref, *refs):
    count = len(steps)
    projected_refs, x_refs, (out_ref, squares_ref) = refs[:count], refs[count : 2 * count], refs[2 * count :]
    per_group, columns = t_ref.shape
    if count:
        weights = halves(couplings(images_of(p_ref, rows, features)[0], steps, projected_refs, features))

    def body(i, here, squares):
        updated = t_ref[:, here]
        if count:
            updated += product(weights, jnp.concatenate([ref[:, here] for ref in x_refs], axis=0))
        out_ref[:, here] = updated
        return squares + jnp.sum(updated * updated, axis=1, keepdims=True)

    squares = loop(columns, 4, body, jnp.zeros((per_group, 1), jnp.float32))
    spread = jnp.broadcast_to(squares, (per_group, per_group))
    squares_ref[...] = jnp.sum(jnp.where(diagonal(per_group), spread, 0.0), axis=0, keepdims=True)


def rest_part(partly, projected, steps, others, blocks, rows, features):
    return pl.pallas_call(
        functools.partial(rest_kernel, features, rows, steps),
        in_specs=[in_vmem] * (2 + 2 * len(steps)),
        out_specs=[in_vmem, in_vmem],
        out_shape=[
            jax.ShapeDtypeStruct(partly.shape, jnp.float32),
            jax.ShapeDtypeStruct((1, partly.shape[0]), jnp.float32),
        ],
        compiler_params=params,
        name="rest_part",
    )(partly, projected, *others, *blocks)


def diagonal(count):
    down = lax.broadcasted_iota(jnp.int32, (count, count), 0)
    across = lax.broadcasted_iota(jnp.int32, (count, count), 1)
    return down == across


def finish_kernel(features, count, updated_ref, *refs):
    squares_refs, (out_ref, scaled, sems) = refs[:count], refs[count:]
    per_group, columns = updated_ref.shape
    squares = squares_refs[0][...]
    for ref in squares_refs[1:]:
        squares += ref[...]
    spread = jnp.broadcast_to(scale_of(squares, features), (per_group, per_group))
    scale = jnp.sum(jnp.where(diagonal(per_group), spread, 0.0), axis=1, keepdims=True)
    tile = tile_of(columns, 7)
    copies = []
    for i in range(columns // tile):
        here = pl.ds(i * tile, tile)
        scaled[:, here] = updated_ref[:, here] * scale
        copies.append(pltpu.make_async_copy(scaled.at[:, here], out_ref.at[:, here], sems.at[i]))
        copies[-1].start()
    for copy in copies:
        copy.wait()


def finish(updated, squares, features):
    count = len(squares)
    return pl.pallas_call(
        functools.partial(finish_kernel, features, count),
        in_specs=[in_vmem] * (1 + count),
        out_specs=anywhere,
        out_shape=jax.ShapeDtypeStruct(updated.shape, jnp.float32),
        scratch_shapes=[
            pltpu.VMEM(updated.shape, jnp.float32),
            pltpu.SemaphoreType.DMA((updated.shape[1] // tile_of(updated.shape[1], 7),)),
        ],
        compiler_params=params,
        name="finish",
    )(updated, *squares)


def exchange(array, axis, step):
    return lax.ppermute(array, axis, [(i, i ^ step) for i in range(lax.axis_size(axis))])


def terms(array, axis, together):
    size = lax.axis_size(axis)
    if size & (size - 1):
        return [lax.psum(array, axis)]
    parts, step = [array], 1
    while step < size:
        array = sum(parts[1:], parts[0])
        width = min(1 << together, size // step)
        parts = [array] + [exchange(array, axis, step * k) for k in range(1, width)]
        step *= width
    return parts


def gather(own):
    size = lax.axis_size("comp")
    if size & (size - 1):
        arrays, group = lax.all_gather(own, "comp"), lax.axis_index("comp")
        return {step: arrays[owner(group, step, size)] for step in range(1, size)}
    return {step: exchange(own, "comp", step) for step in range(1, size)}


def shards(samples, start_vectors):
    comp = lax.axis_size("comp")
    feat = lax.axis_size("feat")
    sample = samples[0]
    rows = sample.shape[0]
    features = sample.shape[1] * feat
    even = comp & (comp - 1) == 0

    blocks = {step: exchange(start_vectors, "comp", step) for step in range(2, comp, 2)} if even else gather(start_vectors)
    projected, vectors, sample = project(
        *(pltpu.with_memory_space_constraint(array, pltpu.HBM) for array in (start_vectors, sample))
    )
    if even and comp > 1:
        blocks[1] = exchange(vectors, "comp", 1)
    parts = terms(projected, "feat", 1)
    projected = sum(parts[1:], parts[0])
    if even:
        others = {step: exchange(projected, "comp", step) for step in range(1, comp) if step == 1 or step % 2 == 0}
    else:
        others = gather(projected)
    near = [1][: comp - 1]
    far = list(range(2, comp))

    def of(arrays, steps):
        return [arrays[step] for step in steps]

    partly = first_part(projected, sample, vectors, near, of(others, near), of(blocks, near), features)
    if even:
        for step in range(2, comp, 2):
            blocks[step], others[step], others[1] = lax.optimization_barrier((blocks[step], others[step], others[1]))
            blocks[step + 1] = exchange(blocks[step], "comp", 1)
            others[step + 1] = exchange(others[step], "comp", 1)
    updated, squares = rest_part(partly, projected, far, of(others, far), of(blocks, far), rows, features)
    return finish(updated, terms(squares, "feat", 2), features)


def solution(mesh):
    in_specs = (P(None, None, "feat"), P("comp", "feat"))
    out_specs = P("comp", "feat")
    return jax.shard_map(shards, mesh=mesh, in_specs=in_specs, out_specs=out_specs, check_vma=False)
```

```python
import functools

import jax
import jax.numpy as jnp
from jax import lax
from jax.experimental import pallas as pl
from jax.experimental.pallas import tpu as pltpu
from jax.sharding import PartitionSpec as P

step_rate = 0.1
epsilon = 1e-06
lanes = 128
in_vmem = pl.BlockSpec(memory_space=pltpu.VMEM)
anywhere = pl.BlockSpec(memory_space=pl.ANY)
params = pltpu.CompilerParams(vmem_limit_bytes=16 << 20)


def tile_of(columns, most):
    if columns % lanes:
        return columns
    units = columns // lanes
    return lanes * max(u for u in range(1, most + 1) if units % u == 0)


def halves(array):
    top = array.astype(jnp.bfloat16)
    return top, (array - top.astype(jnp.float32)).astype(jnp.bfloat16)


def product(left, right, transposed=False):
    dims = (((1,), (1 if transposed else 0,)), ((), ()))
    dot = functools.partial(lax.dot_general, dimension_numbers=dims, preferred_element_type=jnp.float32)
    left_top, left_rest = left if isinstance(left, tuple) else halves(left)
    right_top, right_rest = halves(right)
    rows = left_top.shape[0]
    both = dot(jnp.concatenate([left_top, left_rest], axis=0), right_top)
    return both[:rows] + (both[rows:] + dot(left_top, right_rest))


def scale_of(squares, features):
    return lax.rsqrt(squares / features + epsilon)


def loop(columns, most, body, init):
    tile = tile_of(columns, most)
    return lax.fori_loop(0, columns // tile, lambda i, c: body(i, pl.ds(pl.multiple_of(i * tile, tile), tile), c), init, unroll=True)


def project_kernel(x_hbm, s_hbm, out_ref, x_ref, s_ref, sems):
    per_group, columns = x_ref.shape
    rows = s_ref.shape[0]

    def copies(i, here):
        return (
            pltpu.make_async_copy(x_hbm.at[:, here], x_ref.at[:, here], sems.at[0, i]),
            pltpu.make_async_copy(s_hbm.at[:, here], s_ref.at[:, here], sems.at[1, i]),
        )

    def begin(i, here, carry):
        for copy in copies(i, here):
            copy.start()
        return carry

    def body(i, here, carry):
        for copy in copies(i, here):
            copy.wait()
        x = x_ref[:, here]
        projected, squares = carry
        projected += product(x, s_ref[:, here], transposed=True)
        return projected, squares + jnp.sum(x * x, axis=1, keepdims=True)

    loop(columns, 4, begin, 0)
    zeros = jnp.zeros((per_group, rows), jnp.float32), jnp.zeros((per_group, 1), jnp.float32)
    projected, squares = loop(columns, 4, body, zeros)
    out_ref[:, :rows] = projected
    out_ref[:, rows:] = jnp.broadcast_to(squares, (per_group, out_ref.shape[1] - rows))


def project(x, sample):
    per_group, columns = x.shape
    rows = sample.shape[0]
    width = -(-(rows + 1) // lanes) * lanes
    return pl.pallas_call(
        project_kernel,
        in_specs=[anywhere] * 2,
        out_specs=[in_vmem] * 3,
        out_shape=[
            jax.ShapeDtypeStruct((per_group, width), jnp.float32),
            jax.ShapeDtypeStruct(x.shape, jnp.float32),
            jax.ShapeDtypeStruct(sample.shape, jnp.float32),
        ],
        scratch_shapes=[pltpu.SemaphoreType.DMA((2, columns // tile_of(columns, 4)))],
        compiler_params=params,
        name="project",
    )(x, sample)


def images_of(p_ref, rows, features):
    scale = scale_of(p_ref[:, rows : rows + 1], features)
    return p_ref[:, :rows] * scale, scale


def owner(group, step, size):
    return (group + step) % size if size & (size - 1) else group ^ step


def couplings(images, steps, projected_refs, features):
    group, size = lax.axis_index("comp"), lax.axis_size("comp")
    rows = images.shape[1]
    others = []
    for step, p_ref in zip(steps, projected_refs):
        other, scale = images_of(p_ref, rows, features)
        others.append(other * (scale * jnp.where(owner(group, step, size) < group, -step_rate / (features * rows), 0.0)))
    return product(images, jnp.concatenate(others, axis=0), transposed=True)


def first_kernel(features, steps, p_ref, s_ref, x_ref, *refs):
    count = len(steps)
    projected_refs, x_refs, out_ref = refs[:count], refs[count : 2 * count], refs[2 * count]
    rows = s_ref.shape[0]
    images, scale = images_of(p_ref, rows, features)
    shared = product(images, images * scale, transposed=True)
    later = lax.broadcasted_iota(jnp.int32, shared.shape, 0)
    earlier = lax.broadcasted_iota(jnp.int32, shared.shape, 1)
    weights = [images * (step_rate / rows), jnp.where(earlier < later, shared * (-step_rate / (features * rows)), 0.0)]
    if count:
        weights.append(couplings(images, steps, projected_refs, features))
    weights = halves(jnp.concatenate(weights, axis=1))

    def body(i, here, carry):
        x = x_ref[:, here]
        others = [ref[:, here] for ref in x_refs]
        out_ref[:, here] = scale * x + product(weights, jnp.concatenate([s_ref[:, here], x, *others], axis=0))
        return carry

    loop(x_ref.shape[1], 4, body, 0)


def first_part(projected, sample, x, steps, others, blocks, features):
    return pl.pallas_call(
        functools.partial(first_kernel, features, steps),
        in_specs=[in_vmem] * (3 + 2 * len(steps)),
        out_specs=in_vmem,
        out_shape=jax.ShapeDtypeStruct(x.shape, jnp.float32),
        compiler_params=params,
        name="first_part",
    )(projected, sample, x, *others, *blocks)


def rest_kernel(features, rows, steps, t_ref, p_ref, *refs):
    count = len(steps)
    projected_refs, x_refs, (out_ref, squares_ref) = refs[:count], refs[count : 2 * count], refs[2 * count :]
    per_group, columns = t_ref.shape
    if count:
        weights = halves(couplings(images_of(p_ref, rows, features)[0], steps, projected_refs, features))

    def body(i, here, squares):
        updated = t_ref[:, here]
        if count:
            updated += product(weights, jnp.concatenate([ref[:, here] for ref in x_refs], axis=0))
        out_ref[:, here] = updated
        return squares + jnp.sum(updated * updated, axis=1, keepdims=True)

    squares = loop(columns, 4, body, jnp.zeros((per_group, 1), jnp.float32))
    spread = jnp.broadcast_to(squares, (per_group, per_group))
    row = jnp.sum(jnp.where(diagonal(per_group), spread, 0.0), axis=0, keepdims=True)
    squares_ref[...] = jnp.broadcast_to(row[None], squares_ref.shape)


def rest_part(partly, projected, steps, others, blocks, rows, features):
    return pl.pallas_call(
        functools.partial(rest_kernel, features, rows, steps),
        in_specs=[in_vmem] * (2 + 2 * len(steps)),
        out_specs=[in_vmem, in_vmem],
        out_shape=[
            jax.ShapeDtypeStruct(partly.shape, jnp.float32),
            jax.ShapeDtypeStruct((lax.axis_size("feat"), 1, partly.shape[0]), jnp.float32),
        ],
        compiler_params=params,
        name="rest_part",
    )(partly, projected, *others, *blocks)


def diagonal(count):
    down = lax.broadcasted_iota(jnp.int32, (count, count), 0)
    across = lax.broadcasted_iota(jnp.int32, (count, count), 1)
    return down == across


def finish_kernel(features, count, updated_ref, *refs):
    squares_refs, (out_ref, scaled, sems) = refs[:count], refs[count:]
    per_group, columns = updated_ref.shape
    squares = jnp.sum(squares_refs[0][...], axis=0)
    spread = jnp.broadcast_to(scale_of(squares, features), (per_group, per_group))
    scale = jnp.sum(jnp.where(diagonal(per_group), spread, 0.0), axis=1, keepdims=True)
    tile = tile_of(columns, 7)
    copies = []
    for i in range(columns // tile):
        here = pl.ds(i * tile, tile)
        scaled[:, here] = updated_ref[:, here] * scale
        copies.append(pltpu.make_async_copy(scaled.at[:, here], out_ref.at[:, here], sems.at[i]))
        copies[-1].start()
    for copy in copies:
        copy.wait()


def finish(updated, squares, features):
    count = len(squares)
    return pl.pallas_call(
        functools.partial(finish_kernel, features, count),
        in_specs=[in_vmem] * (1 + count),
        out_specs=anywhere,
        out_shape=jax.ShapeDtypeStruct(updated.shape, jnp.float32),
        scratch_shapes=[
            pltpu.VMEM(updated.shape, jnp.float32),
            pltpu.SemaphoreType.DMA((updated.shape[1] // tile_of(updated.shape[1], 7),)),
        ],
        compiler_params=params,
        name="finish",
    )(updated, *squares)


def exchange(array, axis, step):
    return lax.ppermute(array, axis, [(i, i ^ step) for i in range(lax.axis_size(axis))])


def terms(array, axis, together):
    size = lax.axis_size(axis)
    if size & (size - 1):
        return [lax.psum(array, axis)]
    parts, step = [array], 1
    while step < size:
        array = sum(parts[1:], parts[0])
        width = min(1 << together, size // step)
        parts = [array] + [exchange(array, axis, step * k) for k in range(1, width)]
        step *= width
    return parts


def gather(own):
    size = lax.axis_size("comp")
    if size & (size - 1):
        arrays, group = lax.all_gather(own, "comp"), lax.axis_index("comp")
        return {step: arrays[owner(group, step, size)] for step in range(1, size)}
    return {step: exchange(own, "comp", step) for step in range(1, size)}


def shards(samples, start_vectors):
    comp = lax.axis_size("comp")
    feat = lax.axis_size("feat")
    sample = samples[0]
    rows = sample.shape[0]
    features = sample.shape[1] * feat
    even = comp & (comp - 1) == 0

    blocks = {step: exchange(start_vectors, "comp", step) for step in range(2, comp, 2)} if even else gather(start_vectors)
    projected, vectors, sample = project(
        *(pltpu.with_memory_space_constraint(array, pltpu.HBM) for array in (start_vectors, sample))
    )
    if even and comp > 1:
        blocks[1] = exchange(vectors, "comp", 1)
    parts = terms(projected, "feat", 1)
    projected = sum(parts[1:], parts[0])
    if even:
        others = {step: exchange(projected, "comp", step) for step in range(1, comp) if step == 1 or step % 2 == 0}
    else:
        others = gather(projected)
    near = [1][: comp - 1]
    far = list(range(2, comp))

    def of(arrays, steps):
        return [arrays[step] for step in steps]

    partly = first_part(projected, sample, vectors, near, of(others, near), of(blocks, near), features)
    if even:
        for step in range(2, comp, 2):
            blocks[step], others[step], others[1] = lax.optimization_barrier((blocks[step], others[step], others[1]))
            blocks[step + 1] = exchange(blocks[step], "comp", 1)
            others[step + 1] = exchange(others[step], "comp", 1)
    updated, squares = rest_part(partly, projected, far, of(others, far), of(blocks, far), rows, features)
    return finish(updated, [lax.all_to_all(squares, "feat", split_axis=0, concat_axis=0, tiled=True)], features)


def solution(mesh):
    in_specs = (P(None, None, "feat"), P("comp", "feat"))
    out_specs = P("comp", "feat")
    return jax.shard_map(shards, mesh=mesh, in_specs=in_specs, out_specs=out_specs, check_vma=False)
```

```python
import functools

import jax
import jax.numpy as jnp
from jax import lax
from jax.experimental import pallas as pl
from jax.experimental.pallas import tpu as pltpu
from jax.sharding import PartitionSpec as P

step_rate = 0.1
epsilon = 1e-06
lanes = 128
in_vmem = pl.BlockSpec(memory_space=pltpu.VMEM)
anywhere = pl.BlockSpec(memory_space=pl.ANY)
params = pltpu.CompilerParams(vmem_limit_bytes=16 << 20)


def tile_of(columns, most):
    if columns % lanes:
        return columns
    units = columns // lanes
    return lanes * max(u for u in range(1, most + 1) if units % u == 0)


def halves(array):
    top = array.astype(jnp.bfloat16)
    return top, (array - top.astype(jnp.float32)).astype(jnp.bfloat16)


def product(left, right, transposed=False):
    dims = (((1,), (1 if transposed else 0,)), ((), ()))
    dot = functools.partial(lax.dot_general, dimension_numbers=dims, preferred_element_type=jnp.float32)
    left_top, left_rest = left if isinstance(left, tuple) else halves(left)
    right_top, right_rest = halves(right)
    rows = left_top.shape[0]
    both = dot(jnp.concatenate([left_top, left_rest], axis=0), right_top)
    return both[:rows] + (both[rows:] + dot(left_top, right_rest))


def scale_of(squares, features):
    return lax.rsqrt(squares / features + epsilon)


def loop(columns, most, body, init):
    tile = tile_of(columns, most)
    return lax.fori_loop(0, columns // tile, lambda i, c: body(i, pl.ds(pl.multiple_of(i * tile, tile), tile), c), init, unroll=True)


def project_kernel(x_hbm, s_hbm, out_ref, x_ref, s_ref, sems):
    per_group, columns = x_ref.shape
    rows = s_ref.shape[0]

    def copies(i, here):
        return (
            pltpu.make_async_copy(x_hbm.at[:, here], x_ref.at[:, here], sems.at[0, i]),
            pltpu.make_async_copy(s_hbm.at[:, here], s_ref.at[:, here], sems.at[1, i]),
        )

    def begin(i, here, carry):
        for copy in copies(i, here):
            copy.start()
        return carry

    def body(i, here, carry):
        for copy in copies(i, here):
            copy.wait()
        x = x_ref[:, here]
        projected, squares = carry
        projected += product(x, s_ref[:, here], transposed=True)
        return projected, squares + jnp.sum(x * x, axis=1, keepdims=True)

    loop(columns, 4, begin, 0)
    zeros = jnp.zeros((per_group, rows), jnp.float32), jnp.zeros((per_group, 1), jnp.float32)
    projected, squares = loop(columns, 4, body, zeros)
    out_ref[:, :rows] = projected
    out_ref[:, rows:] = jnp.broadcast_to(squares, (per_group, out_ref.shape[1] - rows))


def project(x, sample):
    per_group, columns = x.shape
    rows = sample.shape[0]
    width = -(-(rows + 1) // lanes) * lanes
    return pl.pallas_call(
        project_kernel,
        in_specs=[anywhere] * 2,
        out_specs=[in_vmem] * 3,
        out_shape=[
            jax.ShapeDtypeStruct((per_group, width), jnp.float32),
            jax.ShapeDtypeStruct(x.shape, jnp.float32),
            jax.ShapeDtypeStruct(sample.shape, jnp.float32),
        ],
        scratch_shapes=[pltpu.SemaphoreType.DMA((2, columns // tile_of(columns, 4)))],
        compiler_params=params,
        name="project",
    )(x, sample)


def images_of(p_ref, rows, features):
    scale = scale_of(p_ref[:, rows : rows + 1], features)
    return p_ref[:, :rows] * scale, scale


def owner(group, step, size):
    return (group + step) % size if size & (size - 1) else group ^ step


def couplings(images, steps, projected_refs, features):
    group, size = lax.axis_index("comp"), lax.axis_size("comp")
    rows = images.shape[1]
    others = []
    for step, p_ref in zip(steps, projected_refs):
        other, scale = images_of(p_ref, rows, features)
        others.append(other * (scale * jnp.where(owner(group, step, size) < group, -step_rate / (features * rows), 0.0)))
    return product(images, jnp.concatenate(others, axis=0), transposed=True)


def first_kernel(features, steps, p_ref, s_ref, x_ref, *refs):
    count = len(steps)
    projected_refs, x_refs, out_ref = refs[:count], refs[count : 2 * count], refs[2 * count]
    rows = s_ref.shape[0]
    images, scale = images_of(p_ref, rows, features)
    shared = product(images, images * scale, transposed=True)
    later = lax.broadcasted_iota(jnp.int32, shared.shape, 0)
    earlier = lax.broadcasted_iota(jnp.int32, shared.shape, 1)
    weights = [images * (step_rate / rows), jnp.where(earlier < later, shared * (-step_rate / (features * rows)), 0.0)]
    if count:
        weights.append(couplings(images, steps, projected_refs, features))
    weights = halves(jnp.concatenate(weights, axis=1))

    def body(i, here, carry):
        x = x_ref[:, here]
        others = [ref[:, here] for ref in x_refs]
        out_ref[:, here] = scale * x + product(weights, jnp.concatenate([s_ref[:, here], x, *others], axis=0))
        return carry

    loop(x_ref.shape[1], 4, body, 0)


def first_part(projected, sample, x, steps, others, blocks, features):
    return pl.pallas_call(
        functools.partial(first_kernel, features, steps),
        in_specs=[in_vmem] * (3 + 2 * len(steps)),
        out_specs=in_vmem,
        out_shape=jax.ShapeDtypeStruct(x.shape, jnp.float32),
        compiler_params=params,
        name="first_part",
    )(projected, sample, x, *others, *blocks)


def rest_kernel(features, rows, steps, t_ref, p_ref, *refs):
    count = len(steps)
    projected_refs, x_refs, (out_ref, squares_ref) = refs[:count], refs[count : 2 * count], refs[2 * count :]
    per_group, columns = t_ref.shape
    if count:
        weights = halves(couplings(images_of(p_ref, rows, features)[0], steps, projected_refs, features))

    def body(i, here, squares):
        updated = t_ref[:, here]
        if count:
            updated += product(weights, jnp.concatenate([ref[:, here] for ref in x_refs], axis=0))
        out_ref[:, here] = updated
        return squares + jnp.sum(updated * updated, axis=1, keepdims=True)

    squares = loop(columns, 4, body, jnp.zeros((per_group, 1), jnp.float32))
    spread = jnp.broadcast_to(squares, (per_group, per_group))
    squares_ref[...] = jnp.sum(jnp.where(diagonal(per_group), spread, 0.0), axis=0, keepdims=True)


def rest_part(partly, projected, steps, others, blocks, rows, features):
    return pl.pallas_call(
        functools.partial(rest_kernel, features, rows, steps),
        in_specs=[in_vmem] * (2 + 2 * len(steps)),
        out_specs=[in_vmem, in_vmem],
        out_shape=[
            jax.ShapeDtypeStruct(partly.shape, jnp.float32),
            jax.ShapeDtypeStruct((1, partly.shape[0]), jnp.float32),
        ],
        compiler_params=params,
        name="rest_part",
    )(partly, projected, *others, *blocks)


def diagonal(count):
    down = lax.broadcasted_iota(jnp.int32, (count, count), 0)
    across = lax.broadcasted_iota(jnp.int32, (count, count), 1)
    return down == across


def finish_kernel(features, count, updated_ref, *refs):
    squares_refs, (out_ref, scaled, sems) = refs[:count], refs[count:]
    per_group, columns = updated_ref.shape
    squares = squares_refs[0][...]
    for ref in squares_refs[1:]:
        squares += ref[...]
    spread = jnp.broadcast_to(scale_of(squares, features), (per_group, per_group))
    scale = jnp.sum(jnp.where(diagonal(per_group), spread, 0.0), axis=1, keepdims=True)
    tile = tile_of(columns, 7)
    copies = []
    for i in range(columns // tile):
        here = pl.ds(i * tile, tile)
        scaled[:, here] = updated_ref[:, here] * scale
        copies.append(pltpu.make_async_copy(scaled.at[:, here], out_ref.at[:, here], sems.at[i]))
        copies[-1].start()
    for copy in copies:
        copy.wait()


def finish(updated, squares, features):
    count = len(squares)
    return pl.pallas_call(
        functools.partial(finish_kernel, features, count),
        in_specs=[in_vmem] * (1 + count),
        out_specs=anywhere,
        out_shape=jax.ShapeDtypeStruct(updated.shape, jnp.float32),
        scratch_shapes=[
            pltpu.VMEM(updated.shape, jnp.float32),
            pltpu.SemaphoreType.DMA((updated.shape[1] // tile_of(updated.shape[1], 7),)),
        ],
        compiler_params=params,
        name="finish",
    )(updated, *squares)


def exchange(array, axis, step):
    return lax.ppermute(array, axis, [(i, i ^ step) for i in range(lax.axis_size(axis))])


def terms(array, axis, together):
    size = lax.axis_size(axis)
    if size & (size - 1):
        return [lax.psum(array, axis)]
    parts, step = [array], 1
    while step < size:
        array = sum(parts[1:], parts[0])
        width = min(1 << together, size // step)
        parts = [array] + [exchange(array, axis, step * k) for k in range(1, width)]
        step *= width
    return parts


def gather(own):
    size = lax.axis_size("comp")
    if size & (size - 1):
        arrays, group = lax.all_gather(own, "comp"), lax.axis_index("comp")
        return {step: arrays[owner(group, step, size)] for step in range(1, size)}
    return {step: exchange(own, "comp", step) for step in range(1, size)}


def shards(samples, start_vectors):
    comp = lax.axis_size("comp")
    feat = lax.axis_size("feat")
    sample = samples[0]
    rows = sample.shape[0]
    features = sample.shape[1] * feat
    even = comp & (comp - 1) == 0

    blocks = {step: exchange(start_vectors, "comp", step) for step in range(2, comp, 2)} if even else gather(start_vectors)
    projected, vectors, sample = project(
        *(pltpu.with_memory_space_constraint(array, pltpu.HBM) for array in (start_vectors, sample))
    )
    if even and comp > 1:
        blocks[1] = exchange(vectors, "comp", 1)
    parts = terms(projected, "feat", 1)
    projected = sum(parts[1:], parts[0])
    if even:
        others = {step: exchange(projected, "comp", step) for step in range(1, comp, 2)}
    else:
        others = gather(projected)
    near = [1][: comp - 1]
    far = list(range(2, comp))

    def of(arrays, steps):
        return [arrays[step] for step in steps]

    partly = first_part(projected, sample, vectors, near, of(others, near), of(blocks, near), features)
    if even:
        for step in range(2, comp, 2):
            blocks[step], others[step + 1], others[1] = lax.optimization_barrier(
                (blocks[step], others[step + 1], others[1])
            )
            blocks[step + 1] = exchange(blocks[step], "comp", 1)
            others[step] = exchange(others[step + 1], "comp", 1)
    updated, squares = rest_part(partly, projected, far, of(others, far), of(blocks, far), rows, features)
    return finish(updated, terms(squares, "feat", 2), features)


def solution(mesh):
    in_specs = (P(None, None, "feat"), P("comp", "feat"))
    out_specs = P("comp", "feat")
    return jax.shard_map(shards, mesh=mesh, in_specs=in_specs, out_specs=out_specs, check_vma=False)
```

```python
import functools

import jax
import jax.numpy as jnp
from jax import lax
from jax.experimental import pallas as pl
from jax.experimental.pallas import tpu as pltpu
from jax.sharding import PartitionSpec as P

step_rate = 0.1
epsilon = 1e-06
lanes = 128
in_vmem = pl.BlockSpec(memory_space=pltpu.VMEM)
anywhere = pl.BlockSpec(memory_space=pl.ANY)
params = pltpu.CompilerParams(vmem_limit_bytes=16 << 20)


def tile_of(columns, most):
    if columns % lanes:
        return columns
    units = columns // lanes
    return lanes * max(u for u in range(1, most + 1) if units % u == 0)


def halves(array):
    top = array.astype(jnp.bfloat16)
    return top, (array - top.astype(jnp.float32)).astype(jnp.bfloat16)


def product(left, right, transposed=False):
    dims = (((1,), (1 if transposed else 0,)), ((), ()))
    dot = functools.partial(lax.dot_general, dimension_numbers=dims, preferred_element_type=jnp.float32)
    left_top, left_rest = left if isinstance(left, tuple) else halves(left)
    right_top, right_rest = halves(right)
    rows = left_top.shape[0]
    both = dot(jnp.concatenate([left_top, left_rest], axis=0), right_top)
    return both[:rows] + (both[rows:] + dot(left_top, right_rest))


def scale_of(squares, features):
    return lax.rsqrt(squares / features + epsilon)


def loop(columns, most, body, init):
    tile = tile_of(columns, most)
    return lax.fori_loop(0, columns // tile, lambda i, c: body(i, pl.ds(pl.multiple_of(i * tile, tile), tile), c), init, unroll=True)


def project_kernel(x_hbm, s_hbm, out_ref, x_ref, s_ref, sems):
    per_group, columns = x_ref.shape
    rows = s_ref.shape[0]

    def copies(i, here):
        return (
            pltpu.make_async_copy(x_hbm.at[:, here], x_ref.at[:, here], sems.at[0, i]),
            pltpu.make_async_copy(s_hbm.at[:, here], s_ref.at[:, here], sems.at[1, i]),
        )

    def begin(i, here, carry):
        for copy in copies(i, here):
            copy.start()
        return carry

    def body(i, here, carry):
        for copy in copies(i, here):
            copy.wait()
        x = x_ref[:, here]
        projected, squares = carry
        projected += product(x, s_ref[:, here], transposed=True)
        return projected, squares + jnp.sum(x * x, axis=1, keepdims=True)

    loop(columns, 4, begin, 0)
    zeros = jnp.zeros((per_group, rows), jnp.float32), jnp.zeros((per_group, 1), jnp.float32)
    projected, squares = loop(columns, 4, body, zeros)
    out_ref[:, :rows] = projected
    out_ref[:, rows:] = jnp.broadcast_to(squares, (per_group, out_ref.shape[1] - rows))


def project(x, sample):
    per_group, columns = x.shape
    rows = sample.shape[0]
    width = -(-(rows + 1) // lanes) * lanes
    return pl.pallas_call(
        project_kernel,
        in_specs=[anywhere] * 2,
        out_specs=[in_vmem] * 3,
        out_shape=[
            jax.ShapeDtypeStruct((per_group, width), jnp.float32),
            jax.ShapeDtypeStruct(x.shape, jnp.float32),
            jax.ShapeDtypeStruct(sample.shape, jnp.float32),
        ],
        scratch_shapes=[pltpu.SemaphoreType.DMA((2, columns // tile_of(columns, 4)))],
        compiler_params=params,
        name="project",
    )(x, sample)


def images_of(p_ref, rows, features):
    scale = scale_of(p_ref[:, rows : rows + 1], features)
    return p_ref[:, :rows] * scale, scale


def owner(group, step, size):
    return (group + step) % size if size & (size - 1) else group ^ step


def couplings(images, steps, projected_refs, features):
    group, size = lax.axis_index("comp"), lax.axis_size("comp")
    rows = images.shape[1]
    others = []
    for step, p_ref in zip(steps, projected_refs):
        other, scale = images_of(p_ref, rows, features)
        others.append(other * (scale * jnp.where(owner(group, step, size) < group, -step_rate / (features * rows), 0.0)))
    return product(images, jnp.concatenate(others, axis=0), transposed=True)


def first_kernel(features, steps, p_ref, s_ref, x_ref, *refs):
    count = len(steps)
    projected_refs, x_refs, out_ref = refs[:count], refs[count : 2 * count], refs[2 * count]
    rows = s_ref.shape[0]
    images, scale = images_of(p_ref, rows, features)
    shared = product(images, images * scale, transposed=True)
    later = lax.broadcasted_iota(jnp.int32, shared.shape, 0)
    earlier = lax.broadcasted_iota(jnp.int32, shared.shape, 1)
    weights = [images * (step_rate / rows), jnp.where(earlier < later, shared * (-step_rate / (features * rows)), 0.0)]
    if count:
        weights.append(couplings(images, steps, projected_refs, features))
    weights = halves(jnp.concatenate(weights, axis=1))

    def body(i, here, carry):
        x = x_ref[:, here]
        others = [ref[:, here] for ref in x_refs]
        out_ref[:, here] = scale * x + product(weights, jnp.concatenate([s_ref[:, here], x, *others], axis=0))
        return carry

    loop(x_ref.shape[1], 4, body, 0)


def first_part(projected, sample, x, steps, others, blocks, features):
    return pl.pallas_call(
        functools.partial(first_kernel, features, steps),
        in_specs=[in_vmem] * (3 + 2 * len(steps)),
        out_specs=in_vmem,
        out_shape=jax.ShapeDtypeStruct(x.shape, jnp.float32),
        compiler_params=params,
        name="first_part",
    )(projected, sample, x, *others, *blocks)


def rest_kernel(features, rows, steps, t_ref, p_ref, *refs):
    count = len(steps)
    projected_refs, x_refs, (out_ref, squares_ref) = refs[:count], refs[count : 2 * count], refs[2 * count :]
    per_group, columns = t_ref.shape
    if count:
        weights = halves(couplings(images_of(p_ref, rows, features)[0], steps, projected_refs, features))

    def body(i, here, squares):
        updated = t_ref[:, here]
        if count:
            updated += product(weights, jnp.concatenate([ref[:, here] for ref in x_refs], axis=0))
        out_ref[:, here] = updated
        return squares + jnp.sum(updated * updated, axis=1, keepdims=True)

    squares = loop(columns, 4, body, jnp.zeros((per_group, 1), jnp.float32))
    spread = jnp.broadcast_to(squares, (per_group, per_group))
    squares_ref[...] = jnp.sum(jnp.where(diagonal(per_group), spread, 0.0), axis=0, keepdims=True)


def rest_part(partly, projected, steps, others, blocks, rows, features):
    return pl.pallas_call(
        functools.partial(rest_kernel, features, rows, steps),
        in_specs=[in_vmem] * (2 + 2 * len(steps)),
        out_specs=[in_vmem, in_vmem],
        out_shape=[
            jax.ShapeDtypeStruct(partly.shape, jnp.float32),
            jax.ShapeDtypeStruct((1, partly.shape[0]), jnp.float32),
        ],
        compiler_params=params,
        name="rest_part",
    )(partly, projected, *others, *blocks)


def diagonal(count):
    down = lax.broadcasted_iota(jnp.int32, (count, count), 0)
    across = lax.broadcasted_iota(jnp.int32, (count, count), 1)
    return down == across


def finish_kernel(features, count, updated_ref, *refs):
    squares_refs, (out_ref, scaled, sems) = refs[:count], refs[count:]
    per_group, columns = updated_ref.shape
    squares = squares_refs[0][...]
    for ref in squares_refs[1:]:
        squares += ref[...]
    spread = jnp.broadcast_to(scale_of(squares, features), (per_group, per_group))
    scale = jnp.sum(jnp.where(diagonal(per_group), spread, 0.0), axis=1, keepdims=True)
    tile = tile_of(columns, 7)
    copies = []
    for i in range(columns // tile):
        here = pl.ds(i * tile, tile)
        scaled[:, here] = updated_ref[:, here] * scale
        copies.append(pltpu.make_async_copy(scaled.at[:, here], out_ref.at[:, here], sems.at[i]))
        copies[-1].start()
    for copy in copies:
        copy.wait()


def finish(updated, squares, features):
    count = len(squares)
    return pl.pallas_call(
        functools.partial(finish_kernel, features, count),
        in_specs=[in_vmem] * (1 + count),
        out_specs=anywhere,
        out_shape=jax.ShapeDtypeStruct(updated.shape, jnp.float32),
        scratch_shapes=[
            pltpu.VMEM(updated.shape, jnp.float32),
            pltpu.SemaphoreType.DMA((updated.shape[1] // tile_of(updated.shape[1], 7),)),
        ],
        compiler_params=params,
        name="finish",
    )(updated, *squares)


def exchange(array, axis, step):
    return lax.ppermute(array, axis, [(i, i ^ step) for i in range(lax.axis_size(axis))])


def terms(array, axis, together):
    size = lax.axis_size(axis)
    if size & (size - 1):
        return [lax.psum(array, axis)]
    parts, step = [array], 1
    while step < size:
        array = sum(parts[1:], parts[0])
        width = min(1 << together, size // step)
        parts = [array] + [exchange(array, axis, step * k) for k in range(1, width)]
        step *= width
    return parts


def flipped_terms(array):
    comp, feat = lax.axis_size("comp"), lax.axis_size("feat")
    if comp % 2 or comp & (comp - 1) or feat & (feat - 1):
        return terms(array, "feat", 2)
    widths, step = [], 1
    while step < feat:
        widths.append(min(4, feat // step))
        step *= widths[-1]
    parts, step = [array], 1
    for stage, width in enumerate(widths):
        array = sum(parts[1:], parts[0])
        flip = int(stage + 1 < len(widths) or len(widths) % 2 == 0)
        parts = [] if flip else [array]
        for k in range(0 if flip else 1, width):
            pairs = [
                (i * feat + j, (i ^ flip) * feat + (j ^ (k * step))) for i in range(comp) for j in range(feat)
            ]
            parts.append(lax.ppermute(array, ("comp", "feat"), pairs))
        step *= width
    return parts


def gather(own):
    size = lax.axis_size("comp")
    if size & (size - 1):
        arrays, group = lax.all_gather(own, "comp"), lax.axis_index("comp")
        return {step: arrays[owner(group, step, size)] for step in range(1, size)}
    return {step: exchange(own, "comp", step) for step in range(1, size)}


def shards(samples, start_vectors):
    comp = lax.axis_size("comp")
    feat = lax.axis_size("feat")
    sample = samples[0]
    rows = sample.shape[0]
    features = sample.shape[1] * feat
    even = comp & (comp - 1) == 0

    blocks = {step: exchange(start_vectors, "comp", step) for step in range(2, comp, 2)} if even else gather(start_vectors)
    projected, vectors, sample = project(
        *(pltpu.with_memory_space_constraint(array, pltpu.HBM) for array in (start_vectors, sample))
    )
    if even and comp > 1:
        blocks[1] = exchange(vectors, "comp", 1)
    parts = terms(projected, "feat", 1)
    projected = sum(parts[1:], parts[0])
    if even:
        others = {step: exchange(projected, "comp", step) for step in range(1, comp, 2)}
    else:
        others = gather(projected)
    near = [1][: comp - 1]
    far = list(range(2, comp))

    def of(arrays, steps):
        return [arrays[step] for step in steps]

    partly = first_part(projected, sample, vectors, near, of(others, near), of(blocks, near), features)
    if even:
        for step in range(2, comp, 2):
            blocks[step], others[step + 1], others[1] = lax.optimization_barrier(
                (blocks[step], others[step + 1], others[1])
            )
            blocks[step + 1] = exchange(blocks[step], "comp", 1)
            others[step] = exchange(others[step + 1], "comp", 1)
    updated, squares = rest_part(partly, projected, far, of(others, far), of(blocks, far), rows, features)
    return finish(updated, flipped_terms(squares), features)


def solution(mesh):
    in_specs = (P(None, None, "feat"), P("comp", "feat"))
    out_specs = P("comp", "feat")
    return jax.shard_map(shards, mesh=mesh, in_specs=in_specs, out_specs=out_specs, check_vma=False)
```

```python
import functools

import jax
import jax.numpy as jnp
from jax import lax
from jax.experimental import pallas as pl
from jax.experimental.pallas import tpu as pltpu
from jax.sharding import PartitionSpec as P

step_rate = 0.1
epsilon = 1e-06
lanes = 128
in_vmem = pl.BlockSpec(memory_space=pltpu.VMEM)
anywhere = pl.BlockSpec(memory_space=pl.ANY)
params = pltpu.CompilerParams(vmem_limit_bytes=16 << 20)


def tile_of(columns, most):
    if columns % lanes:
        return columns
    units = columns // lanes
    return lanes * max(u for u in range(1, most + 1) if units % u == 0)


def halves(array):
    top = array.astype(jnp.bfloat16)
    return top, (array - top.astype(jnp.float32)).astype(jnp.bfloat16)


def product(left, right, transposed=False):
    dims = (((1,), (1 if transposed else 0,)), ((), ()))
    dot = functools.partial(lax.dot_general, dimension_numbers=dims, preferred_element_type=jnp.float32)
    left_top, left_rest = left if isinstance(left, tuple) else halves(left)
    right_top, right_rest = halves(right)
    rows = left_top.shape[0]
    both = dot(jnp.concatenate([left_top, left_rest], axis=0), right_top)
    return both[:rows] + (both[rows:] + dot(left_top, right_rest))


def scale_of(squares, features):
    return lax.rsqrt(squares / features + epsilon)


def loop(columns, most, body, init):
    tile = tile_of(columns, most)
    for i in range(columns // tile):
        init = body(i, pl.ds(i * tile, tile), init)
    return init


def columns_at(held, here):
    width = held[0].shape[1]
    wanted = range(here.start, here.start + here.size)
    parts = []
    for k, ref in enumerate(held):
        first, last = max(wanted.start, k * width), min(wanted.stop, (k + 1) * width)
        if first < last:
            parts.append(ref[:, first - k * width : last - k * width])
    return parts[0] if len(parts) == 1 else jnp.concatenate(parts, axis=1)


def pieces_of(columns):
    tile = tile_of(columns, columns // (4 * lanes) or 1)
    return [slice(start, start + tile) for start in range(0, columns, tile)]


def project_kernel(x_hbm, s_hbm, out_ref, x_ref, s_ref, sems):
    per_group, columns = x_ref.shape
    rows = s_ref.shape[0]

    def copies(i, here):
        return (
            pltpu.make_async_copy(x_hbm.at[:, here], x_ref.at[:, here], sems.at[0, i]),
            pltpu.make_async_copy(s_hbm.at[:, here], s_ref.at[:, here], sems.at[1, i]),
        )

    def begin(i, here, carry):
        for copy in copies(i, here):
            copy.start()
        return carry

    def body(i, here, carry):
        for copy in copies(i, here):
            copy.wait()
        x = x_ref[:, here]
        projected, squares = carry
        projected += product(x, s_ref[:, here], transposed=True)
        return projected, squares + jnp.sum(x * x, axis=1, keepdims=True)

    loop(columns, 4, begin, 0)
    zeros = jnp.zeros((per_group, rows), jnp.float32), jnp.zeros((per_group, 1), jnp.float32)
    projected, squares = loop(columns, 4, body, zeros)
    out_ref[:, :rows] = projected
    out_ref[:, rows:] = jnp.broadcast_to(squares, (per_group, out_ref.shape[1] - rows))


def project(x, sample):
    per_group, columns = x.shape
    rows = sample.shape[0]
    width = -(-(rows + 1) // lanes) * lanes
    return pl.pallas_call(
        project_kernel,
        in_specs=[anywhere] * 2,
        out_specs=[in_vmem] * 3,
        out_shape=[
            jax.ShapeDtypeStruct((per_group, width), jnp.float32),
            jax.ShapeDtypeStruct(x.shape, jnp.float32),
            jax.ShapeDtypeStruct(sample.shape, jnp.float32),
        ],
        scratch_shapes=[pltpu.SemaphoreType.DMA((2, columns // tile_of(columns, 4)))],
        compiler_params=params,
        name="project",
    )(x, sample)


def images_of(p_ref, rows, features):
    scale = scale_of(p_ref[:, rows : rows + 1], features)
    return p_ref[:, :rows] * scale, scale


def owner(group, step, size):
    return (group + step) % size if size & (size - 1) else group ^ step


def couplings(images, steps, projected_refs, features):
    group, size = lax.axis_index("comp"), lax.axis_size("comp")
    rows = images.shape[1]
    others = []
    for step, p_ref in zip(steps, projected_refs):
        other, scale = images_of(p_ref, rows, features)
        others.append(other * (scale * jnp.where(owner(group, step, size) < group, -step_rate / (features * rows), 0.0)))
    return product(images, jnp.concatenate(others, axis=0), transposed=True)


def first_kernel(features, steps, p_ref, s_ref, x_ref, *refs):
    count = len(steps)
    projected_refs, x_refs, out_ref = refs[:count], refs[count : 2 * count], refs[2 * count]
    rows = s_ref.shape[0]
    images, scale = images_of(p_ref, rows, features)
    shared = product(images, images * scale, transposed=True)
    later = lax.broadcasted_iota(jnp.int32, shared.shape, 0)
    earlier = lax.broadcasted_iota(jnp.int32, shared.shape, 1)
    weights = [images * (step_rate / rows), jnp.where(earlier < later, shared * (-step_rate / (features * rows)), 0.0)]
    if count:
        weights.append(couplings(images, steps, projected_refs, features))
    weights = halves(jnp.concatenate(weights, axis=1))

    def body(i, here, carry):
        x = x_ref[:, here]
        others = [ref[:, here] for ref in x_refs]
        out_ref[:, here] = scale * x + product(weights, jnp.concatenate([s_ref[:, here], x, *others], axis=0))
        return carry

    loop(x_ref.shape[1], 4, body, 0)


def first_part(projected, sample, x, steps, others, blocks, features):
    return pl.pallas_call(
        functools.partial(first_kernel, features, steps),
        in_specs=[in_vmem] * (3 + 2 * len(steps)),
        out_specs=in_vmem,
        out_shape=jax.ShapeDtypeStruct(x.shape, jnp.float32),
        compiler_params=params,
        name="first_part",
    )(projected, sample, x, *others, *blocks)


def rest_kernel(features, rows, steps, t_ref, p_ref, *refs):
    count = len(steps)
    projected_refs, x_refs, (out_ref, squares_ref) = refs[:count], list(refs[count:-2]), refs[-2:]
    per_group, columns = t_ref.shape
    far = []
    for step in steps:
        held = [x_refs.pop(0)]
        while sum(ref.shape[1] for ref in held) < columns:
            held.append(x_refs.pop(0))
        far.append(held)
    if count:
        weights = halves(couplings(images_of(p_ref, rows, features)[0], steps, projected_refs, features))

    def body(i, here, squares):
        updated = t_ref[:, here]
        if count:
            updated += product(weights, jnp.concatenate([columns_at(held, here) for held in far], axis=0))
        out_ref[:, here] = updated
        return squares + jnp.sum(updated * updated, axis=1, keepdims=True)

    squares = loop(columns, 4, body, jnp.zeros((per_group, 1), jnp.float32))
    spread = jnp.broadcast_to(squares, (per_group, per_group))
    squares_ref[...] = jnp.sum(jnp.where(diagonal(per_group), spread, 0.0), axis=0, keepdims=True)


def rest_part(partly, projected, steps, others, blocks, rows, features):
    return pl.pallas_call(
        functools.partial(rest_kernel, features, rows, steps),
        in_specs=[in_vmem] * (2 + len(others) + len(blocks)),
        out_specs=[in_vmem, in_vmem],
        out_shape=[
            jax.ShapeDtypeStruct(partly.shape, jnp.float32),
            jax.ShapeDtypeStruct((1, partly.shape[0]), jnp.float32),
        ],
        compiler_params=params,
        name="rest_part",
    )(partly, projected, *others, *blocks)


def diagonal(count):
    down = lax.broadcasted_iota(jnp.int32, (count, count), 0)
    across = lax.broadcasted_iota(jnp.int32, (count, count), 1)
    return down == across


def finish_kernel(features, count, updated_ref, *refs):
    squares_refs, (out_ref, scaled, sems) = refs[:count], refs[count:]
    per_group, columns = updated_ref.shape
    squares = squares_refs[0][...]
    for ref in squares_refs[1:]:
        squares += ref[...]
    spread = jnp.broadcast_to(scale_of(squares, features), (per_group, per_group))
    scale = jnp.sum(jnp.where(diagonal(per_group), spread, 0.0), axis=1, keepdims=True)
    tile = tile_of(columns, 7)
    copies = []
    for i in range(columns // tile):
        here = pl.ds(i * tile, tile)
        scaled[:, here] = updated_ref[:, here] * scale
        copies.append(pltpu.make_async_copy(scaled.at[:, here], out_ref.at[:, here], sems.at[i]))
        copies[-1].start()
    for copy in copies:
        copy.wait()


def finish(updated, squares, features):
    count = len(squares)
    return pl.pallas_call(
        functools.partial(finish_kernel, features, count),
        in_specs=[in_vmem] * (1 + count),
        out_specs=anywhere,
        out_shape=jax.ShapeDtypeStruct(updated.shape, jnp.float32),
        scratch_shapes=[
            pltpu.VMEM(updated.shape, jnp.float32),
            pltpu.SemaphoreType.DMA((updated.shape[1] // tile_of(updated.shape[1], 7),)),
        ],
        compiler_params=params,
        name="finish",
    )(updated, *squares)


def exchange(array, axis, step):
    return lax.ppermute(array, axis, [(i, i ^ step) for i in range(lax.axis_size(axis))])


def terms(array, axis, together):
    size = lax.axis_size(axis)
    if size & (size - 1):
        return [lax.psum(array, axis)]
    parts, step = [array], 1
    while step < size:
        array = sum(parts[1:], parts[0])
        width = min(1 << together, size // step)
        parts = [array] + [exchange(array, axis, step * k) for k in range(1, width)]
        step *= width
    return parts


def flipped_terms(array):
    comp, feat = lax.axis_size("comp"), lax.axis_size("feat")
    if comp % 2 or comp & (comp - 1) or feat & (feat - 1):
        return terms(array, "feat", 2)
    widths, step = [], 1
    while step < feat:
        widths.append(min(4, feat // step))
        step *= widths[-1]
    parts, step = [array], 1
    for stage, width in enumerate(widths):
        array = sum(parts[1:], parts[0])
        flip = int(stage + 1 < len(widths) or len(widths) % 2 == 0)
        parts = [] if flip else [array]
        for k in range(0 if flip else 1, width):
            pairs = [
                (i * feat + j, (i ^ flip) * feat + (j ^ (k * step))) for i in range(comp) for j in range(feat)
            ]
            parts.append(lax.ppermute(array, ("comp", "feat"), pairs))
        step *= width
    return parts


def gather(own):
    size = lax.axis_size("comp")
    if size & (size - 1):
        arrays, group = lax.all_gather(own, "comp"), lax.axis_index("comp")
        return {step: arrays[owner(group, step, size)] for step in range(1, size)}
    return {step: exchange(own, "comp", step) for step in range(1, size)}


def shards(samples, start_vectors):
    comp = lax.axis_size("comp")
    feat = lax.axis_size("feat")
    sample = samples[0]
    rows = sample.shape[0]
    features = sample.shape[1] * feat
    even = comp & (comp - 1) == 0

    blocks = {step: exchange(start_vectors, "comp", step) for step in range(2, comp, 2)} if even else gather(start_vectors)
    projected, vectors, sample = project(
        *(pltpu.with_memory_space_constraint(array, pltpu.HBM) for array in (start_vectors, sample))
    )
    if even and comp > 1:
        blocks[1] = exchange(vectors, "comp", 1)
    parts = terms(projected, "feat", 1)
    projected = sum(parts[1:], parts[0])
    if even:
        others = {step: exchange(projected, "comp", step) for step in range(1, comp) if step == 1 or step % 2 == 0}
    else:
        others = gather(projected)
    near = [1][: comp - 1]
    far = list(range(2, comp))

    def of(arrays, steps):
        return [piece for step in steps for piece in (arrays[step] if isinstance(arrays[step], list) else [arrays[step]])]

    partly = first_part(projected, sample, vectors, near, of(others, near), of(blocks, near), features)
    if even:
        for step in range(2, comp, 2):
            blocks[step], others[1] = lax.optimization_barrier((blocks[step], others[1]))
            blocks[step + 1] = [exchange(blocks[step][:, here], "comp", 1) for here in pieces_of(blocks[step].shape[1])]
            others[step + 1] = exchange(others[step], "comp", 1)
    updated, squares = rest_part(partly, projected, far, of(others, far), of(blocks, far), rows, features)
    return finish(updated, flipped_terms(squares), features)


def solution(mesh):
    in_specs = (P(None, None, "feat"), P("comp", "feat"))
    out_specs = P("comp", "feat")
    return jax.shard_map(shards, mesh=mesh, in_specs=in_specs, out_specs=out_specs, check_vma=False)
```

```python
import functools
import math

import jax
import jax.numpy as jnp
from jax import lax
from jax.experimental import pallas as pl
from jax.experimental.pallas import tpu as pltpu
from jax.sharding import PartitionSpec as P

step_rate = 0.1
epsilon = 1e-06
lanes = 128
in_vmem = pl.BlockSpec(memory_space=pltpu.VMEM)
anywhere = pl.BlockSpec(memory_space=pl.ANY)
params = pltpu.CompilerParams(vmem_limit_bytes=16 << 20)


def tile_of(columns, most):
    if columns % lanes:
        return columns
    units = columns // lanes
    return lanes * max(u for u in range(1, most + 1) if units % u == 0)


def halves(array):
    top = array.astype(jnp.bfloat16)
    return top, (array - top.astype(jnp.float32)).astype(jnp.bfloat16)


def product(left, right, transposed=False):
    dims = (((1,), (1 if transposed else 0,)), ((), ()))
    dot = functools.partial(lax.dot_general, dimension_numbers=dims, preferred_element_type=jnp.float32)
    left_top, left_rest = left if isinstance(left, tuple) else halves(left)
    right_top, right_rest = halves(right)
    rows = left_top.shape[0]
    both = dot(jnp.concatenate([left_top, left_rest], axis=0), right_top)
    return both[:rows] + (both[rows:] + dot(left_top, right_rest))


def scale_of(squares, features):
    return lax.rsqrt(squares / features + epsilon)


def tiles_of(columns, most):
    tile = tile_of(columns, most)
    return [pl.ds(start, tile) for start in range(0, columns, tile)]


def place_of(columns, width):
    core = lax.rem(lax.axis_index("comp"), 2)
    return core, pl.multiple_of(core * (columns - width), lanes)


def project_kernel(x_hbm, s_hbm, out_ref, s_ref, x_ref, sems):
    rows, columns = s_ref.shape
    copies = []
    for i, here in enumerate(tiles_of(columns, 4)):
        copies.append(
            (
                pltpu.make_async_copy(x_hbm.at[:, here], x_ref.at[:, here], sems.at[0, i]),
                pltpu.make_async_copy(s_hbm.at[:, here], s_ref.at[:, here], sems.at[1, i]),
            )
        )
        for copy in copies[-1]:
            copy.start()
    projected, squares = 0.0, 0.0
    for i, here in enumerate(tiles_of(columns, 4)):
        for copy in copies[i]:
            copy.wait()
        x = x_ref[:, here]
        projected += product(x, s_ref[:, here], transposed=True)
        squares += jnp.sum(x * x, axis=1, keepdims=True)
    out_ref[:, :rows] = projected
    out_ref[:, rows:] = jnp.broadcast_to(squares, (out_ref.shape[0], out_ref.shape[1] - rows))


def project(x, sample):
    per_group, columns = x.shape
    rows = sample.shape[0]
    width = -(-(rows + 1) // lanes) * lanes
    return pl.pallas_call(
        project_kernel,
        in_specs=[anywhere] * 2,
        out_specs=[in_vmem] * 2,
        out_shape=[
            jax.ShapeDtypeStruct((per_group, width), jnp.float32),
            jax.ShapeDtypeStruct(sample.shape, jnp.float32),
        ],
        scratch_shapes=[
            pltpu.VMEM(x.shape, jnp.float32),
            pltpu.SemaphoreType.DMA((2, columns // tile_of(columns, 4))),
        ],
        compiler_params=params,
        name="project",
    )(x, sample)


def images_of(p_ref, rows, features):
    scale = scale_of(p_ref[:, rows : rows + 1], features)
    return p_ref[:, :rows] * scale, scale


def chip_kernel(features, cores, p_ref, q_ref, s_ref, x_ref, y_ref, out_ref):
    rows, columns = s_ref.shape
    per_group, width = x_ref.shape
    core, start = place_of(columns, width)
    images, scales = zip(*(images_of(ref, rows, features) for ref in (p_ref, q_ref)))
    images, scale = jnp.concatenate(images, axis=0), jnp.concatenate(scales, axis=0)
    shared = product(images, images * scale, transposed=True)

    def component(axis):
        index = lax.broadcasted_iota(jnp.int32, shared.shape, axis)
        own = index < per_group
        return jnp.where(own, index + core * per_group, index - core * per_group)

    earlier = component(1) < component(0)
    coupling = jnp.where(earlier, shared * (-step_rate / (features * rows)), 0.0)
    weights = halves(jnp.concatenate([images * (step_rate / rows), coupling], axis=1))
    for here in tiles_of(width, 4):
        there = pl.ds(pl.multiple_of(start + here.start, lanes), here.size)
        vectors = jnp.concatenate([x_ref[:, here], y_ref[:, here]], axis=0)
        out_ref[:, here] = scale * vectors + product(weights, jnp.concatenate([s_ref[:, there], vectors], axis=0))


def chip_part(projected, beside, sample, mine, near, features):
    return pl.pallas_call(
        functools.partial(chip_kernel, features, 2),
        in_specs=[in_vmem] * 5,
        out_specs=in_vmem,
        out_shape=jax.ShapeDtypeStruct((2 * mine.shape[0], mine.shape[1]), jnp.float32),
        compiler_params=params,
        name="chip_part",
    )(projected, beside, sample, mine, near)


def diagonal(count):
    down = lax.broadcasted_iota(jnp.int32, (count, count), 0)
    across = lax.broadcasted_iota(jnp.int32, (count, count), 1)
    return down == across


def as_row(column):
    count = column.shape[0]
    return jnp.sum(jnp.where(diagonal(count), jnp.broadcast_to(column, (count, count)), 0.0), axis=0, keepdims=True)


def rest_kernel(features, rows, columns, steps, t_ref, p_ref, q_ref, *refs):
    count = 2 * len(steps)
    projected_refs, x_refs, (own_ref, other_ref, squares_ref) = refs[:count], refs[count : 2 * count], refs[2 * count :]
    width = t_ref.shape[1]
    per_group = t_ref.shape[0] // 2
    core = place_of(columns, width)[0]
    chip = lax.axis_index("comp") // 2
    if steps:
        images = jnp.concatenate([images_of(ref, rows, features)[0] for ref in (p_ref, q_ref)], axis=0)
        others = []
        for k, ref in enumerate(projected_refs):
            other, scale = images_of(ref, rows, features)
            factor = jnp.where(chip ^ (steps[k // 2] // 2) < chip, -step_rate / (features * rows), 0.0)
            others.append(other * (scale * factor))
        weights = halves(product(images, jnp.concatenate(others, axis=0), transposed=True))
    overlap = 2 * width - columns
    squares = 0.0
    for here in tiles_of(width, 4):
        updated = t_ref[:, here]
        if steps:
            updated += product(weights, jnp.concatenate([ref[:, here] for ref in x_refs], axis=0))
        own_ref[:, here], other_ref[:, here] = updated[:per_group], updated[per_group:]
        if here.start < overlap:
            column = here.start + lax.broadcasted_iota(jnp.int32, updated.shape, 1)
            updated = jnp.where((core == 0) | (column >= overlap), updated, 0.0)
        squares += jnp.sum(updated * updated, axis=1, keepdims=True)
    own, other = as_row(squares[:per_group]), as_row(squares[per_group:])
    squares_ref[0:1, :] = jnp.where(core == 0, own, other)
    squares_ref[1:2, :] = jnp.where(core == 0, other, own)


def rest_part(partly, projected, beside, steps, others, blocks, rows, columns, features):
    per_group, width = partly.shape[0] // 2, partly.shape[1]
    return pl.pallas_call(
        functools.partial(rest_kernel, features, rows, columns, steps),
        in_specs=[in_vmem] * (3 + len(others) + len(blocks)),
        out_specs=[in_vmem] * 3,
        out_shape=[
            jax.ShapeDtypeStruct((per_group, width), jnp.float32),
            jax.ShapeDtypeStruct((per_group, width), jnp.float32),
            jax.ShapeDtypeStruct((2, per_group), jnp.float32),
        ],
        compiler_params=params,
        name="rest_part",
    )(partly, projected, beside, *others, *blocks)


def finish_kernel(features, count, own_ref, other_ref, *refs):
    squares_refs, (out_ref, scaled, sems) = refs[:count], refs[count:]
    per_group, columns = out_ref.shape
    width = own_ref.shape[1]
    core, start = place_of(columns, width)
    squares = squares_refs[0][...]
    for ref in squares_refs[1:]:
        squares += ref[...]
    row = jnp.where(core == 0, squares[0:1], squares[1:2])
    spread = jnp.broadcast_to(scale_of(row, features), (per_group, per_group))
    scale = jnp.sum(jnp.where(diagonal(per_group), spread, 0.0), axis=1, keepdims=True)
    copies = []
    apart = 2 * width == columns
    for ref, first in ((other_ref, columns - width - start), (own_ref, start)):
        for here in tiles_of(width, 7):
            there = pl.ds(pl.multiple_of(first + here.start, lanes), here.size)
            scaled[:, there] = ref[:, here] * scale
            if apart:
                copies.append(pltpu.make_async_copy(scaled.at[:, there], out_ref.at[:, there], sems.at[len(copies)]))
                copies[-1].start()
    if not apart:
        copies.append(pltpu.make_async_copy(scaled, out_ref, sems.at[0]))
        copies[-1].start()
    for copy in copies:
        copy.wait()


def finish(own, other, squares, columns, features):
    per_group, width = own.shape
    return pl.pallas_call(
        functools.partial(finish_kernel, features, len(squares)),
        in_specs=[in_vmem] * (2 + len(squares)),
        out_specs=anywhere,
        out_shape=jax.ShapeDtypeStruct((per_group, columns), jnp.float32),
        scratch_shapes=[
            pltpu.VMEM((per_group, columns), jnp.float32),
            pltpu.SemaphoreType.DMA((2 * len(tiles_of(width, 7)),)),
        ],
        compiler_params=params,
        name="finish",
    )(own, other, *squares)


def exchange(array, axis, step):
    return lax.ppermute(array, axis, [(i, i ^ step) for i in range(lax.axis_size(axis))])


def terms(array, together, flip):
    comp, feat = lax.axis_size("comp"), lax.axis_size("feat")
    parts, step = [array], 1
    while step < feat:
        array = sum(parts[1:], parts[0])
        width = min(1 << together, feat // step)
        parts = [array]
        for k in range(1, width):
            pairs = [(i * feat + j, (i ^ flip) * feat + (j ^ (k * step))) for i in range(comp) for j in range(feat)]
            parts.append(lax.ppermute(array, ("comp", "feat"), pairs))
        step *= width
    return parts


def by_columns(samples, start_vectors):
    comp, feat = lax.axis_size("comp"), lax.axis_size("feat")
    sample = samples[0]
    rows, columns = sample.shape
    features = columns * feat
    width = -(-columns // (2 * lanes)) * lanes
    core = lax.axis_index("comp") % 2
    steps = list(range(2, comp, 2))

    mine = lax.dynamic_slice_in_dim(start_vectors, core * (columns - width), width, 1)
    theirs = lax.dynamic_slice_in_dim(start_vectors, (1 - core) * (columns - width), width, 1)
    near = exchange(theirs, "comp", 1)
    far = {step: [exchange(mine, "comp", step)] for step in steps}
    projected, sample = project(
        *(pltpu.with_memory_space_constraint(array, pltpu.HBM) for array in (start_vectors, sample))
    )
    near, projected = lax.optimization_barrier((near, projected))
    for step in steps:
        far[step].append(exchange(near, "comp", step))
    parts = terms(projected, 1, 0)
    projected = sum(parts[1:], parts[0])
    beside = exchange(projected, "comp", 1)
    others = []
    for step in steps:
        cross = exchange(projected, "comp", step + 1)
        others += [exchange(cross, "comp", 1), cross]
    partly = chip_part(projected, beside, sample, mine, near, features)
    blocks = [array for step in steps for array in far[step]]
    own, other, squares = rest_part(partly, projected, beside, steps, others, blocks, rows, columns, features)
    other = exchange(other, "comp", 1)
    squares = terms(squares + exchange(squares, "comp", 1), 2, 1)
    return finish(own, other, squares, columns, features)


def plainly(samples, start_vectors):
    per_group = start_vectors.shape[0]
    sample = samples[0]
    rows = sample.shape[0]
    features = sample.shape[1] * lax.axis_size("feat")
    root_width = math.sqrt(features)
    total = per_group * lax.axis_size("comp")
    own_columns = lax.axis_index("comp") * per_group + jnp.arange(per_group, dtype=jnp.int32)
    earlier = jnp.arange(total, dtype=jnp.int32)[:, None] < own_columns[None, :]
    einsum = functools.partial(jnp.einsum, precision=lax.Precision.HIGHEST)

    def normalize(updated):
        summed = lax.psum(jnp.sum(updated * updated, axis=1), "feat")
        return updated * scale_of(summed, features)[:, None]

    vectors = normalize(start_vectors)
    images = lax.psum(einsum("rd,kd->rk", sample, vectors) / root_width, "feat")
    every = lax.all_gather(images, "comp", axis=1, tiled=True)
    coupling = jnp.where(earlier, einsum("rj,ri->ji", every, images) / rows, 0.0)
    penalty = einsum("ji,jd->id", coupling, lax.all_gather(vectors, "comp", axis=0, tiled=True))
    gradient = root_width * einsum("rk,rd->kd", images, sample) / rows - penalty
    return normalize(vectors + step_rate * gradient)


def shards(samples, start_vectors):
    sizes = lax.axis_size("comp"), lax.axis_size("feat")
    in_pairs = sizes[0] > 1 and all(size & (size - 1) == 0 for size in sizes)
    whole_tiles = start_vectors.shape[1] % lanes == 0 and start_vectors.shape[0] % 16 == 0 and samples.shape[1] % 16 == 0
    return (by_columns if in_pairs and whole_tiles else plainly)(samples, start_vectors)


def solution(mesh):
    in_specs = (P(None, None, "feat"), P("comp", "feat"))
    out_specs = P("comp", "feat")
    return jax.shard_map(shards, mesh=mesh, in_specs=in_specs, out_specs=out_specs, check_vma=False)
```

```python
import functools

import jax
import jax.numpy as jnp
from jax import lax
from jax.experimental import pallas as pl
from jax.experimental.pallas import tpu as pltpu
from jax.sharding import PartitionSpec as P

step_rate = 0.1
epsilon = 1e-06
lanes = 128
in_vmem = pl.BlockSpec(memory_space=pltpu.VMEM)
anywhere = pl.BlockSpec(memory_space=pl.ANY)
params = pltpu.CompilerParams(vmem_limit_bytes=16 << 20)


def tile_of(columns, most):
    if columns % lanes:
        return columns
    units = columns // lanes
    return lanes * max(u for u in range(1, most + 1) if units % u == 0)


def halves(array):
    top = array.astype(jnp.bfloat16)
    return top, (array - top.astype(jnp.float32)).astype(jnp.bfloat16)


def product(left, right, transposed=False):
    dims = (((1,), (1 if transposed else 0,)), ((), ()))
    dot = functools.partial(lax.dot_general, dimension_numbers=dims, preferred_element_type=jnp.float32)
    left_top, left_rest = left if isinstance(left, tuple) else halves(left)
    right_top, right_rest = halves(right)
    rows = left_top.shape[0]
    both = dot(jnp.concatenate([left_top, left_rest], axis=0), right_top)
    return both[:rows] + (both[rows:] + dot(left_top, right_rest))


def scale_of(squares, features):
    return lax.rsqrt(squares / features + epsilon)


def loop(columns, most, body, init):
    tile = tile_of(columns, most)
    return lax.fori_loop(0, columns // tile, lambda i, c: body(i, pl.ds(pl.multiple_of(i * tile, tile), tile), c), init, unroll=True)


def project_kernel(x_hbm, s_hbm, out_ref, x_ref, s_ref, sems):
    per_group, columns = x_ref.shape
    rows = s_ref.shape[0]

    def copies(i, here):
        return (
            pltpu.make_async_copy(x_hbm.at[:, here], x_ref.at[:, here], sems.at[0, i]),
            pltpu.make_async_copy(s_hbm.at[:, here], s_ref.at[:, here], sems.at[1, i]),
        )

    def begin(i, here, carry):
        for copy in copies(i, here):
            copy.start()
        return carry

    def body(i, here, carry):
        for copy in copies(i, here):
            copy.wait()
        x = x_ref[:, here]
        projected, squares = carry
        projected += product(x, s_ref[:, here], transposed=True)
        return projected, squares + jnp.sum(x * x, axis=1, keepdims=True)

    loop(columns, 4, begin, 0)
    zeros = jnp.zeros((per_group, rows), jnp.float32), jnp.zeros((per_group, 1), jnp.float32)
    projected, squares = loop(columns, 4, body, zeros)
    out_ref[:, :rows] = projected
    out_ref[:, rows:] = jnp.broadcast_to(squares, (per_group, out_ref.shape[1] - rows))


def project(x, sample):
    per_group, columns = x.shape
    rows = sample.shape[0]
    width = -(-(rows + 1) // lanes) * lanes
    return pl.pallas_call(
        project_kernel,
        in_specs=[anywhere] * 2,
        out_specs=[in_vmem] * 3,
        out_shape=[
            jax.ShapeDtypeStruct((per_group, width), jnp.float32),
            jax.ShapeDtypeStruct(x.shape, jnp.float32),
            jax.ShapeDtypeStruct(sample.shape, jnp.float32),
        ],
        scratch_shapes=[pltpu.SemaphoreType.DMA((2, columns // tile_of(columns, 4)))],
        compiler_params=params,
        name="project",
    )(x, sample)


def images_of(p_ref, rows, features):
    scale = scale_of(p_ref[:, rows : rows + 1], features)
    return p_ref[:, :rows] * scale, scale


def owner(group, step, size):
    return (group + step) % size if size & (size - 1) else group ^ step


def couplings(images, steps, projected_refs, features):
    group, size = lax.axis_index("comp"), lax.axis_size("comp")
    rows = images.shape[1]
    others = []
    for step, p_ref in zip(steps, projected_refs):
        other, scale = images_of(p_ref, rows, features)
        others.append(other * (scale * jnp.where(owner(group, step, size) < group, -step_rate / (features * rows), 0.0)))
    return product(images, jnp.concatenate(others, axis=0), transposed=True)


def first_kernel(features, steps, p_ref, s_ref, x_ref, *refs):
    count = len(steps)
    projected_refs, x_refs, out_ref = refs[:count], refs[count : 2 * count], refs[2 * count]
    rows = s_ref.shape[0]
    images, scale = images_of(p_ref, rows, features)
    shared = product(images, images * scale, transposed=True)
    later = lax.broadcasted_iota(jnp.int32, shared.shape, 0)
    earlier = lax.broadcasted_iota(jnp.int32, shared.shape, 1)
    weights = [images * (step_rate / rows), jnp.where(earlier < later, shared * (-step_rate / (features * rows)), 0.0)]
    if count:
        weights.append(couplings(images, steps, projected_refs, features))
    weights = halves(jnp.concatenate(weights, axis=1))

    def body(i, here, carry):
        x = x_ref[:, here]
        others = [ref[:, here] for ref in x_refs]
        out_ref[:, here] = scale * x + product(weights, jnp.concatenate([s_ref[:, here], x, *others], axis=0))
        return carry

    loop(x_ref.shape[1], 4, body, 0)


def first_part(projected, sample, x, steps, others, blocks, features):
    return pl.pallas_call(
        functools.partial(first_kernel, features, steps),
        in_specs=[in_vmem] * (3 + 2 * len(steps)),
        out_specs=in_vmem,
        out_shape=jax.ShapeDtypeStruct(x.shape, jnp.float32),
        compiler_params=params,
        name="first_part",
    )(projected, sample, x, *others, *blocks)


def couple_kernel(features, rows, steps, p_ref, *refs):
    projected_refs, (top_ref, rest_ref) = refs[:-2], refs[-2:]
    top_ref[...], rest_ref[...] = halves(couplings(images_of(p_ref, rows, features)[0], steps, projected_refs, features))


def couple(projected, steps, others, rows, features):
    per_group = projected.shape[0]
    return pl.pallas_call(
        functools.partial(couple_kernel, features, rows, steps),
        in_specs=[in_vmem] * (1 + len(steps)),
        out_specs=[in_vmem] * 2,
        out_shape=[jax.ShapeDtypeStruct((per_group, per_group * len(steps)), jnp.bfloat16)] * 2,
        compiler_params=params,
        cost_estimate=pl.CostEstimate(flops=8900000000, bytes_accessed=4 * projected.size, transcendentals=0),
        name="couple",
    )(projected, *others)


def rest_kernel(count, t_ref, *refs):
    x_refs, (out_ref, squares_ref) = refs[-2 - count : -2], refs[-2:]
    per_group, columns = t_ref.shape
    if count:
        weights = refs[0][...], refs[1][...]

    def body(i, here, squares):
        updated = t_ref[:, here]
        if count:
            updated += product(weights, jnp.concatenate([ref[:, here] for ref in x_refs], axis=0))
        out_ref[:, here] = updated
        return squares + jnp.sum(updated * updated, axis=1, keepdims=True)

    squares = loop(columns, 4, body, jnp.zeros((per_group, 1), jnp.float32))
    spread = jnp.broadcast_to(squares, (per_group, per_group))
    squares_ref[...] = jnp.sum(jnp.where(diagonal(per_group), spread, 0.0), axis=0, keepdims=True)


def rest_part(partly, weights, blocks):
    return pl.pallas_call(
        functools.partial(rest_kernel, len(blocks)),
        in_specs=[in_vmem] * (1 + len(weights) + len(blocks)),
        out_specs=[in_vmem, in_vmem],
        out_shape=[
            jax.ShapeDtypeStruct(partly.shape, jnp.float32),
            jax.ShapeDtypeStruct((1, partly.shape[0]), jnp.float32),
        ],
        compiler_params=params,
        name="rest_part",
    )(partly, *weights, *blocks)


def diagonal(count):
    down = lax.broadcasted_iota(jnp.int32, (count, count), 0)
    across = lax.broadcasted_iota(jnp.int32, (count, count), 1)
    return down == across


def finish_kernel(features, count, updated_ref, *refs):
    squares_refs, (out_ref, scaled, sems) = refs[:count], refs[count:]
    per_group, columns = updated_ref.shape
    squares = squares_refs[0][...]
    for ref in squares_refs[1:]:
        squares += ref[...]
    spread = jnp.broadcast_to(scale_of(squares, features), (per_group, per_group))
    scale = jnp.sum(jnp.where(diagonal(per_group), spread, 0.0), axis=1, keepdims=True)
    tile = tile_of(columns, 7)
    copies = []
    for i in range(columns // tile):
        here = pl.ds(i * tile, tile)
        scaled[:, here] = updated_ref[:, here] * scale
        copies.append(pltpu.make_async_copy(scaled.at[:, here], out_ref.at[:, here], sems.at[i]))
        copies[-1].start()
    for copy in copies:
        copy.wait()


def finish(updated, squares, features):
    count = len(squares)
    return pl.pallas_call(
        functools.partial(finish_kernel, features, count),
        in_specs=[in_vmem] * (1 + count),
        out_specs=anywhere,
        out_shape=jax.ShapeDtypeStruct(updated.shape, jnp.float32),
        scratch_shapes=[
            pltpu.VMEM(updated.shape, jnp.float32),
            pltpu.SemaphoreType.DMA((updated.shape[1] // tile_of(updated.shape[1], 7),)),
        ],
        compiler_params=params,
        name="finish",
    )(updated, *squares)


def exchange(array, axis, step):
    return lax.ppermute(array, axis, [(i, i ^ step) for i in range(lax.axis_size(axis))])


def terms(array, axis, together):
    size = lax.axis_size(axis)
    if size & (size - 1):
        return [lax.psum(array, axis)]
    parts, step = [array], 1
    while step < size:
        array = sum(parts[1:], parts[0])
        width = min(1 << together, size // step)
        parts = [array] + [exchange(array, axis, step * k) for k in range(1, width)]
        step *= width
    return parts


def flipped_terms(array):
    comp, feat = lax.axis_size("comp"), lax.axis_size("feat")
    if comp % 2 or comp & (comp - 1) or feat & (feat - 1):
        return terms(array, "feat", 2)
    widths, step = [], 1
    while step < feat:
        widths.append(min(4, feat // step))
        step *= widths[-1]
    parts, step = [array], 1
    for stage, width in enumerate(widths):
        array = sum(parts[1:], parts[0])
        flip = int(stage + 1 < len(widths) or len(widths) % 2 == 0)
        parts = [] if flip else [array]
        for k in range(0 if flip else 1, width):
            pairs = [
                (i * feat + j, (i ^ flip) * feat + (j ^ (k * step))) for i in range(comp) for j in range(feat)
            ]
            parts.append(lax.ppermute(array, ("comp", "feat"), pairs))
        step *= width
    return parts


def gather(own):
    size = lax.axis_size("comp")
    if size & (size - 1):
        arrays, group = lax.all_gather(own, "comp"), lax.axis_index("comp")
        return {step: arrays[owner(group, step, size)] for step in range(1, size)}
    return {step: exchange(own, "comp", step) for step in range(1, size)}


def shards(samples, start_vectors):
    comp = lax.axis_size("comp")
    feat = lax.axis_size("feat")
    sample = samples[0]
    rows = sample.shape[0]
    features = sample.shape[1] * feat
    even = comp & (comp - 1) == 0

    blocks = {step: exchange(start_vectors, "comp", step) for step in range(2, comp, 2)} if even else gather(start_vectors)
    projected, vectors, sample = project(
        *(pltpu.with_memory_space_constraint(array, pltpu.HBM) for array in (start_vectors, sample))
    )
    if even and comp > 1:
        blocks[1] = exchange(start_vectors, "comp", 1)
    parts = terms(projected, "feat", 1)
    projected = sum(parts[1:], parts[0])
    if even:
        others = {step: exchange(projected, "comp", step) for step in range(1, comp) if step == 1 or step % 2 == 0}
    else:
        others = gather(projected)
    near = [1][: comp - 1]
    far = list(range(2, comp))

    def of(arrays, steps):
        return [arrays[step] for step in steps]

    partly = first_part(projected, sample, vectors, near, of(others, near), of(blocks, near), features)
    if even:
        for step in range(2, comp, 2):
            blocks[step], partly = lax.optimization_barrier((blocks[step], partly))
            blocks[step + 1] = exchange(blocks[step], "comp", 1)
            others[step + 1] = exchange(others[step], "comp", 1)
    weights = couple(projected, far, of(others, far), rows, features) if far else []
    updated, squares = rest_part(partly, weights, of(blocks, far))
    return finish(updated, flipped_terms(squares), features)


def solution(mesh):
    in_specs = (P(None, None, "feat"), P("comp", "feat"))
    out_specs = P("comp", "feat")
    return jax.shard_map(shards, mesh=mesh, in_specs=in_specs, out_specs=out_specs, check_vma=False)
```

```python
import functools

import jax
import jax.numpy as jnp
from jax import lax
from jax.experimental import pallas as pl
from jax.experimental.pallas import tpu as pltpu
from jax.sharding import PartitionSpec as P

step_rate = 0.1
epsilon = 1e-06
lanes = 128
in_vmem = pl.BlockSpec(memory_space=pltpu.VMEM)
anywhere = pl.BlockSpec(memory_space=pl.ANY)
params = pltpu.CompilerParams(vmem_limit_bytes=16 << 20)


def tile_of(columns, most):
    if columns % lanes:
        return columns
    units = columns // lanes
    return lanes * max(u for u in range(1, most + 1) if units % u == 0)


def halves(array):
    top = array.astype(jnp.bfloat16)
    return top, (array - top.astype(jnp.float32)).astype(jnp.bfloat16)


def product(left, right, transposed=False):
    dims = (((1,), (1 if transposed else 0,)), ((), ()))
    dot = functools.partial(lax.dot_general, dimension_numbers=dims, preferred_element_type=jnp.float32)
    left_top, left_rest = left if isinstance(left, tuple) else halves(left)
    right_top, right_rest = halves(right)
    rows = left_top.shape[0]
    both = dot(jnp.concatenate([left_top, left_rest], axis=0), right_top)
    return both[:rows] + (both[rows:] + dot(left_top, right_rest))


def scale_of(squares, features):
    return lax.rsqrt(squares / features + epsilon)


def loop(columns, most, body, init):
    tile = tile_of(columns, most)
    return lax.fori_loop(0, columns // tile, lambda i, c: body(i, pl.ds(pl.multiple_of(i * tile, tile), tile), c), init, unroll=True)


def project_kernel(x_hbm, s_hbm, out_ref, x_ref, s_ref, sems):
    per_group, columns = x_ref.shape
    rows = s_ref.shape[0]

    def copies(i, here):
        return (
            pltpu.make_async_copy(x_hbm.at[:, here], x_ref.at[:, here], sems.at[0, i]),
            pltpu.make_async_copy(s_hbm.at[:, here], s_ref.at[:, here], sems.at[1, i]),
        )

    def begin(i, here, carry):
        for copy in copies(i, here):
            copy.start()
        return carry

    def body(i, here, carry):
        for copy in copies(i, here):
            copy.wait()
        x = x_ref[:, here]
        projected, squares = carry
        projected += product(x, s_ref[:, here], transposed=True)
        return projected, squares + jnp.sum(x * x, axis=1, keepdims=True)

    loop(columns, 4, begin, 0)
    zeros = jnp.zeros((per_group, rows), jnp.float32), jnp.zeros((per_group, 1), jnp.float32)
    projected, squares = loop(columns, 4, body, zeros)
    out_ref[:, :rows] = projected
    out_ref[:, rows:] = jnp.broadcast_to(squares, (per_group, out_ref.shape[1] - rows))


def project(x, sample):
    per_group, columns = x.shape
    rows = sample.shape[0]
    width = -(-(rows + 1) // lanes) * lanes
    return pl.pallas_call(
        project_kernel,
        in_specs=[anywhere] * 2,
        out_specs=[in_vmem] * 3,
        out_shape=[
            jax.ShapeDtypeStruct((per_group, width), jnp.float32),
            jax.ShapeDtypeStruct(x.shape, jnp.float32),
            jax.ShapeDtypeStruct(sample.shape, jnp.float32),
        ],
        scratch_shapes=[pltpu.SemaphoreType.DMA((2, columns // tile_of(columns, 4)))],
        compiler_params=params,
        name="project",
    )(x, sample)


def images_of(p_ref, rows, features):
    scale = scale_of(p_ref[:, rows : rows + 1], features)
    return p_ref[:, :rows] * scale, scale


def owner(group, step, size):
    return (group + step) % size if size & (size - 1) else group ^ step


def couplings(images, steps, projected_refs, features):
    group, size = lax.axis_index("comp"), lax.axis_size("comp")
    rows = images.shape[1]
    others = []
    for step, p_ref in zip(steps, projected_refs):
        other, scale = images_of(p_ref, rows, features)
        others.append(other * (scale * jnp.where(owner(group, step, size) < group, -step_rate / (features * rows), 0.0)))
    return product(images, jnp.concatenate(others, axis=0), transposed=True)


def first_kernel(features, steps, p_ref, s_ref, x_ref, *refs):
    count = len(steps)
    projected_refs, x_refs, out_ref = refs[:count], refs[count : 2 * count], refs[2 * count]
    rows = s_ref.shape[0]
    images, scale = images_of(p_ref, rows, features)
    shared = product(images, images * scale, transposed=True)
    later = lax.broadcasted_iota(jnp.int32, shared.shape, 0)
    earlier = lax.broadcasted_iota(jnp.int32, shared.shape, 1)
    weights = [images * (step_rate / rows), jnp.where(earlier < later, shared * (-step_rate / (features * rows)), 0.0)]
    if count:
        weights.append(couplings(images, steps, projected_refs, features))
    weights = halves(jnp.concatenate(weights, axis=1))

    def body(i, here, carry):
        x = x_ref[:, here]
        others = [ref[:, here] for ref in x_refs]
        out_ref[:, here] = scale * x + product(weights, jnp.concatenate([s_ref[:, here], x, *others], axis=0))
        return carry

    loop(x_ref.shape[1], 4, body, 0)


def first_part(projected, sample, x, steps, others, blocks, features):
    return pl.pallas_call(
        functools.partial(first_kernel, features, steps),
        in_specs=[in_vmem] * (3 + 2 * len(steps)),
        out_specs=in_vmem,
        out_shape=jax.ShapeDtypeStruct(x.shape, jnp.float32),
        compiler_params=params,
        name="first_part",
    )(projected, sample, x, *others, *blocks)


def rest_kernel(features, rows, steps, t_ref, p_ref, *refs):
    count = len(steps)
    projected_refs, x_refs, (out_ref, squares_ref) = refs[:count], refs[count : 2 * count], refs[2 * count :]
    per_group, columns = t_ref.shape
    if count:
        weights = halves(couplings(images_of(p_ref, rows, features)[0], steps, projected_refs, features))

    def body(i, here, squares):
        updated = t_ref[:, here]
        if count:
            updated += product(weights, jnp.concatenate([ref[:, here] for ref in x_refs], axis=0))
        out_ref[:, here] = updated
        return squares + jnp.sum(updated * updated, axis=1, keepdims=True)

    squares = loop(columns, 4, body, jnp.zeros((per_group, 1), jnp.float32))
    spread = jnp.broadcast_to(squares, (per_group, per_group))
    squares_ref[...] = jnp.sum(jnp.where(diagonal(per_group), spread, 0.0), axis=0, keepdims=True)


def rest_part(partly, projected, steps, others, blocks, rows, features):
    return pl.pallas_call(
        functools.partial(rest_kernel, features, rows, steps),
        in_specs=[in_vmem] * (2 + 2 * len(steps)),
        out_specs=[in_vmem, in_vmem],
        out_shape=[
            jax.ShapeDtypeStruct(partly.shape, jnp.float32),
            jax.ShapeDtypeStruct((1, partly.shape[0]), jnp.float32),
        ],
        compiler_params=params,
        name="rest_part",
    )(partly, projected, *others, *blocks)


def diagonal(count):
    down = lax.broadcasted_iota(jnp.int32, (count, count), 0)
    across = lax.broadcasted_iota(jnp.int32, (count, count), 1)
    return down == across


def finish_kernel(features, count, updated_ref, *refs):
    squares_refs, (out_ref, scaled, sems) = refs[:count], refs[count:]
    per_group, columns = updated_ref.shape
    squares = squares_refs[0][...]
    for ref in squares_refs[1:]:
        squares += ref[...]
    spread = jnp.broadcast_to(scale_of(squares, features), (per_group, per_group))
    scale = jnp.sum(jnp.where(diagonal(per_group), spread, 0.0), axis=1, keepdims=True)
    tile = tile_of(columns, 7)
    copies = []
    for i in range(columns // tile):
        here = pl.ds(i * tile, tile)
        scaled[:, here] = updated_ref[:, here] * scale
        copies.append(pltpu.make_async_copy(scaled.at[:, here], out_ref.at[:, here], sems.at[i]))
        copies[-1].start()
    for copy in copies:
        copy.wait()


def finish(updated, squares, features):
    count = len(squares)
    return pl.pallas_call(
        functools.partial(finish_kernel, features, count),
        in_specs=[in_vmem] * (1 + count),
        out_specs=anywhere,
        out_shape=jax.ShapeDtypeStruct(updated.shape, jnp.float32),
        scratch_shapes=[
            pltpu.VMEM(updated.shape, jnp.float32),
            pltpu.SemaphoreType.DMA((updated.shape[1] // tile_of(updated.shape[1], 7),)),
        ],
        compiler_params=params,
        name="finish",
    )(updated, *squares)


def exchange(array, axis, step):
    return lax.ppermute(array, axis, [(i, i ^ step) for i in range(lax.axis_size(axis))])


def terms(array, axis, together):
    size = lax.axis_size(axis)
    if size & (size - 1):
        return [lax.psum(array, axis)]
    parts, step = [array], 1
    while step < size:
        array = sum(parts[1:], parts[0])
        width = min(1 << together, size // step)
        parts = [array] + [exchange(array, axis, step * k) for k in range(1, width)]
        step *= width
    return parts


def flipped_terms(array):
    comp, feat = lax.axis_size("comp"), lax.axis_size("feat")
    if comp % 2 or comp & (comp - 1) or feat & (feat - 1):
        return terms(array, "feat", 2)
    widths, step = [], 1
    while step < feat:
        widths.append(min(4, feat // step))
        step *= widths[-1]
    parts, step = [array], 1
    for stage, width in enumerate(widths):
        array = sum(parts[1:], parts[0])
        flip = int(stage + 1 < len(widths) or len(widths) % 2 == 0)
        parts = [] if flip else [array]
        for k in range(0 if flip else 1, width):
            pairs = [
                (i * feat + j, (i ^ flip) * feat + (j ^ (k * step))) for i in range(comp) for j in range(feat)
            ]
            parts.append(lax.ppermute(array, ("comp", "feat"), pairs))
        step *= width
    return parts


def gather(own):
    size = lax.axis_size("comp")
    if size & (size - 1):
        arrays, group = lax.all_gather(own, "comp"), lax.axis_index("comp")
        return {step: arrays[owner(group, step, size)] for step in range(1, size)}
    return {step: exchange(own, "comp", step) for step in range(1, size)}


def shards(samples, start_vectors):
    comp = lax.axis_size("comp")
    feat = lax.axis_size("feat")
    sample = samples[0]
    rows = sample.shape[0]
    features = sample.shape[1] * feat
    even = comp & (comp - 1) == 0

    blocks = {step: exchange(start_vectors, "comp", step) for step in range(3, comp, 2)} if even else gather(start_vectors)
    projected, vectors, sample = project(
        *(pltpu.with_memory_space_constraint(array, pltpu.HBM) for array in (start_vectors, sample))
    )
    if even and comp > 1:
        blocks[1] = exchange(vectors, "comp", 1)
    parts = terms(projected, "feat", 1)
    projected = sum(parts[1:], parts[0])
    if even:
        others = {step: exchange(projected, "comp", step) for step in range(1, comp) if step == 1 or step % 2 == 0}
    else:
        others = gather(projected)
    near = [1][: comp - 1]
    far = list(range(2, comp))

    def of(arrays, steps):
        return [arrays[step] for step in steps]

    partly = first_part(projected, sample, vectors, near, of(others, near), of(blocks, near), features)
    if even:
        for step in range(2, comp, 2):
            blocks[step + 1], others[step], others[1] = lax.optimization_barrier(
                (blocks[step + 1], others[step], others[1])
            )
            blocks[step] = exchange(blocks[step + 1], "comp", 1)
            others[step + 1] = exchange(others[step], "comp", 1)
    updated, squares = rest_part(partly, projected, far, of(others, far), of(blocks, far), rows, features)
    return finish(updated, flipped_terms(squares), features)


def solution(mesh):
    in_specs = (P(None, None, "feat"), P("comp", "feat"))
    out_specs = P("comp", "feat")
    return jax.shard_map(shards, mesh=mesh, in_specs=in_specs, out_specs=out_specs, check_vma=False)
```

```python
import functools

import jax
import jax.numpy as jnp
from jax import lax
from jax.experimental import pallas as pl
from jax.experimental.pallas import tpu as pltpu
from jax.sharding import PartitionSpec as P

step_rate = 0.1
epsilon = 1e-06
lanes = 128
in_vmem = pl.BlockSpec(memory_space=pltpu.VMEM)
anywhere = pl.BlockSpec(memory_space=pl.ANY)
params = pltpu.CompilerParams(vmem_limit_bytes=16 << 20)


def tile_of(columns, most):
    if columns % lanes:
        return columns
    units = columns // lanes
    return lanes * max(u for u in range(1, most + 1) if units % u == 0)


def halves(array):
    top = array.astype(jnp.bfloat16)
    return top, (array - top.astype(jnp.float32)).astype(jnp.bfloat16)


def product(left, right, transposed=False):
    dims = (((1,), (1 if transposed else 0,)), ((), ()))
    dot = functools.partial(lax.dot_general, dimension_numbers=dims, preferred_element_type=jnp.float32)
    left_top, left_rest = left if isinstance(left, tuple) else halves(left)
    right_top, right_rest = halves(right)
    rows = left_top.shape[0]
    both = dot(jnp.concatenate([left_top, left_rest], axis=0), right_top)
    return both[:rows] + (both[rows:] + dot(left_top, right_rest))


def scale_of(squares, features):
    return lax.rsqrt(squares / features + epsilon)


def loop(columns, most, body, init):
    tile = tile_of(columns, most)
    return lax.fori_loop(0, columns // tile, lambda i, c: body(i, pl.ds(pl.multiple_of(i * tile, tile), tile), c), init, unroll=True)


def project_kernel(x_hbm, s_hbm, out_ref, x_ref, s_ref, sems):
    per_group, columns = x_ref.shape
    rows = s_ref.shape[0]

    def copies(i, here):
        return (
            pltpu.make_async_copy(x_hbm.at[:, here], x_ref.at[:, here], sems.at[0, i]),
            pltpu.make_async_copy(s_hbm.at[:, here], s_ref.at[:, here], sems.at[1, i]),
        )

    def begin(i, here, carry):
        for copy in copies(i, here):
            copy.start()
        return carry

    def body(i, here, carry):
        for copy in copies(i, here):
            copy.wait()
        x = x_ref[:, here]
        projected, squares = carry
        projected += product(x, s_ref[:, here], transposed=True)
        return projected, squares + jnp.sum(x * x, axis=1, keepdims=True)

    loop(columns, 4, begin, 0)
    zeros = jnp.zeros((per_group, rows), jnp.float32), jnp.zeros((per_group, 1), jnp.float32)
    projected, squares = loop(columns, 4, body, zeros)
    out_ref[:, :rows] = projected
    out_ref[:, rows:] = jnp.broadcast_to(squares, (per_group, out_ref.shape[1] - rows))


def project(x, sample):
    per_group, columns = x.shape
    rows = sample.shape[0]
    width = -(-(rows + 1) // lanes) * lanes
    return pl.pallas_call(
        project_kernel,
        in_specs=[anywhere] * 2,
        out_specs=[in_vmem] * 3,
        out_shape=[
            jax.ShapeDtypeStruct((per_group, width), jnp.float32),
            jax.ShapeDtypeStruct(x.shape, jnp.float32),
            jax.ShapeDtypeStruct(sample.shape, jnp.float32),
        ],
        scratch_shapes=[pltpu.SemaphoreType.DMA((2, columns // tile_of(columns, 4)))],
        compiler_params=params,
        name="project",
    )(x, sample)


def images_of(p_ref, rows, features):
    scale = scale_of(p_ref[:, rows : rows + 1], features)
    return p_ref[:, :rows] * scale, scale


def owner(group, step, size):
    return (group + step) % size if size & (size - 1) else group ^ step


def couplings(images, steps, projected_refs, features):
    group, size = lax.axis_index("comp"), lax.axis_size("comp")
    rows = images.shape[1]
    others = []
    for step, p_ref in zip(steps, projected_refs):
        other, scale = images_of(p_ref, rows, features)
        others.append(other * (scale * jnp.where(owner(group, step, size) < group, -step_rate / (features * rows), 0.0)))
    return product(images, jnp.concatenate(others, axis=0), transposed=True)


def first_kernel(features, steps, p_ref, s_ref, x_ref, *refs):
    count = len(steps)
    projected_refs, x_refs, out_ref = refs[:count], refs[count : 2 * count], refs[2 * count]
    rows = s_ref.shape[0]
    images, scale = images_of(p_ref, rows, features)
    shared = product(images, images * scale, transposed=True)
    later = lax.broadcasted_iota(jnp.int32, shared.shape, 0)
    earlier = lax.broadcasted_iota(jnp.int32, shared.shape, 1)
    weights = [images * (step_rate / rows), jnp.where(earlier < later, shared * (-step_rate / (features * rows)), 0.0)]
    if count:
        weights.append(couplings(images, steps, projected_refs, features))
    weights = halves(jnp.concatenate(weights, axis=1))

    def body(i, here, carry):
        x = x_ref[:, here]
        others = [ref[:, here] for ref in x_refs]
        out_ref[:, here] = scale * x + product(weights, jnp.concatenate([s_ref[:, here], x, *others], axis=0))
        return carry

    loop(x_ref.shape[1], 4, body, 0)


def first_part(projected, sample, x, steps, others, blocks, features):
    return pl.pallas_call(
        functools.partial(first_kernel, features, steps),
        in_specs=[in_vmem] * (3 + 2 * len(steps)),
        out_specs=in_vmem,
        out_shape=jax.ShapeDtypeStruct(x.shape, jnp.float32),
        compiler_params=params,
        name="first_part",
    )(projected, sample, x, *others, *blocks)


def couple_kernel(features, rows, steps, p_ref, *refs):
    projected_refs, (top_ref, rest_ref) = refs[:-2], refs[-2:]
    top_ref[...], rest_ref[...] = halves(couplings(images_of(p_ref, rows, features)[0], steps, projected_refs, features))


def couple(projected, steps, others, rows, features):
    per_group = projected.shape[0]
    return pl.pallas_call(
        functools.partial(couple_kernel, features, rows, steps),
        in_specs=[in_vmem] * (1 + len(steps)),
        out_specs=[in_vmem] * 2,
        out_shape=[jax.ShapeDtypeStruct((per_group, per_group * len(steps)), jnp.bfloat16)] * 2,
        compiler_params=params,
        cost_estimate=pl.CostEstimate(flops=9000000000, bytes_accessed=4 * projected.size, transcendentals=0),
        name="couple",
    )(projected, *others)


def rest_kernel(count, t_ref, *refs):
    x_refs, (out_ref, squares_ref, wide_ref) = refs[-3 - count : -3], refs[-3:]
    per_group, columns = t_ref.shape
    if count:
        weights = refs[0][...], refs[1][...]

    def body(i, here, squares):
        updated = t_ref[:, here]
        if count:
            updated += product(weights, jnp.concatenate([ref[:, here] for ref in x_refs], axis=0))
        out_ref[:, here] = updated
        return squares + jnp.sum(updated * updated, axis=1, keepdims=True)

    squares = loop(columns, 4, body, jnp.zeros((per_group, 1), jnp.float32))
    spread = jnp.broadcast_to(squares, (per_group, per_group))
    row = jnp.sum(jnp.where(diagonal(per_group), spread, 0.0), axis=0, keepdims=True)
    squares_ref[...] = row
    wide_ref[...] = jnp.broadcast_to(row, wide_ref.shape)


def rest_part(partly, weights, blocks):
    return pl.pallas_call(
        functools.partial(rest_kernel, len(blocks)),
        in_specs=[in_vmem] * (1 + len(weights) + len(blocks)),
        out_specs=[in_vmem] * 3,
        out_shape=[
            jax.ShapeDtypeStruct(partly.shape, jnp.float32),
            jax.ShapeDtypeStruct((1, partly.shape[0]), jnp.float32),
            jax.ShapeDtypeStruct((8, partly.shape[0]), jnp.float32),
        ],
        compiler_params=params,
        name="rest_part",
    )(partly, *weights, *blocks)


def diagonal(count):
    down = lax.broadcasted_iota(jnp.int32, (count, count), 0)
    across = lax.broadcasted_iota(jnp.int32, (count, count), 1)
    return down == across


def finish_kernel(features, count, updated_ref, *refs):
    squares_refs, (out_ref, scaled, sems) = refs[:count], refs[count:]
    per_group, columns = updated_ref.shape
    squares = squares_refs[0][...]
    for ref in squares_refs[1:]:
        squares += ref[...]
    spread = jnp.broadcast_to(scale_of(squares, features), (per_group, per_group))
    scale = jnp.sum(jnp.where(diagonal(per_group), spread, 0.0), axis=1, keepdims=True)
    tile = tile_of(columns, 7)
    copies = []
    for i in range(columns // tile):
        here = pl.ds(i * tile, tile)
        scaled[:, here] = updated_ref[:, here] * scale
        copies.append(pltpu.make_async_copy(scaled.at[:, here], out_ref.at[:, here], sems.at[i]))
        copies[-1].start()
    for copy in copies:
        copy.wait()


def finish(updated, squares, features):
    count = len(squares)
    return pl.pallas_call(
        functools.partial(finish_kernel, features, count),
        in_specs=[in_vmem] * (1 + count),
        out_specs=anywhere,
        out_shape=jax.ShapeDtypeStruct(updated.shape, jnp.float32),
        scratch_shapes=[
            pltpu.VMEM(updated.shape, jnp.float32),
            pltpu.SemaphoreType.DMA((updated.shape[1] // tile_of(updated.shape[1], 7),)),
        ],
        compiler_params=params,
        name="finish",
    )(updated, *squares)


def exchange(array, axis, step):
    return lax.ppermute(array, axis, [(i, i ^ step) for i in range(lax.axis_size(axis))])


def terms(array, axis, together):
    size = lax.axis_size(axis)
    if size & (size - 1):
        return [lax.psum(array, axis)]
    parts, step = [array], 1
    while step < size:
        array = sum(parts[1:], parts[0])
        width = min(1 << together, size // step)
        parts = [array] + [exchange(array, axis, step * k) for k in range(1, width)]
        step *= width
    return parts


def flipped_terms(array, wide):
    comp, feat = lax.axis_size("comp"), lax.axis_size("feat")
    if comp % 2 or comp & (comp - 1) or feat & (feat - 1):
        return terms(array, "feat", 2)
    widths, step = [], 1
    while step < feat:
        widths.append(min(4, feat // step))
        step *= widths[-1]
    parts, step = [array], 1
    for stage, width in enumerate(widths):
        array = sum(parts[1:], parts[0])
        flip = int(stage + 1 < len(widths) or len(widths) % 2 == 0)
        parts = [] if flip else [array]
        for k in range(0 if flip else 1, width):
            pairs = [
                (i * feat + j, (i ^ flip) * feat + (j ^ (k * step))) for i in range(comp) for j in range(feat)
            ]
            farthest = stage == 0 and k == width - 1
            parts.append(lax.ppermute(wide if farthest else array, ("comp", "feat"), pairs)[:1])
        step *= width
    return parts


def gather(own):
    size = lax.axis_size("comp")
    if size & (size - 1):
        arrays, group = lax.all_gather(own, "comp"), lax.axis_index("comp")
        return {step: arrays[owner(group, step, size)] for step in range(1, size)}
    return {step: exchange(own, "comp", step) for step in range(1, size)}


def shards(samples, start_vectors):
    comp = lax.axis_size("comp")
    feat = lax.axis_size("feat")
    sample = samples[0]
    rows = sample.shape[0]
    features = sample.shape[1] * feat
    even = comp & (comp - 1) == 0

    blocks = {step: exchange(start_vectors, "comp", step) for step in range(2, comp, 2)} if even else gather(start_vectors)
    projected, vectors, sample = project(
        *(pltpu.with_memory_space_constraint(array, pltpu.HBM) for array in (start_vectors, sample))
    )
    if even and comp > 1:
        blocks[1] = exchange(vectors, "comp", 1)
    parts = terms(projected, "feat", 1)
    projected = sum(parts[1:], parts[0])
    if even:
        others = {step: exchange(projected, "comp", step) for step in range(1, comp, 2)}
    else:
        others = gather(projected)
    near = [1][: comp - 1]
    far = list(range(2, comp))

    def of(arrays, steps):
        return [arrays[step] for step in steps]

    partly = first_part(projected, sample, vectors, near, of(others, near), of(blocks, near), features)
    if even:
        for step in range(2, comp, 2):
            blocks[step], others[1] = lax.optimization_barrier((blocks[step], others[1]))
            blocks[step + 1] = exchange(blocks[step], "comp", 1)
            others[step] = exchange(others[step + 1], "comp", 1)
    projected, partly = lax.optimization_barrier((projected, partly))
    weights = couple(projected, far, of(others, far), rows, features) if far else []
    updated, squares, wide = rest_part(partly, weights, of(blocks, far))
    return finish(updated, flipped_terms(squares, wide), features)


def solution(mesh):
    in_specs = (P(None, None, "feat"), P("comp", "feat"))
    out_specs = P("comp", "feat")
    return jax.shard_map(shards, mesh=mesh, in_specs=in_specs, out_specs=out_specs, check_vma=False)
```

```python
import functools

import jax
import jax.numpy as jnp
from jax import lax
from jax.experimental import pallas as pl
from jax.experimental.pallas import tpu as pltpu
from jax.sharding import PartitionSpec as P

step_rate = 0.1
epsilon = 1e-06
lanes = 128
in_vmem = pl.BlockSpec(memory_space=pltpu.VMEM)
anywhere = pl.BlockSpec(memory_space=pl.ANY)
params = pltpu.CompilerParams(vmem_limit_bytes=16 << 20)


def tile_of(columns, most):
    if columns % lanes:
        return columns
    units = columns // lanes
    return lanes * max(u for u in range(1, most + 1) if units % u == 0)


def halves(array):
    top = array.astype(jnp.bfloat16)
    return top, (array - top.astype(jnp.float32)).astype(jnp.bfloat16)


def product(left, right, transposed=False):
    dims = (((1,), (1 if transposed else 0,)), ((), ()))
    dot = functools.partial(lax.dot_general, dimension_numbers=dims, preferred_element_type=jnp.float32)
    left_top, left_rest = left if isinstance(left, tuple) else halves(left)
    right_top, right_rest = halves(right)
    rows = left_top.shape[0]
    both = dot(jnp.concatenate([left_top, left_rest], axis=0), right_top)
    return both[:rows] + (both[rows:] + dot(left_top, right_rest))


def scale_of(squares, features):
    return lax.rsqrt(squares / features + epsilon)


def loop(columns, most, body, init):
    tile = tile_of(columns, most)
    return lax.fori_loop(0, columns // tile, lambda i, c: body(i, pl.ds(pl.multiple_of(i * tile, tile), tile), c), init, unroll=True)


def project_kernel(x_hbm, s_hbm, out_ref, x_ref, s_ref, sems):
    per_group, columns = x_ref.shape
    rows = s_ref.shape[0]

    def copies(i, here):
        return (
            pltpu.make_async_copy(x_hbm.at[:, here], x_ref.at[:, here], sems.at[0, i]),
            pltpu.make_async_copy(s_hbm.at[:, here], s_ref.at[:, here], sems.at[1, i]),
        )

    def begin(i, here, carry):
        for copy in copies(i, here):
            copy.start()
        return carry

    def body(i, here, carry):
        for copy in copies(i, here):
            copy.wait()
        x = x_ref[:, here]
        projected, squares = carry
        projected += product(x, s_ref[:, here], transposed=True)
        return projected, squares + jnp.sum(x * x, axis=1, keepdims=True)

    loop(columns, 4, begin, 0)
    zeros = jnp.zeros((per_group, rows), jnp.float32), jnp.zeros((per_group, 1), jnp.float32)
    projected, squares = loop(columns, 4, body, zeros)
    out_ref[:, :rows] = projected
    out_ref[:, rows:] = jnp.broadcast_to(squares, (per_group, out_ref.shape[1] - rows))


def project(x, sample):
    per_group, columns = x.shape
    rows = sample.shape[0]
    width = -(-(rows + 1) // lanes) * lanes
    return pl.pallas_call(
        project_kernel,
        in_specs=[anywhere] * 2,
        out_specs=[in_vmem] * 3,
        out_shape=[
            jax.ShapeDtypeStruct((per_group, width), jnp.float32),
            jax.ShapeDtypeStruct(x.shape, jnp.float32),
            jax.ShapeDtypeStruct(sample.shape, jnp.float32),
        ],
        scratch_shapes=[pltpu.SemaphoreType.DMA((2, columns // tile_of(columns, 4)))],
        compiler_params=params,
        name="project",
    )(x, sample)


def images_of(p_ref, rows, features):
    scale = scale_of(p_ref[:, rows : rows + 1], features)
    return p_ref[:, :rows] * scale, scale


def owner(group, step, size):
    return (group + step) % size if size & (size - 1) else group ^ step


def couplings(images, steps, projected_refs, features):
    group, size = lax.axis_index("comp"), lax.axis_size("comp")
    rows = images.shape[1]
    others = []
    for step, p_ref in zip(steps, projected_refs):
        other, scale = images_of(p_ref, rows, features)
        others.append(other * (scale * jnp.where(owner(group, step, size) < group, -step_rate / (features * rows), 0.0)))
    return product(images, jnp.concatenate(others, axis=0), transposed=True)


def first_kernel(features, steps, p_ref, s_ref, x_ref, *refs):
    count = len(steps)
    projected_refs, x_refs, out_ref = refs[:count], refs[count : 2 * count], refs[2 * count]
    rows = s_ref.shape[0]
    images, scale = images_of(p_ref, rows, features)
    shared = product(images, images * scale, transposed=True)
    later = lax.broadcasted_iota(jnp.int32, shared.shape, 0)
    earlier = lax.broadcasted_iota(jnp.int32, shared.shape, 1)
    weights = [images * (step_rate / rows), jnp.where(earlier < later, shared * (-step_rate / (features * rows)), 0.0)]
    if count:
        weights.append(couplings(images, steps, projected_refs, features))
    weights = halves(jnp.concatenate(weights, axis=1))

    def body(i, here, carry):
        x = x_ref[:, here]
        others = [ref[:, here] for ref in x_refs]
        out_ref[:, here] = scale * x + product(weights, jnp.concatenate([s_ref[:, here], x, *others], axis=0))
        return carry

    loop(x_ref.shape[1], 4, body, 0)


def first_part(projected, sample, x, steps, others, blocks, features):
    return pl.pallas_call(
        functools.partial(first_kernel, features, steps),
        in_specs=[in_vmem] * (3 + 2 * len(steps)),
        out_specs=in_vmem,
        out_shape=jax.ShapeDtypeStruct(x.shape, jnp.float32),
        compiler_params=params,
        name="first_part",
    )(projected, sample, x, *others, *blocks)


def couple_kernel(features, rows, steps, p_ref, *refs):
    projected_refs, (top_ref, rest_ref) = refs[:-2], refs[-2:]
    top_ref[...], rest_ref[...] = halves(couplings(images_of(p_ref, rows, features)[0], steps, projected_refs, features))


def couple(projected, steps, others, rows, features):
    per_group = projected.shape[0]
    return pl.pallas_call(
        functools.partial(couple_kernel, features, rows, steps),
        in_specs=[in_vmem] * (1 + len(steps)),
        out_specs=[in_vmem] * 2,
        out_shape=[jax.ShapeDtypeStruct((per_group, per_group * len(steps)), jnp.bfloat16)] * 2,
        compiler_params=params,
        cost_estimate=pl.CostEstimate(flops=9000000000, bytes_accessed=4 * projected.size, transcendentals=0),
        name="couple",
    )(projected, *others)


def rest_kernel(count, t_ref, *refs):
    x_refs, (out_ref, squares_ref, wide_ref) = refs[-3 - count : -3], refs[-3:]
    per_group, columns = t_ref.shape
    if count:
        weights = refs[0][...], refs[1][...]

    def body(i, here, squares):
        updated = t_ref[:, here]
        if count:
            updated += product(weights, jnp.concatenate([ref[:, here] for ref in x_refs], axis=0))
        out_ref[:, here] = updated
        return squares + jnp.sum(updated * updated, axis=1, keepdims=True)

    squares = loop(columns, 4, body, jnp.zeros((per_group, 1), jnp.float32))
    spread = jnp.broadcast_to(squares, (per_group, per_group))
    row = jnp.sum(jnp.where(diagonal(per_group), spread, 0.0), axis=0, keepdims=True)
    squares_ref[...] = row
    wide_ref[...] = jnp.broadcast_to(row, wide_ref.shape)


def rest_part(partly, weights, blocks):
    return pl.pallas_call(
        functools.partial(rest_kernel, len(blocks)),
        in_specs=[in_vmem] * (1 + len(weights) + len(blocks)),
        out_specs=[in_vmem] * 3,
        out_shape=[
            jax.ShapeDtypeStruct(partly.shape, jnp.float32),
            jax.ShapeDtypeStruct((1, partly.shape[0]), jnp.float32),
            jax.ShapeDtypeStruct((8, partly.shape[0]), jnp.float32),
        ],
        compiler_params=params,
        name="rest_part",
    )(partly, *weights, *blocks)


def diagonal(count):
    down = lax.broadcasted_iota(jnp.int32, (count, count), 0)
    across = lax.broadcasted_iota(jnp.int32, (count, count), 1)
    return down == across


def finish_kernel(features, count, updated_ref, *refs):
    squares_refs, (out_ref, scaled, sems) = refs[:count], refs[count:]
    per_group, columns = updated_ref.shape
    squares = squares_refs[0][:1]
    for ref in squares_refs[1:]:
        squares += ref[:1]
    spread = jnp.broadcast_to(scale_of(squares, features), (per_group, per_group))
    scale = jnp.sum(jnp.where(diagonal(per_group), spread, 0.0), axis=1, keepdims=True)
    tile = tile_of(columns, 4)
    copies = []
    for i in range(columns // tile):
        here = pl.ds(i * tile, tile)
        scaled[:, here] = updated_ref[:, here] * scale
        copies.append(pltpu.make_async_copy(scaled.at[:, here], out_ref.at[:, here], sems.at[i]))
        copies[-1].start()
    for copy in copies:
        copy.wait()


def finish(updated, squares, features):
    count = len(squares)
    return pl.pallas_call(
        functools.partial(finish_kernel, features, count),
        in_specs=[in_vmem] * (1 + count),
        out_specs=anywhere,
        out_shape=jax.ShapeDtypeStruct(updated.shape, jnp.float32),
        scratch_shapes=[
            pltpu.VMEM(updated.shape, jnp.float32),
            pltpu.SemaphoreType.DMA((updated.shape[1] // tile_of(updated.shape[1], 4),)),
        ],
        compiler_params=params,
        name="finish",
    )(updated, *squares)


def exchange(array, axis, step):
    return lax.ppermute(array, axis, [(i, i ^ step) for i in range(lax.axis_size(axis))])


def terms(array, axis, together):
    size = lax.axis_size(axis)
    if size & (size - 1):
        return [lax.psum(array, axis)]
    parts, step = [array], 1
    while step < size:
        array = sum(parts[1:], parts[0])
        width = min(1 << together, size // step)
        parts = [array] + [exchange(array, axis, step * k) for k in range(1, width)]
        step *= width
    return parts


def flipped_terms(array, wide):
    comp, feat = lax.axis_size("comp"), lax.axis_size("feat")
    if comp % 2 or comp & (comp - 1) or feat & (feat - 1):
        return terms(array, "feat", 2)
    widths, step = [], 1
    while step < feat:
        widths.append(min(4, feat // step))
        step *= widths[-1]
    parts, step = [array], 1
    for stage, width in enumerate(widths):
        if stage:
            array = sum((part[:1] for part in parts[1:]), parts[0][:1])
            wide = jnp.broadcast_to(array, wide.shape)
        flip = int(stage + 1 < len(widths) or len(widths) % 2 == 0)
        parts = [] if flip else [array]
        for k in range(0 if flip else 1, width):
            pairs = [
                (i * feat + j, (i ^ flip) * feat + (j ^ (k * step))) for i in range(comp) for j in range(feat)
            ]
            parts.append(lax.ppermute(wide if k == width - 1 else array, ("comp", "feat"), pairs))
        step *= width
    return parts


def gather(own):
    size = lax.axis_size("comp")
    if size & (size - 1):
        arrays, group = lax.all_gather(own, "comp"), lax.axis_index("comp")
        return {step: arrays[owner(group, step, size)] for step in range(1, size)}
    return {step: exchange(own, "comp", step) for step in range(1, size)}


def shards(samples, start_vectors):
    comp = lax.axis_size("comp")
    feat = lax.axis_size("feat")
    sample = samples[0]
    rows = sample.shape[0]
    features = sample.shape[1] * feat
    even = comp & (comp - 1) == 0

    blocks = {step: exchange(start_vectors, "comp", step) for step in range(2, comp, 2)} if even else gather(start_vectors)
    projected, vectors, sample = project(
        *(pltpu.with_memory_space_constraint(array, pltpu.HBM) for array in (start_vectors, sample))
    )
    if even and comp > 1:
        blocks[1] = exchange(vectors, "comp", 1)
    parts = terms(projected, "feat", 1)
    projected = sum(parts[1:], parts[0])
    if even:
        others = {step: exchange(projected, "comp", step) for step in range(1, comp, 2)}
    else:
        others = gather(projected)
    near = [1][: comp - 1]
    far = list(range(2, comp))

    def of(arrays, steps):
        return [arrays[step] for step in steps]

    partly = first_part(projected, sample, vectors, near, of(others, near), of(blocks, near), features)
    if even:
        for step in range(2, comp, 2):
            blocks[step], others[1] = lax.optimization_barrier((blocks[step], others[1]))
            blocks[step + 1] = exchange(blocks[step], "comp", 1)
            others[step] = exchange(others[step + 1], "comp", 1)
    projected, partly = lax.optimization_barrier((projected, partly))
    weights = couple(projected, far, of(others, far), rows, features) if far else []
    updated, squares, wide = rest_part(partly, weights, of(blocks, far))
    return finish(updated, flipped_terms(squares, wide), features)


def solution(mesh):
    in_specs = (P(None, None, "feat"), P("comp", "feat"))
    out_specs = P("comp", "feat")
    return jax.shard_map(shards, mesh=mesh, in_specs=in_specs, out_specs=out_specs, check_vma=False)
```

```python
import functools

import jax
import jax.numpy as jnp
from jax import lax
from jax.experimental import pallas as pl
from jax.experimental.pallas import tpu as pltpu
from jax.sharding import PartitionSpec as P

step_rate = 0.1
epsilon = 1e-06
lanes = 128
in_vmem = pl.BlockSpec(memory_space=pltpu.VMEM)
anywhere = pl.BlockSpec(memory_space=pl.ANY)
params = pltpu.CompilerParams(vmem_limit_bytes=16 << 20)


def tile_of(columns, most):
    if columns % lanes:
        return columns
    units = columns // lanes
    return lanes * max(u for u in range(1, most + 1) if units % u == 0)


def halves(array):
    top = array.astype(jnp.bfloat16)
    return top, (array - top.astype(jnp.float32)).astype(jnp.bfloat16)


def product(left, right, transposed=False):
    dims = (((1,), (1 if transposed else 0,)), ((), ()))
    dot = functools.partial(lax.dot_general, dimension_numbers=dims, preferred_element_type=jnp.float32)
    left_top, left_rest = left if isinstance(left, tuple) else halves(left)
    right_top, right_rest = halves(right)
    rows = left_top.shape[0]
    both = dot(jnp.concatenate([left_top, left_rest], axis=0), right_top)
    return both[:rows] + (both[rows:] + dot(left_top, right_rest))


def scale_of(squares, features):
    return lax.rsqrt(squares / features + epsilon)


def loop(columns, most, body, init):
    tile = tile_of(columns, most)
    for i in range(columns // tile):
        init = body(i, pl.ds(i * tile, tile), init)
    return init


def squares_by_lane(array):
    squares = array * array
    if array.shape[1] % lanes:
        return jnp.sum(squares, axis=1, keepdims=True)
    return sum(squares[:, k : k + lanes] for k in range(0, array.shape[1], lanes))


def relay_pieces(columns):
    first = columns // lanes // 2 * lanes + lanes
    return [(start, stop) for start, stop in ((0, first), (first, columns)) if start < stop <= columns]


def project_kernel(x_hbm, s_hbm, out_ref, x_ref, s_ref, sems):
    per_group, columns = x_ref.shape
    rows = s_ref.shape[0]

    def copies(i, here):
        return (
            pltpu.make_async_copy(x_hbm.at[:, here], x_ref.at[:, here], sems.at[0, i]),
            pltpu.make_async_copy(s_hbm.at[:, here], s_ref.at[:, here], sems.at[1, i]),
        )

    def begin(i, here, carry):
        for copy in copies(i, here):
            copy.start()
        return carry

    def body(i, here, carry):
        for copy in copies(i, here):
            copy.wait()
        x = x_ref[:, here]
        projected, squares = carry
        projected += product(x, s_ref[:, here], transposed=True)
        return projected, squares + squares_by_lane(x)

    loop(columns, 4, begin, 0)
    projected, squares = loop(columns, 4, body, (0.0, 0.0))
    squares = jnp.sum(squares, axis=1, keepdims=True)
    out_ref[:, :rows] = projected
    out_ref[:, rows:] = jnp.broadcast_to(squares, (per_group, out_ref.shape[1] - rows))


def project(x, sample):
    per_group, columns = x.shape
    rows = sample.shape[0]
    width = -(-(rows + 1) // lanes) * lanes
    return pl.pallas_call(
        project_kernel,
        in_specs=[anywhere] * 2,
        out_specs=[in_vmem] * 3,
        out_shape=[
            jax.ShapeDtypeStruct((per_group, width), jnp.float32),
            jax.ShapeDtypeStruct(x.shape, jnp.float32),
            jax.ShapeDtypeStruct(sample.shape, jnp.float32),
        ],
        scratch_shapes=[pltpu.SemaphoreType.DMA((2, columns // tile_of(columns, 4)))],
        compiler_params=params,
        name="project",
    )(x, sample)


def images_of(p_ref, rows, features):
    scale = scale_of(p_ref[:, rows : rows + 1], features)
    return p_ref[:, :rows] * scale, scale


def owner(group, step, size):
    return (group + step) % size if size & (size - 1) else group ^ step


def couplings(images, steps, projected_refs, features):
    group, size = lax.axis_index("comp"), lax.axis_size("comp")
    rows = images.shape[1]
    others = []
    for step, p_ref in zip(steps, projected_refs):
        other, scale = images_of(p_ref, rows, features)
        others.append(other * (scale * jnp.where(owner(group, step, size) < group, -step_rate / (features * rows), 0.0)))
    return product(images, jnp.concatenate(others, axis=0), transposed=True)


def first_kernel(features, steps, p_ref, s_ref, x_ref, *refs):
    count = len(steps)
    projected_refs, x_refs, out_ref = refs[:count], refs[count : 2 * count], refs[2 * count]
    rows = s_ref.shape[0]
    images, scale = images_of(p_ref, rows, features)
    shared = product(images, images * scale, transposed=True)
    later = lax.broadcasted_iota(jnp.int32, shared.shape, 0)
    earlier = lax.broadcasted_iota(jnp.int32, shared.shape, 1)
    weights = [images * (step_rate / rows), jnp.where(earlier < later, shared * (-step_rate / (features * rows)), 0.0)]
    if count:
        weights.append(couplings(images, steps, projected_refs, features))
    weights = halves(jnp.concatenate(weights, axis=1))

    def body(i, here, carry):
        x = x_ref[:, here]
        others = [ref[:, here] for ref in x_refs]
        out_ref[:, here] = scale * x + product(weights, jnp.concatenate([s_ref[:, here], x, *others], axis=0))
        return carry

    loop(x_ref.shape[1], 4, body, 0)


def first_part(projected, sample, x, steps, others, blocks, features):
    return pl.pallas_call(
        functools.partial(first_kernel, features, steps),
        in_specs=[in_vmem] * (3 + 2 * len(steps)),
        out_specs=in_vmem,
        out_shape=jax.ShapeDtypeStruct(x.shape, jnp.float32),
        compiler_params=params,
        name="first_part",
    )(projected, sample, x, *others, *blocks)


def couple_kernel(features, rows, steps, p_ref, *refs):
    projected_refs, (top_ref, rest_ref) = refs[:-2], refs[-2:]
    top_ref[...], rest_ref[...] = halves(couplings(images_of(p_ref, rows, features)[0], steps, projected_refs, features))


def couple(projected, steps, others, rows, features):
    per_group = projected.shape[0]
    return pl.pallas_call(
        functools.partial(couple_kernel, features, rows, steps),
        in_specs=[in_vmem] * (1 + len(steps)),
        out_specs=[in_vmem] * 2,
        out_shape=[jax.ShapeDtypeStruct((per_group, per_group * len(steps)), jnp.bfloat16)] * 2,
        compiler_params=params,
        cost_estimate=pl.CostEstimate(flops=4250000000, bytes_accessed=4 * projected.size, transcendentals=0),
        name="couple",
    )(projected, *others)


def rest_kernel(pieces, t_ref, *refs):
    refs, (out_ref, squares_ref, wide_ref) = list(refs[:-3]), refs[-3:]
    per_group, columns = t_ref.shape
    if pieces:
        weights = refs.pop(0)[...], refs.pop(0)[...]
    held = [[(*edges, refs.pop(0)) for edges in ranges] for ranges in pieces]

    def part(ranges, here):
        columns = []
        for start, stop, ref in ranges:
            first, last = max(start, here.start), min(stop, here.start + here.size)
            if first < last:
                columns.append(ref[:, first - start : last - start])
        return columns[0] if len(columns) == 1 else jnp.concatenate(columns, axis=1)

    def body(i, here, squares):
        updated = t_ref[:, here]
        if pieces:
            updated += product(weights, jnp.concatenate([part(ranges, here) for ranges in held], axis=0))
        out_ref[:, here] = updated
        return squares + squares_by_lane(updated)

    squares = jnp.sum(loop(columns, 4, body, 0.0), axis=1, keepdims=True)
    spread = jnp.broadcast_to(squares, (per_group, per_group))
    row = jnp.sum(jnp.where(diagonal(per_group), spread, 0.0), axis=0, keepdims=True)
    squares_ref[...] = row
    wide_ref[...] = jnp.broadcast_to(row, wide_ref.shape)


def rest_part(partly, weights, blocks):
    pieces = []
    for block in blocks:
        edges = [sum(piece.shape[1] for piece in block[:k]) for k in range(len(block) + 1)]
        pieces.append(list(zip(edges[:-1], edges[1:])))
    blocks = [piece for block in blocks for piece in block]
    return pl.pallas_call(
        functools.partial(rest_kernel, pieces),
        in_specs=[in_vmem] * (1 + len(weights) + len(blocks)),
        out_specs=[in_vmem] * 3,
        out_shape=[
            jax.ShapeDtypeStruct(partly.shape, jnp.float32),
            jax.ShapeDtypeStruct((1, partly.shape[0]), jnp.float32),
            jax.ShapeDtypeStruct((8, partly.shape[0]), jnp.float32),
        ],
        compiler_params=params,
        name="rest_part",
    )(partly, *weights, *blocks)


def diagonal(count):
    down = lax.broadcasted_iota(jnp.int32, (count, count), 0)
    across = lax.broadcasted_iota(jnp.int32, (count, count), 1)
    return down == across


def finish_kernel(features, count, updated_ref, *refs):
    squares_refs, (out_ref, scaled, sems) = refs[:count], refs[count:]
    per_group, columns = updated_ref.shape
    squares = squares_refs[0][:1]
    for ref in squares_refs[1:]:
        squares += ref[:1]
    spread = jnp.broadcast_to(scale_of(squares, features), (per_group, per_group))
    scale = jnp.sum(jnp.where(diagonal(per_group), spread, 0.0), axis=1, keepdims=True)
    tile = tile_of(columns, 4)
    copies = []
    for i in range(columns // tile):
        here = pl.ds(i * tile, tile)
        scaled[:, here] = updated_ref[:, here] * scale
        copies.append(pltpu.make_async_copy(scaled.at[:, here], out_ref.at[:, here], sems.at[i]))
        copies[-1].start()
    for copy in copies:
        copy.wait()


def finish(updated, squares, features):
    count = len(squares)
    return pl.pallas_call(
        functools.partial(finish_kernel, features, count),
        in_specs=[in_vmem] * (1 + count),
        out_specs=anywhere,
        out_shape=jax.ShapeDtypeStruct(updated.shape, jnp.float32),
        scratch_shapes=[
            pltpu.VMEM(updated.shape, jnp.float32),
            pltpu.SemaphoreType.DMA((updated.shape[1] // tile_of(updated.shape[1], 4),)),
        ],
        compiler_params=params,
        name="finish",
    )(updated, *squares)


def exchange(array, axis, step):
    return lax.ppermute(array, axis, [(i, i ^ step) for i in range(lax.axis_size(axis))])


def terms(array, axis, together):
    size = lax.axis_size(axis)
    if size & (size - 1):
        return [lax.psum(array, axis)]
    parts, step = [array], 1
    while step < size:
        array = sum(parts[1:], parts[0])
        width = min(1 << together, size // step)
        parts = [array] + [exchange(array, axis, step * k) for k in range(1, width)]
        step *= width
    return parts


def flipped_terms(array, wide):
    comp, feat = lax.axis_size("comp"), lax.axis_size("feat")
    if comp % 2 or comp & (comp - 1) or feat & (feat - 1):
        return terms(array, "feat", 2)
    widths, step = [], 1
    while step < feat:
        widths.append(min(4, feat // step))
        step *= widths[-1]
    parts, step = [array], 1
    for stage, width in enumerate(widths):
        if stage:
            array = sum((part[:1] for part in parts[1:]), parts[0][:1])
            wide = jnp.broadcast_to(array, wide.shape)
        flip = int(stage + 1 < len(widths) or len(widths) % 2 == 0)
        parts = [] if flip else [array]
        for k in range(0 if flip else 1, width):
            pairs = [
                (i * feat + j, (i ^ flip) * feat + (j ^ (k * step))) for i in range(comp) for j in range(feat)
            ]
            parts.append(lax.ppermute(wide if k == width - 1 else array, ("comp", "feat"), pairs))
        step *= width
    return parts


def gather(own):
    size = lax.axis_size("comp")
    if size & (size - 1):
        arrays, group = lax.all_gather(own, "comp"), lax.axis_index("comp")
        return {step: arrays[owner(group, step, size)] for step in range(1, size)}
    return {step: exchange(own, "comp", step) for step in range(1, size)}


def shards(samples, start_vectors):
    comp = lax.axis_size("comp")
    feat = lax.axis_size("feat")
    sample = samples[0]
    rows = sample.shape[0]
    features = sample.shape[1] * feat
    even = comp & (comp - 1) == 0

    blocks = {step: exchange(start_vectors, "comp", step) for step in range(2, comp, 2)} if even else gather(start_vectors)
    projected, vectors, sample = project(
        *(pltpu.with_memory_space_constraint(array, pltpu.HBM) for array in (start_vectors, sample))
    )
    if even and comp > 1:
        blocks[1] = exchange(vectors, "comp", 1)
    parts = terms(projected, "feat", 1)
    projected = sum(parts[1:], parts[0])
    if even:
        others = {step: exchange(projected, "comp", step) for step in range(1, comp, 2)}
    else:
        others = gather(projected)
    near = [1][: comp - 1]
    far = list(range(2, comp))

    def of(arrays, steps):
        return [arrays[step] for step in steps]

    partly = first_part(projected, sample, vectors, near, of(others, near), of(blocks, near), features)
    if even:
        for step in range(2, comp, 2):
            blocks[step], others[1] = lax.optimization_barrier((blocks[step], others[1]))
            vectors = blocks[step]
            blocks[step + 1] = [exchange(vectors[:, i:j], "comp", 1) for i, j in relay_pieces(vectors.shape[1])]
            others[step] = exchange(others[step + 1], "comp", 1)
    projected, partly = lax.optimization_barrier((projected, partly))
    weights = couple(projected, far, of(others, far), rows, features) if far else []
    updated, squares, wide = rest_part(partly, weights, [b if isinstance(b, list) else [b] for b in of(blocks, far)])
    return finish(updated, flipped_terms(squares, wide), features)


def solution(mesh):
    in_specs = (P(None, None, "feat"), P("comp", "feat"))
    out_specs = P("comp", "feat")
    return jax.shard_map(shards, mesh=mesh, in_specs=in_specs, out_specs=out_specs, check_vma=False)
```

```python
import functools

import jax
import jax.numpy as jnp
from jax import lax
from jax.experimental import pallas as pl
from jax.experimental.pallas import tpu as pltpu
from jax.sharding import PartitionSpec as P

step_rate = 0.1
epsilon = 1e-06
lanes = 128
in_vmem = pl.BlockSpec(memory_space=pltpu.VMEM)
anywhere = pl.BlockSpec(memory_space=pl.ANY)
params = pltpu.CompilerParams(vmem_limit_bytes=16 << 20)


def tile_of(columns, most):
    if columns % lanes:
        return columns
    units = columns // lanes
    return lanes * max(u for u in range(1, most + 1) if units % u == 0)


def halves(array):
    top = array.astype(jnp.bfloat16)
    return top, (array - top.astype(jnp.float32)).astype(jnp.bfloat16)


def product(left, right, transposed=False):
    dims = (((1,), (1 if transposed else 0,)), ((), ()))
    dot = functools.partial(lax.dot_general, dimension_numbers=dims, preferred_element_type=jnp.float32)
    left_top, left_rest = left if isinstance(left, tuple) else halves(left)
    right_top, right_rest = halves(right)
    rows = left_top.shape[0]
    both = dot(jnp.concatenate([left_top, left_rest], axis=0), right_top)
    return both[:rows] + (both[rows:] + dot(left_top, right_rest))


def scale_of(squares, features):
    return lax.rsqrt(squares / features + epsilon)


def loop(columns, most, body, init):
    tile = tile_of(columns, most)
    return lax.fori_loop(0, columns // tile, lambda i, c: body(i, pl.ds(pl.multiple_of(i * tile, tile), tile), c), init, unroll=True)


def project_kernel(x_hbm, s_hbm, out_ref, x_ref, s_ref, sems):
    per_group, columns = x_ref.shape
    rows = s_ref.shape[0]

    def copies(i, here):
        return (
            pltpu.make_async_copy(x_hbm.at[:, here], x_ref.at[:, here], sems.at[0, i]),
            pltpu.make_async_copy(s_hbm.at[:, here], s_ref.at[:, here], sems.at[1, i]),
        )

    def begin(i, here, carry):
        for copy in copies(i, here):
            copy.start()
        return carry

    def body(i, here, carry):
        for copy in copies(i, here):
            copy.wait()
        x = x_ref[:, here]
        projected, squares = carry
        projected += product(x, s_ref[:, here], transposed=True)
        return projected, squares + jnp.sum(x * x, axis=1, keepdims=True)

    loop(columns, 4, begin, 0)
    zeros = jnp.zeros((per_group, rows), jnp.float32), jnp.zeros((per_group, 1), jnp.float32)
    projected, squares = loop(columns, 4, body, zeros)
    out_ref[:, :rows] = projected
    out_ref[:, rows:] = jnp.broadcast_to(squares, (per_group, out_ref.shape[1] - rows))


def project(x, sample):
    per_group, columns = x.shape
    rows = sample.shape[0]
    width = -(-(rows + 1) // lanes) * lanes
    return pl.pallas_call(
        project_kernel,
        in_specs=[anywhere] * 2,
        out_specs=[in_vmem] * 3,
        out_shape=[
            jax.ShapeDtypeStruct((per_group, width), jnp.float32),
            jax.ShapeDtypeStruct(x.shape, jnp.float32),
            jax.ShapeDtypeStruct(sample.shape, jnp.float32),
        ],
        scratch_shapes=[pltpu.SemaphoreType.DMA((2, columns // tile_of(columns, 4)))],
        compiler_params=params,
        name="project",
    )(x, sample)


def images_of(p_ref, rows, features):
    scale = scale_of(p_ref[:, rows : rows + 1], features)
    return p_ref[:, :rows] * scale, scale


def owner(group, step, size):
    return (group + step) % size if size & (size - 1) else group ^ step


def couplings(images, steps, projected_refs, features):
    group, size = lax.axis_index("comp"), lax.axis_size("comp")
    rows = images.shape[1]
    others = []
    for step, p_ref in zip(steps, projected_refs):
        other, scale = images_of(p_ref, rows, features)
        others.append(other * (scale * jnp.where(owner(group, step, size) < group, -step_rate / (features * rows), 0.0)))
    return product(images, jnp.concatenate(others, axis=0), transposed=True)


def first_kernel(features, steps, p_ref, s_ref, x_ref, *refs):
    count = len(steps)
    projected_refs, x_refs, out_ref = refs[:count], refs[count : 2 * count], refs[2 * count]
    rows = s_ref.shape[0]
    images, scale = images_of(p_ref, rows, features)
    shared = product(images, images * scale, transposed=True)
    later = lax.broadcasted_iota(jnp.int32, shared.shape, 0)
    earlier = lax.broadcasted_iota(jnp.int32, shared.shape, 1)
    weights = [images * (step_rate / rows), jnp.where(earlier < later, shared * (-step_rate / (features * rows)), 0.0)]
    if count:
        weights.append(couplings(images, steps, projected_refs, features))
    weights = halves(jnp.concatenate(weights, axis=1))

    def body(i, here, carry):
        x = x_ref[:, here]
        others = [ref[:, here] for ref in x_refs]
        out_ref[:, here] = scale * x + product(weights, jnp.concatenate([s_ref[:, here], x, *others], axis=0))
        return carry

    loop(x_ref.shape[1], 4, body, 0)


def first_part(projected, sample, x, steps, others, blocks, features):
    return pl.pallas_call(
        functools.partial(first_kernel, features, steps),
        in_specs=[in_vmem] * (3 + 2 * len(steps)),
        out_specs=in_vmem,
        out_shape=jax.ShapeDtypeStruct(x.shape, jnp.float32),
        compiler_params=params,
        name="first_part",
    )(projected, sample, x, *others, *blocks)


def couple_kernel(features, rows, steps, p_ref, *refs):
    projected_refs, (top_ref, rest_ref) = refs[:-2], refs[-2:]
    top_ref[...], rest_ref[...] = halves(couplings(images_of(p_ref, rows, features)[0], steps, projected_refs, features))


def couple(projected, steps, others, rows, features):
    per_group = projected.shape[0]
    return pl.pallas_call(
        functools.partial(couple_kernel, features, rows, steps),
        in_specs=[in_vmem] * (1 + len(steps)),
        out_specs=[in_vmem] * 2,
        out_shape=[jax.ShapeDtypeStruct((per_group, per_group * len(steps)), jnp.bfloat16)] * 2,
        compiler_params=params,
        cost_estimate=pl.CostEstimate(flops=8650000000, bytes_accessed=4 * projected.size, transcendentals=0),
        name="couple",
    )(projected, *others)


def rest_kernel(count, t_ref, *refs):
    x_refs, (out_ref, squares_ref, wide_ref) = refs[-3 - count : -3], refs[-3:]
    per_group, columns = t_ref.shape
    if count:
        weights = refs[0][...], refs[1][...]

    def body(i, here, squares):
        updated = t_ref[:, here]
        if count:
            updated += product(weights, jnp.concatenate([ref[:, here] for ref in x_refs], axis=0))
        out_ref[:, here] = updated
        return squares + jnp.sum(updated * updated, axis=1, keepdims=True)

    squares = loop(columns, 4, body, jnp.zeros((per_group, 1), jnp.float32))
    spread = jnp.broadcast_to(squares, (per_group, per_group))
    row = jnp.sum(jnp.where(diagonal(per_group), spread, 0.0), axis=0, keepdims=True)
    squares_ref[...] = row
    wide_ref[...] = jnp.broadcast_to(row, wide_ref.shape)


def rest_part(partly, weights, blocks):
    return pl.pallas_call(
        functools.partial(rest_kernel, len(blocks)),
        in_specs=[in_vmem] * (1 + len(weights) + len(blocks)),
        out_specs=[in_vmem] * 3,
        out_shape=[
            jax.ShapeDtypeStruct(partly.shape, jnp.float32),
            jax.ShapeDtypeStruct((1, partly.shape[0]), jnp.float32),
            jax.ShapeDtypeStruct((8, partly.shape[0]), jnp.float32),
        ],
        compiler_params=params,
        name="rest_part",
    )(partly, *weights, *blocks)


def diagonal(count):
    down = lax.broadcasted_iota(jnp.int32, (count, count), 0)
    across = lax.broadcasted_iota(jnp.int32, (count, count), 1)
    return down == across


def finish_kernel(features, count, updated_ref, *refs):
    squares_refs, (out_ref, scaled, sems) = refs[:count], refs[count:]
    per_group, columns = updated_ref.shape
    squares = squares_refs[0][:1]
    for ref in squares_refs[1:]:
        squares += ref[:1]
    spread = jnp.broadcast_to(scale_of(squares, features), (per_group, per_group))
    scale = jnp.sum(jnp.where(diagonal(per_group), spread, 0.0), axis=1, keepdims=True)
    tile = tile_of(columns, 4)
    copies = []
    for i in range(columns // tile):
        here = pl.ds(i * tile, tile)
        scaled[:, here] = updated_ref[:, here] * scale
        copies.append(pltpu.make_async_copy(scaled.at[:, here], out_ref.at[:, here], sems.at[i]))
        copies[-1].start()
    for copy in copies:
        copy.wait()


def finish(updated, squares, features):
    count = len(squares)
    return pl.pallas_call(
        functools.partial(finish_kernel, features, count),
        in_specs=[in_vmem] * (1 + count),
        out_specs=anywhere,
        out_shape=jax.ShapeDtypeStruct(updated.shape, jnp.float32),
        scratch_shapes=[
            pltpu.VMEM(updated.shape, jnp.float32),
            pltpu.SemaphoreType.DMA((updated.shape[1] // tile_of(updated.shape[1], 4),)),
        ],
        compiler_params=params,
        name="finish",
    )(updated, *squares)


def exchange(array, axis, step):
    return lax.ppermute(array, axis, [(i, i ^ step) for i in range(lax.axis_size(axis))])


def terms(array, axis, together):
    size = lax.axis_size(axis)
    if size & (size - 1):
        return [lax.psum(array, axis)]
    parts, step = [array], 1
    while step < size:
        array = sum(parts[1:], parts[0])
        width = min(1 << together, size // step)
        parts = [array] + [exchange(array, axis, step * k) for k in range(1, width)]
        step *= width
    return parts


def flipped_terms(array, wide):
    comp, feat = lax.axis_size("comp"), lax.axis_size("feat")
    if comp % 2 or comp & (comp - 1) or feat & (feat - 1):
        return terms(array, "feat", 2)
    widths, step = [], 1
    while step < feat:
        widths.append(min(4, feat // step))
        step *= widths[-1]
    parts, step = [array], 1
    for stage, width in enumerate(widths):
        if stage:
            array = sum((part[:1] for part in parts[1:]), parts[0][:1])
            wide = jnp.broadcast_to(array, wide.shape)
        flip = int(stage + 1 < len(widths) or len(widths) % 2 == 0)
        parts = [] if flip else [array]
        for k in range(0 if flip else 1, width):
            pairs = [
                (i * feat + j, (i ^ flip) * feat + (j ^ (k * step))) for i in range(comp) for j in range(feat)
            ]
            parts.append(lax.ppermute(wide if k == width - 1 else array, ("comp", "feat"), pairs))
        step *= width
    return parts


def gather(own):
    size = lax.axis_size("comp")
    if size & (size - 1):
        arrays, group = lax.all_gather(own, "comp"), lax.axis_index("comp")
        return {step: arrays[owner(group, step, size)] for step in range(1, size)}
    return {step: exchange(own, "comp", step) for step in range(1, size)}


def shards(samples, start_vectors):
    comp = lax.axis_size("comp")
    feat = lax.axis_size("feat")
    sample = samples[0]
    rows = sample.shape[0]
    features = sample.shape[1] * feat
    even = comp & (comp - 1) == 0

    blocks = {step: exchange(start_vectors, "comp", step) for step in range(2, comp, 2)} if even else gather(start_vectors)
    projected, vectors, sample = project(
        *(pltpu.with_memory_space_constraint(array, pltpu.HBM) for array in (start_vectors, sample))
    )
    if even and comp > 1:
        blocks[1] = exchange(vectors, "comp", 1)
    parts = terms(projected, "feat", 1)
    projected = sum(parts[1:], parts[0])
    far = list(range(1, comp))

    def of(arrays, steps):
        return [arrays[step] for step in steps]

    others = {} if even else gather(projected)
    if even:
        others = {step: exchange(projected, "comp", step) for step in [1][: comp - 1]}
        others, projected = lax.optimization_barrier((others, projected))
    partly = first_part(projected, sample, vectors, [], [], [], features)
    projected, partly = lax.optimization_barrier((projected, partly))
    if even:
        others.update({step: exchange(projected, "comp", step) for step in range(3, comp, 2)})
        for step in range(2, comp, 2):
            blocks[step], partly = lax.optimization_barrier((blocks[step], partly))
            blocks[step + 1] = exchange(blocks[step], "comp", 1)
            others[step] = exchange(others[step + 1], "comp", 1)
    if even and comp > 1:
        projected, blocks[1] = lax.optimization_barrier((projected, blocks[1]))
    weights = couple(projected, far, of(others, far), rows, features) if far else []
    updated, squares, wide = rest_part(partly, weights, of(blocks, far))
    return finish(updated, flipped_terms(squares, wide), features)


def solution(mesh):
    in_specs = (P(None, None, "feat"), P("comp", "feat"))
    out_specs = P("comp", "feat")
    return jax.shard_map(shards, mesh=mesh, in_specs=in_specs, out_specs=out_specs, check_vma=False)
```

```python
import functools

import jax
import jax.numpy as jnp
from jax import lax
from jax.experimental import pallas as pl
from jax.experimental.pallas import tpu as pltpu
from jax.sharding import PartitionSpec as P

step_rate = 0.1
epsilon = 1e-06
lanes = 128
in_vmem = pl.BlockSpec(memory_space=pltpu.VMEM)
anywhere = pl.BlockSpec(memory_space=pl.ANY)
params = pltpu.CompilerParams(vmem_limit_bytes=16 << 20)


def tile_of(columns, most):
    if columns % lanes:
        return columns
    units = columns // lanes
    return lanes * max(u for u in range(1, most + 1) if units % u == 0)


def halves(array):
    top = array.astype(jnp.bfloat16)
    return top, (array - top.astype(jnp.float32)).astype(jnp.bfloat16)


def product(left, right, transposed=False):
    dims = (((1,), (1 if transposed else 0,)), ((), ()))
    dot = functools.partial(lax.dot_general, dimension_numbers=dims, preferred_element_type=jnp.float32)
    left_top, left_rest = left if isinstance(left, tuple) else halves(left)
    right_top, right_rest = halves(right)
    rows = left_top.shape[0]
    both = dot(jnp.concatenate([left_top, left_rest], axis=0), right_top)
    return both[:rows] + (both[rows:] + dot(left_top, right_rest))


def scale_of(squares, features):
    return lax.rsqrt(squares / features + epsilon)


def loop(columns, most, body, init):
    tile = tile_of(columns, most)
    return lax.fori_loop(0, columns // tile, lambda i, c: body(i, pl.ds(pl.multiple_of(i * tile, tile), tile), c), init, unroll=True)


def project_kernel(x_hbm, s_hbm, out_ref, x_ref, s_ref, sems):
    per_group, columns = x_ref.shape
    rows = s_ref.shape[0]

    def copies(i, here):
        return (
            pltpu.make_async_copy(x_hbm.at[:, here], x_ref.at[:, here], sems.at[0, i]),
            pltpu.make_async_copy(s_hbm.at[:, here], s_ref.at[:, here], sems.at[1, i]),
        )

    def begin(i, here, carry):
        for copy in copies(i, here):
            copy.start()
        return carry

    def body(i, here, carry):
        for copy in copies(i, here):
            copy.wait()
        x = x_ref[:, here]
        projected, squares = carry
        projected += product(x, s_ref[:, here], transposed=True)
        return projected, squares + jnp.sum(x * x, axis=1, keepdims=True)

    loop(columns, 4, begin, 0)
    zeros = jnp.zeros((per_group, rows), jnp.float32), jnp.zeros((per_group, 1), jnp.float32)
    projected, squares = loop(columns, 4, body, zeros)
    out_ref[:, :rows] = projected
    out_ref[:, rows:] = jnp.broadcast_to(squares, (per_group, out_ref.shape[1] - rows))


def project(x, sample):
    per_group, columns = x.shape
    rows = sample.shape[0]
    width = -(-(rows + 1) // lanes) * lanes
    return pl.pallas_call(
        project_kernel,
        in_specs=[anywhere] * 2,
        out_specs=[in_vmem] * 3,
        out_shape=[
            jax.ShapeDtypeStruct((per_group, width), jnp.float32),
            jax.ShapeDtypeStruct(x.shape, jnp.float32),
            jax.ShapeDtypeStruct(sample.shape, jnp.float32),
        ],
        scratch_shapes=[pltpu.SemaphoreType.DMA((2, columns // tile_of(columns, 4)))],
        compiler_params=params,
        name="project",
    )(x, sample)


def images_of(p_ref, rows, features):
    scale = scale_of(p_ref[:, rows : rows + 1], features)
    return p_ref[:, :rows] * scale, scale


def owner(group, step, size):
    return (group + step) % size if size & (size - 1) else group ^ step


def couplings(images, steps, projected_refs, features):
    group, size = lax.axis_index("comp"), lax.axis_size("comp")
    rows = images.shape[1]
    others = []
    for step, p_ref in zip(steps, projected_refs):
        other, scale = images_of(p_ref, rows, features)
        others.append(other * (scale * jnp.where(owner(group, step, size) < group, -step_rate / (features * rows), 0.0)))
    return product(images, jnp.concatenate(others, axis=0), transposed=True)


def first_kernel(features, steps, p_ref, s_ref, x_ref, *refs):
    count = len(steps)
    projected_refs, x_refs, out_ref = refs[:count], refs[count : 2 * count], refs[2 * count]
    rows = s_ref.shape[0]
    images, scale = images_of(p_ref, rows, features)
    shared = product(images, images * scale, transposed=True)
    later = lax.broadcasted_iota(jnp.int32, shared.shape, 0)
    earlier = lax.broadcasted_iota(jnp.int32, shared.shape, 1)
    weights = [images * (step_rate / rows), jnp.where(earlier < later, shared * (-step_rate / (features * rows)), 0.0)]
    if count:
        weights.append(couplings(images, steps, projected_refs, features))
    weights = halves(jnp.concatenate(weights, axis=1))

    def body(i, here, carry):
        x = x_ref[:, here]
        others = [ref[:, here] for ref in x_refs]
        out_ref[:, here] = scale * x + product(weights, jnp.concatenate([s_ref[:, here], x, *others], axis=0))
        return carry

    loop(x_ref.shape[1], 4, body, 0)


def first_part(projected, sample, x, steps, others, blocks, features):
    return pl.pallas_call(
        functools.partial(first_kernel, features, steps),
        in_specs=[in_vmem] * (3 + 2 * len(steps)),
        out_specs=in_vmem,
        out_shape=jax.ShapeDtypeStruct(x.shape, jnp.float32),
        compiler_params=params,
        name="first_part",
    )(projected, sample, x, *others, *blocks)


def couple_kernel(features, rows, steps, p_ref, *refs):
    projected_refs, (top_ref, rest_ref) = refs[:-2], refs[-2:]
    top_ref[...], rest_ref[...] = halves(couplings(images_of(p_ref, rows, features)[0], steps, projected_refs, features))


def couple(projected, steps, others, rows, features):
    per_group = projected.shape[0]
    return pl.pallas_call(
        functools.partial(couple_kernel, features, rows, steps),
        in_specs=[in_vmem] * (1 + len(steps)),
        out_specs=[in_vmem] * 2,
        out_shape=[jax.ShapeDtypeStruct((per_group, per_group * len(steps)), jnp.bfloat16)] * 2,
        compiler_params=params,
        cost_estimate=pl.CostEstimate(flops=9000000000, bytes_accessed=4 * projected.size, transcendentals=0),
        name="couple",
    )(projected, *others)


def rest_kernel(count, t_ref, *refs):
    x_refs, (out_ref, squares_ref, wide_ref) = refs[-3 - count : -3], refs[-3:]
    per_group, columns = t_ref.shape
    if count:
        weights = refs[0][...], refs[1][...]

    def body(i, here, squares):
        updated = t_ref[:, here]
        if count:
            updated += product(weights, jnp.concatenate([ref[:, here] for ref in x_refs], axis=0))
        out_ref[:, here] = updated
        return squares + jnp.sum(updated * updated, axis=1, keepdims=True)

    squares = loop(columns, 4, body, jnp.zeros((per_group, 1), jnp.float32))
    spread = jnp.broadcast_to(squares, (per_group, per_group))
    row = jnp.sum(jnp.where(diagonal(per_group), spread, 0.0), axis=0, keepdims=True)
    squares_ref[...] = row
    wide_ref[...] = jnp.broadcast_to(row, wide_ref.shape)


def rest_part(partly, weights, blocks):
    return pl.pallas_call(
        functools.partial(rest_kernel, len(blocks)),
        in_specs=[in_vmem] * (1 + len(weights) + len(blocks)),
        out_specs=[in_vmem] * 3,
        out_shape=[
            jax.ShapeDtypeStruct(partly.shape, jnp.float32),
            jax.ShapeDtypeStruct((1, partly.shape[0]), jnp.float32),
            jax.ShapeDtypeStruct((8, partly.shape[0]), jnp.float32),
        ],
        compiler_params=params,
        name="rest_part",
    )(partly, *weights, *blocks)


def diagonal(count):
    down = lax.broadcasted_iota(jnp.int32, (count, count), 0)
    across = lax.broadcasted_iota(jnp.int32, (count, count), 1)
    return down == across


def finish_kernel(features, count, updated_ref, *refs):
    squares_refs, (out_ref, scaled, sems) = refs[:count], refs[count:]
    per_group, columns = updated_ref.shape
    squares = squares_refs[0][:1]
    for ref in squares_refs[1:]:
        squares += ref[:1]
    spread = jnp.broadcast_to(scale_of(squares, features), (per_group, per_group))
    scale = jnp.sum(jnp.where(diagonal(per_group), spread, 0.0), axis=1, keepdims=True)
    tile = tile_of(columns, 4)
    copies = []
    for i in range(columns // tile):
        here = pl.ds(i * tile, tile)
        scaled[:, here] = updated_ref[:, here] * scale
        copies.append(pltpu.make_async_copy(scaled.at[:, here], out_ref.at[:, here], sems.at[i]))
        copies[-1].start()
    for copy in copies:
        copy.wait()


def finish(updated, squares, features):
    count = len(squares)
    return pl.pallas_call(
        functools.partial(finish_kernel, features, count),
        in_specs=[in_vmem] * (1 + count),
        out_specs=anywhere,
        out_shape=jax.ShapeDtypeStruct(updated.shape, jnp.float32),
        scratch_shapes=[
            pltpu.VMEM(updated.shape, jnp.float32),
            pltpu.SemaphoreType.DMA((updated.shape[1] // tile_of(updated.shape[1], 4),)),
        ],
        compiler_params=params,
        name="finish",
    )(updated, *squares)


def exchange(array, axis, step):
    return lax.ppermute(array, axis, [(i, i ^ step) for i in range(lax.axis_size(axis))])


def terms(array, axis, together):
    size = lax.axis_size(axis)
    if size & (size - 1):
        return [lax.psum(array, axis)]
    parts, step = [array], 1
    while step < size:
        array = sum(parts[1:], parts[0])
        width = min(1 << together, size // step)
        parts = [array] + [exchange(array, axis, step * k) for k in range(1, width)]
        step *= width
    return parts


def flipped_terms(array, wide):
    comp, feat = lax.axis_size("comp"), lax.axis_size("feat")
    if comp % 2 or comp & (comp - 1) or feat & (feat - 1):
        return terms(array, "feat", 2)
    bits = [1 << b for b in range(feat.bit_length() - 1)]
    bits = bits[:1] + bits[2:] + bits[1:2]
    stages = [bits[k : k + 2] for k in range(0, len(bits), 2)]
    parts = [array]
    for stage, own in enumerate(stages):
        if stage:
            array = sum((part[:1] for part in parts[1:]), parts[0][:1])
            wide = jnp.broadcast_to(array, wide.shape)
        flip = int(stage + 1 < len(stages) or len(stages) % 2 == 0)
        parts = [] if flip else [array]
        steps = [0, own[0]] + ([own[1], own[0] ^ own[1]] if len(own) > 1 else [])
        for step in steps if flip else steps[1:]:
            pairs = [(i * feat + j, (i ^ flip) * feat + (j ^ step)) for i in range(comp) for j in range(feat)]
            parts.append(lax.ppermute(wide if step == steps[-1] else array, ("comp", "feat"), pairs))
    return parts


def gather(own):
    size = lax.axis_size("comp")
    if size & (size - 1):
        arrays, group = lax.all_gather(own, "comp"), lax.axis_index("comp")
        return {step: arrays[owner(group, step, size)] for step in range(1, size)}
    return {step: exchange(own, "comp", step) for step in range(1, size)}


def shards(samples, start_vectors):
    comp = lax.axis_size("comp")
    feat = lax.axis_size("feat")
    sample = samples[0]
    rows = sample.shape[0]
    features = sample.shape[1] * feat
    even = comp & (comp - 1) == 0

    blocks = {step: exchange(start_vectors, "comp", step) for step in range(2, comp, 2)} if even else gather(start_vectors)
    projected, vectors, sample = project(
        *(pltpu.with_memory_space_constraint(array, pltpu.HBM) for array in (start_vectors, sample))
    )
    if even and comp > 1:
        blocks[1] = exchange(vectors, "comp", 1)
    parts = terms(projected, "feat", 1)
    projected = sum(parts[1:], parts[0])
    if even:
        others = {step: exchange(projected, "comp", step) for step in range(1, comp, 2)}
    else:
        others = gather(projected)
    near = [1][: comp - 1]
    far = list(range(2, comp))

    def of(arrays, steps):
        return [arrays[step] for step in steps]

    partly = first_part(projected, sample, vectors, near, of(others, near), of(blocks, near), features)
    if even:
        for step in range(2, comp, 2):
            blocks[step], others[1] = lax.optimization_barrier((blocks[step], others[1]))
            blocks[step + 1] = exchange(blocks[step], "comp", 1)
            others[step] = exchange(others[step + 1], "comp", 1)
    projected, partly = lax.optimization_barrier((projected, partly))
    weights = couple(projected, far, of(others, far), rows, features) if far else []
    updated, squares, wide = rest_part(partly, weights, of(blocks, far))
    return finish(updated, flipped_terms(squares, wide), features)


def solution(mesh):
    in_specs = (P(None, None, "feat"), P("comp", "feat"))
    out_specs = P("comp", "feat")
    return jax.shard_map(shards, mesh=mesh, in_specs=in_specs, out_specs=out_specs, check_vma=False)
```

```python
import functools

import jax
import jax.numpy as jnp
from jax import lax
from jax.experimental import pallas as pl
from jax.experimental.pallas import tpu as pltpu
from jax.sharding import PartitionSpec as P

step_rate = 0.1
epsilon = 1e-06
lanes = 128
block_rows = 16
in_vmem = pl.BlockSpec(memory_space=pltpu.VMEM)
anywhere = pl.BlockSpec(memory_space=pl.ANY)
params = pltpu.CompilerParams(vmem_limit_bytes=16 << 20)


def tile_of(columns, most):
    if columns % lanes:
        return columns
    units = columns // lanes
    return lanes * max(u for u in range(1, most + 1) if units % u == 0)


def halves(array):
    top = array.astype(jnp.bfloat16)
    return top, (array - top.astype(jnp.float32)).astype(jnp.bfloat16)


def product(left, right, transposed=False):
    dims = (((1,), (1 if transposed else 0,)), ((), ()))
    dot = functools.partial(lax.dot_general, dimension_numbers=dims, preferred_element_type=jnp.float32)
    left_top, left_rest = left if isinstance(left, tuple) else halves(left)
    right_top, right_rest = halves(right)
    rows = left_top.shape[0]
    both = dot(jnp.concatenate([left_top, left_rest], axis=0), right_top)
    return both[:rows] + (both[rows:] + dot(left_top, right_rest))


def scale_of(squares, features):
    return lax.rsqrt(squares / features + epsilon)


def loop(columns, most, body, init):
    tile = tile_of(columns, most)
    return lax.fori_loop(0, columns // tile, lambda i, c: body(i, pl.ds(pl.multiple_of(i * tile, tile), tile), c), init, unroll=True)


def project_kernel(x_hbm, s_hbm, out_ref, x_ref, s_ref, sems):
    per_group, columns = x_ref.shape
    rows = s_ref.shape[0]

    def copies(i, here):
        return (
            pltpu.make_async_copy(x_hbm.at[:, here], x_ref.at[:, here], sems.at[0, i]),
            pltpu.make_async_copy(s_hbm.at[:, here], s_ref.at[:, here], sems.at[1, i]),
        )

    def begin(i, here, carry):
        for copy in copies(i, here):
            copy.start()
        return carry

    def body(i, here, carry):
        for copy in copies(i, here):
            copy.wait()
        x = x_ref[:, here]
        projected, squares = carry
        projected += product(x, s_ref[:, here], transposed=True)
        return projected, squares + jnp.sum(x * x, axis=1, keepdims=True)

    loop(columns, 4, begin, 0)
    zeros = jnp.zeros((per_group, rows), jnp.float32), jnp.zeros((per_group, 1), jnp.float32)
    projected, squares = loop(columns, 4, body, zeros)
    out_ref[:, :rows] = projected
    out_ref[:, rows:] = jnp.broadcast_to(squares, (per_group, out_ref.shape[1] - rows))


def project(x, sample):
    per_group, columns = x.shape
    rows = sample.shape[0]
    width = -(-(rows + 1) // lanes) * lanes
    return pl.pallas_call(
        project_kernel,
        in_specs=[anywhere] * 2,
        out_specs=[in_vmem] * 3,
        out_shape=[
            jax.ShapeDtypeStruct((per_group, width), jnp.float32),
            jax.ShapeDtypeStruct(x.shape, jnp.float32),
            jax.ShapeDtypeStruct(sample.shape, jnp.float32),
        ],
        scratch_shapes=[pltpu.SemaphoreType.DMA((2, columns // tile_of(columns, 4)))],
        compiler_params=params,
        name="project",
    )(x, sample)


def images_of(p_ref, rows, features):
    scale = scale_of(p_ref[:, rows : rows + 1], features)
    return p_ref[:, :rows] * scale, scale


def owner(group, step, size):
    return (group + step) % size if size & (size - 1) else group ^ step


def couplings(images, steps, projected_refs, features):
    group, size = lax.axis_index("comp"), lax.axis_size("comp")
    rows = images.shape[1]
    others = []
    for step, p_ref in zip(steps, projected_refs):
        other, scale = images_of(p_ref, rows, features)
        others.append(other * (scale * jnp.where(owner(group, step, size) < group, -step_rate / (features * rows), 0.0)))
    return product(images, jnp.concatenate(others, axis=0), transposed=True)


def first_kernel(features, steps, p_ref, s_ref, x_ref, *refs):
    count = len(steps)
    projected_refs, x_refs, out_ref = refs[:count], refs[count : 2 * count], refs[2 * count]
    rows = s_ref.shape[0]
    images, scale = images_of(p_ref, rows, features)
    shared = product(images, images * scale, transposed=True)
    later = lax.broadcasted_iota(jnp.int32, shared.shape, 0)
    earlier = lax.broadcasted_iota(jnp.int32, shared.shape, 1)
    weights = [images * (step_rate / rows), jnp.where(earlier < later, shared * (-step_rate / (features * rows)), 0.0)]
    if count:
        weights.append(couplings(images, steps, projected_refs, features))
    weights = halves(jnp.concatenate(weights, axis=1))

    def body(i, here, carry):
        x = x_ref[:, here]
        others = [ref[:, here] for ref in x_refs]
        out_ref[:, here] = scale * x + product(weights, jnp.concatenate([s_ref[:, here], x, *others], axis=0))
        return carry

    loop(x_ref.shape[1], 4, body, 0)


def first_part(projected, sample, x, steps, others, blocks, features):
    return pl.pallas_call(
        functools.partial(first_kernel, features, steps),
        in_specs=[in_vmem] * (3 + 2 * len(steps)),
        out_specs=in_vmem,
        out_shape=jax.ShapeDtypeStruct(x.shape, jnp.float32),
        compiler_params=params,
        name="first_part",
    )(projected, sample, x, *others, *blocks)


def couple_kernel(features, rows, steps, p_ref, *refs):
    projected_refs, (top_ref, rest_ref) = refs[:-2], refs[-2:]
    top_ref[...], rest_ref[...] = halves(couplings(images_of(p_ref, rows, features)[0], steps, projected_refs, features))


def couple(projected, steps, others, rows, features):
    per_group = projected.shape[0]
    return pl.pallas_call(
        functools.partial(couple_kernel, features, rows, steps),
        in_specs=[in_vmem] * (1 + len(steps)),
        out_specs=[in_vmem] * 2,
        out_shape=[jax.ShapeDtypeStruct((per_group, per_group * len(steps)), jnp.bfloat16)] * 2,
        compiler_params=params,
        cost_estimate=pl.CostEstimate(flops=9000000000, bytes_accessed=4 * projected.size, transcendentals=0),
        name="couple",
    )(projected, *others)


def rest_kernel(count, t_ref, *refs):
    x_refs, (out_ref, squares_ref, wide_ref) = refs[-3 - count : -3], refs[-3:]
    per_group, columns = t_ref.shape
    if count:
        weights = refs[0][...], refs[1][...]

    def body(i, here, squares):
        updated = t_ref[:, here]
        if count:
            updated += product(weights, jnp.concatenate([ref[:, here] for ref in x_refs], axis=0))
        out_ref[:, here] = updated
        return squares + jnp.sum(updated * updated, axis=1, keepdims=True)

    squares = loop(columns, 4, body, jnp.zeros((per_group, 1), jnp.float32))
    spread = jnp.broadcast_to(squares, (per_group, per_group))
    row = jnp.sum(jnp.where(diagonal(per_group), spread, 0.0), axis=0, keepdims=True)
    squares_ref[...] = row
    wide_ref[...] = jnp.broadcast_to(row, wide_ref.shape)


def rest_part(partly, weights, blocks):
    return pl.pallas_call(
        functools.partial(rest_kernel, len(blocks)),
        in_specs=[in_vmem] * (1 + len(weights) + len(blocks)),
        out_specs=[in_vmem] * 3,
        out_shape=[
            jax.ShapeDtypeStruct(partly.shape, jnp.float32),
            jax.ShapeDtypeStruct((1, partly.shape[0]), jnp.float32),
            jax.ShapeDtypeStruct((8, partly.shape[0]), jnp.float32),
        ],
        compiler_params=params,
        name="rest_part",
    )(partly, *weights, *blocks)


def diagonal(count):
    down = lax.broadcasted_iota(jnp.int32, (count, count), 0)
    across = lax.broadcasted_iota(jnp.int32, (count, count), 1)
    return down == across


def finish_kernel(features, count, updated_ref, *refs):
    squares_refs, (out_ref, scaled, sems) = refs[:count], refs[count:]
    per_group, columns = updated_ref.shape
    squares = squares_refs[0][:1]
    for ref in squares_refs[1:]:
        squares += ref[:1]
    spread = jnp.broadcast_to(scale_of(squares, features), (per_group, per_group))
    scale = jnp.sum(jnp.where(diagonal(per_group), spread, 0.0), axis=1, keepdims=True)
    copies = []
    for i, first in enumerate(range(0, per_group, block_rows)):
        here = pl.ds(first, min(block_rows, per_group - first))
        scaled[here, :] = updated_ref[here, :] * scale[first : first + block_rows]
        copies.append(pltpu.make_async_copy(scaled.at[here, :], out_ref.at[here, :], sems.at[i]))
        copies[-1].start()
    for copy in copies:
        copy.wait()


def finish(updated, squares, features):
    count = len(squares)
    return pl.pallas_call(
        functools.partial(finish_kernel, features, count),
        in_specs=[in_vmem] * (1 + count),
        out_specs=anywhere,
        out_shape=jax.ShapeDtypeStruct(updated.shape, jnp.float32),
        scratch_shapes=[
            pltpu.VMEM(updated.shape, jnp.float32),
            pltpu.SemaphoreType.DMA((-(-updated.shape[0] // block_rows),)),
        ],
        compiler_params=params,
        name="finish",
    )(updated, *squares)


def exchange(array, axis, step):
    return lax.ppermute(array, axis, [(i, i ^ step) for i in range(lax.axis_size(axis))])


def terms(array, axis, together):
    size = lax.axis_size(axis)
    if size & (size - 1):
        return [lax.psum(array, axis)]
    parts, step = [array], 1
    while step < size:
        array = sum(parts[1:], parts[0])
        width = min(1 << together, size // step)
        parts = [array] + [exchange(array, axis, step * k) for k in range(1, width)]
        step *= width
    return parts


def flipped_terms(array, wide):
    comp, feat = lax.axis_size("comp"), lax.axis_size("feat")
    if comp % 2 or comp & (comp - 1) or feat & (feat - 1):
        return terms(array, "feat", 2)
    widths, step = [], 1
    while step < feat:
        widths.append(min(4, feat // step))
        step *= widths[-1]
    parts, step = [array], 1
    for stage, width in enumerate(widths):
        if stage:
            array = sum((part[:1] for part in parts[1:]), parts[0][:1])
            wide = jnp.broadcast_to(array, wide.shape)
        flip = int(stage + 1 < len(widths) or len(widths) % 2 == 0)
        parts = [] if flip else [array]
        for k in range(0 if flip else 1, width):
            pairs = [
                (i * feat + j, (i ^ flip) * feat + (j ^ (k * step))) for i in range(comp) for j in range(feat)
            ]
            parts.append(lax.ppermute(wide if k == width - 1 else array, ("comp", "feat"), pairs))
        step *= width
    return parts


def gather(own):
    size = lax.axis_size("comp")
    if size & (size - 1):
        arrays, group = lax.all_gather(own, "comp"), lax.axis_index("comp")
        return {step: arrays[owner(group, step, size)] for step in range(1, size)}
    return {step: exchange(own, "comp", step) for step in range(1, size)}


def shards(samples, start_vectors):
    comp = lax.axis_size("comp")
    feat = lax.axis_size("feat")
    sample = samples[0]
    rows = sample.shape[0]
    features = sample.shape[1] * feat
    even = comp & (comp - 1) == 0

    blocks = {step: exchange(start_vectors, "comp", step) for step in range(2, comp, 2)} if even else gather(start_vectors)
    projected, vectors, sample = project(
        *(pltpu.with_memory_space_constraint(array, pltpu.HBM) for array in (start_vectors, sample))
    )
    if even and comp > 1:
        blocks[1] = exchange(vectors, "comp", 1)
    parts = terms(projected, "feat", 1)
    projected = sum(parts[1:], parts[0])
    if even:
        others = {step: exchange(projected, "comp", step) for step in range(1, comp, 2)}
    else:
        others = gather(projected)
    near = [1][: comp - 1]
    far = list(range(2, comp))

    def of(arrays, steps):
        return [arrays[step] for step in steps]

    partly = first_part(projected, sample, vectors, near, of(others, near), of(blocks, near), features)
    if even:
        for step in range(2, comp, 2):
            blocks[step], others[1] = lax.optimization_barrier((blocks[step], others[1]))
            blocks[step + 1] = exchange(blocks[step], "comp", 1)
            others[step] = exchange(others[step + 1], "comp", 1)
    projected, partly = lax.optimization_barrier((projected, partly))
    weights = couple(projected, far, of(others, far), rows, features) if far else []
    updated, squares, wide = rest_part(partly, weights, of(blocks, far))
    return finish(updated, flipped_terms(squares, wide), features)


def solution(mesh):
    in_specs = (P(None, None, "feat"), P("comp", "feat"))
    out_specs = P("comp", "feat")
    return jax.shard_map(shards, mesh=mesh, in_specs=in_specs, out_specs=out_specs, check_vma=False)
```

```python
import functools

import jax
import jax.numpy as jnp
from jax import lax
from jax.experimental import pallas as pl
from jax.experimental.pallas import tpu as pltpu
from jax.sharding import PartitionSpec as P

step_rate = 0.1
epsilon = 1e-06
lanes = 128
in_vmem = pl.BlockSpec(memory_space=pltpu.VMEM)
anywhere = pl.BlockSpec(memory_space=pl.ANY)
params = pltpu.CompilerParams(vmem_limit_bytes=16 << 20)


def tile_of(columns, most):
    if columns % lanes:
        return columns
    units = columns // lanes
    return lanes * max(u for u in range(1, most + 1) if units % u == 0)


def halves(array):
    top = array.astype(jnp.bfloat16)
    return top, (array - top.astype(jnp.float32)).astype(jnp.bfloat16)


def product(left, right, transposed=False):
    dims = (((1,), (1 if transposed else 0,)), ((), ()))
    dot = functools.partial(lax.dot_general, dimension_numbers=dims, preferred_element_type=jnp.float32)
    left_top, left_rest = left if isinstance(left, tuple) else halves(left)
    right_top, right_rest = halves(right)
    rows = left_top.shape[0]
    both = dot(jnp.concatenate([left_top, left_rest], axis=0), right_top)
    return both[:rows] + (both[rows:] + dot(left_top, right_rest))


def scale_of(squares, features):
    return lax.rsqrt(squares / features + epsilon)


def loop(columns, most, body, init):
    tile = tile_of(columns, most)
    for i in range(columns // tile):
        init = body(i, pl.ds(i * tile, tile), init)
    return init


def squares_by_lane(array):
    squares = array * array
    if array.shape[1] % lanes:
        return jnp.sum(squares, axis=1, keepdims=True)
    return sum(squares[:, k : k + lanes] for k in range(0, array.shape[1], lanes))


def relay_pieces(columns):
    first = columns // lanes // 2 * lanes + lanes
    return [(start, stop) for start, stop in ((0, first), (first, columns)) if start < stop <= columns]


def project_kernel(x_hbm, s_hbm, out_ref, x_ref, s_ref, sems):
    per_group, columns = x_ref.shape
    rows = s_ref.shape[0]

    def copies(i, here):
        return (
            pltpu.make_async_copy(x_hbm.at[:, here], x_ref.at[:, here], sems.at[0, i]),
            pltpu.make_async_copy(s_hbm.at[:, here], s_ref.at[:, here], sems.at[1, i]),
        )

    def begin(i, here, carry):
        for copy in copies(i, here):
            copy.start()
        return carry

    def body(i, here, carry):
        for copy in copies(i, here):
            copy.wait()
        x = x_ref[:, here]
        projected, squares = carry
        projected += product(x, s_ref[:, here], transposed=True)
        return projected, squares + squares_by_lane(x)

    loop(columns, 4, begin, 0)
    projected, squares = loop(columns, 4, body, (0.0, 0.0))
    squares = jnp.sum(squares, axis=1, keepdims=True)
    out_ref[:, :rows] = projected
    out_ref[:, rows:] = jnp.broadcast_to(squares, (per_group, out_ref.shape[1] - rows))


def project(x, sample):
    per_group, columns = x.shape
    rows = sample.shape[0]
    width = -(-(rows + 1) // lanes) * lanes
    return pl.pallas_call(
        project_kernel,
        in_specs=[anywhere] * 2,
        out_specs=[in_vmem] * 3,
        out_shape=[
            jax.ShapeDtypeStruct((per_group, width), jnp.float32),
            jax.ShapeDtypeStruct(x.shape, jnp.float32),
            jax.ShapeDtypeStruct(sample.shape, jnp.float32),
        ],
        scratch_shapes=[pltpu.SemaphoreType.DMA((2, columns // tile_of(columns, 4)))],
        compiler_params=params,
        name="project",
    )(x, sample)


def images_of(p_ref, rows, features):
    scale = scale_of(p_ref[:, rows : rows + 1], features)
    return p_ref[:, :rows] * scale, scale


def owner(group, step, size):
    return (group + step) % size if size & (size - 1) else group ^ step


def couplings(images, steps, projected_refs, features):
    group, size = lax.axis_index("comp"), lax.axis_size("comp")
    rows = images.shape[1]
    others = []
    for step, p_ref in zip(steps, projected_refs):
        other, scale = images_of(p_ref, rows, features)
        others.append(other * (scale * jnp.where(owner(group, step, size) < group, -step_rate / (features * rows), 0.0)))
    return product(images, jnp.concatenate(others, axis=0), transposed=True)


def first_kernel(features, steps, p_ref, s_ref, x_ref, *refs):
    count = len(steps)
    projected_refs, x_refs, out_ref = refs[:count], refs[count : 2 * count], refs[2 * count]
    rows = s_ref.shape[0]
    images, scale = images_of(p_ref, rows, features)
    shared = product(images, images * scale, transposed=True)
    later = lax.broadcasted_iota(jnp.int32, shared.shape, 0)
    earlier = lax.broadcasted_iota(jnp.int32, shared.shape, 1)
    weights = [images * (step_rate / rows), jnp.where(earlier < later, shared * (-step_rate / (features * rows)), 0.0)]
    if count:
        weights.append(couplings(images, steps, projected_refs, features))
    weights = halves(jnp.concatenate(weights, axis=1))

    def body(i, here, carry):
        x = x_ref[:, here]
        others = [ref[:, here] for ref in x_refs]
        out_ref[:, here] = scale * x + product(weights, jnp.concatenate([s_ref[:, here], x, *others], axis=0))
        return carry

    loop(x_ref.shape[1], 4, body, 0)


def first_part(projected, sample, x, steps, others, blocks, features):
    return pl.pallas_call(
        functools.partial(first_kernel, features, steps),
        in_specs=[in_vmem] * (3 + 2 * len(steps)),
        out_specs=in_vmem,
        out_shape=jax.ShapeDtypeStruct(x.shape, jnp.float32),
        compiler_params=params,
        name="first_part",
    )(projected, sample, x, *others, *blocks)


def couple_kernel(features, rows, steps, p_ref, *refs):
    projected_refs, (top_ref, rest_ref) = refs[:-2], refs[-2:]
    top_ref[...], rest_ref[...] = halves(couplings(images_of(p_ref, rows, features)[0], steps, projected_refs, features))


def couple(projected, steps, others, rows, features):
    per_group = projected.shape[0]
    return pl.pallas_call(
        functools.partial(couple_kernel, features, rows, steps),
        in_specs=[in_vmem] * (1 + len(steps)),
        out_specs=[in_vmem] * 2,
        out_shape=[jax.ShapeDtypeStruct((per_group, per_group * len(steps)), jnp.bfloat16)] * 2,
        compiler_params=params,
        cost_estimate=pl.CostEstimate(flops=4150000000, bytes_accessed=4 * projected.size, transcendentals=0),
        name="couple",
    )(projected, *others)


def rest_kernel(pieces, t_ref, *refs):
    refs, (out_ref, squares_ref, wide_ref) = list(refs[:-3]), refs[-3:]
    per_group, columns = t_ref.shape
    if pieces:
        weights = refs.pop(0)[...], refs.pop(0)[...]
    held = [[(*edges, refs.pop(0)) for edges in ranges] for ranges in pieces]

    def part(ranges, here):
        columns = []
        for start, stop, ref in ranges:
            first, last = max(start, here.start), min(stop, here.start + here.size)
            if first < last:
                columns.append(ref[:, first - start : last - start])
        return columns[0] if len(columns) == 1 else jnp.concatenate(columns, axis=1)

    def body(i, here, squares):
        updated = t_ref[:, here]
        if pieces:
            updated += product(weights, jnp.concatenate([part(ranges, here) for ranges in held], axis=0))
        out_ref[:, here] = updated
        return squares + squares_by_lane(updated)

    squares = jnp.sum(loop(columns, 4, body, 0.0), axis=1, keepdims=True)
    spread = jnp.broadcast_to(squares, (per_group, per_group))
    row = jnp.sum(jnp.where(diagonal(per_group), spread, 0.0), axis=0, keepdims=True)
    squares_ref[...] = row
    wide_ref[...] = jnp.broadcast_to(row, wide_ref.shape)


def rest_part(partly, weights, blocks):
    pieces = []
    for block in blocks:
        edges = [sum(piece.shape[1] for piece in block[:k]) for k in range(len(block) + 1)]
        pieces.append(list(zip(edges[:-1], edges[1:])))
    blocks = [piece for block in blocks for piece in block]
    return pl.pallas_call(
        functools.partial(rest_kernel, pieces),
        in_specs=[in_vmem] * (1 + len(weights) + len(blocks)),
        out_specs=[in_vmem] * 3,
        out_shape=[
            jax.ShapeDtypeStruct(partly.shape, jnp.float32),
            jax.ShapeDtypeStruct((1, partly.shape[0]), jnp.float32),
            jax.ShapeDtypeStruct((8, partly.shape[0]), jnp.float32),
        ],
        compiler_params=params,
        name="rest_part",
    )(partly, *weights, *blocks)


def diagonal(count):
    down = lax.broadcasted_iota(jnp.int32, (count, count), 0)
    across = lax.broadcasted_iota(jnp.int32, (count, count), 1)
    return down == across


def finish_kernel(features, count, updated_ref, *refs):
    squares_refs, (out_ref, scaled, sems) = refs[:count], refs[count:]
    per_group, columns = updated_ref.shape
    squares = squares_refs[0][:1]
    for ref in squares_refs[1:]:
        squares += ref[:1]
    spread = jnp.broadcast_to(scale_of(squares, features), (per_group, per_group))
    scale = jnp.sum(jnp.where(diagonal(per_group), spread, 0.0), axis=1, keepdims=True)
    tile = tile_of(columns, 4)
    copies = []
    for i in range(columns // tile):
        here = pl.ds(i * tile, tile)
        scaled[:, here] = updated_ref[:, here] * scale
        copies.append(pltpu.make_async_copy(scaled.at[:, here], out_ref.at[:, here], sems.at[i]))
        copies[-1].start()
    for copy in copies:
        copy.wait()


def finish(updated, squares, features):
    count = len(squares)
    return pl.pallas_call(
        functools.partial(finish_kernel, features, count),
        in_specs=[in_vmem] * (1 + count),
        out_specs=anywhere,
        out_shape=jax.ShapeDtypeStruct(updated.shape, jnp.float32),
        scratch_shapes=[
            pltpu.VMEM(updated.shape, jnp.float32),
            pltpu.SemaphoreType.DMA((updated.shape[1] // tile_of(updated.shape[1], 4),)),
        ],
        compiler_params=params,
        name="finish",
    )(updated, *squares)


def exchange(array, axis, step):
    return lax.ppermute(array, axis, [(i, i ^ step) for i in range(lax.axis_size(axis))])


def terms(array, axis, together):
    size = lax.axis_size(axis)
    if size & (size - 1):
        return [lax.psum(array, axis)]
    parts, step = [array], 1
    while step < size:
        array = sum(parts[1:], parts[0])
        width = min(1 << together, size // step)
        parts = [array] + [exchange(array, axis, step * k) for k in range(1, width)]
        step *= width
    return parts


def flipped_terms(array, wide):
    comp, feat = lax.axis_size("comp"), lax.axis_size("feat")
    if comp % 2 or comp & (comp - 1) or feat & (feat - 1):
        return terms(array, "feat", 2)
    widths, step = [], 1
    while step < feat:
        widths.append(min(4, feat // step))
        step *= widths[-1]
    parts, step = [array], 1
    for stage, width in enumerate(widths):
        if stage:
            array = sum((part[:1] for part in parts[1:]), parts[0][:1])
            wide = jnp.broadcast_to(array, wide.shape)
        flip = int(stage + 1 < len(widths) or len(widths) % 2 == 0)
        parts = [] if flip else [array]
        for k in range(0 if flip else 1, width):
            pairs = [
                (i * feat + j, (i ^ flip) * feat + (j ^ (k * step))) for i in range(comp) for j in range(feat)
            ]
            parts.append(lax.ppermute(wide if k == width - 1 else array, ("comp", "feat"), pairs))
        step *= width
    return parts


def gather(own):
    size = lax.axis_size("comp")
    if size & (size - 1):
        arrays, group = lax.all_gather(own, "comp"), lax.axis_index("comp")
        return {step: arrays[owner(group, step, size)] for step in range(1, size)}
    return {step: exchange(own, "comp", step) for step in range(1, size)}


def shards(samples, start_vectors):
    comp = lax.axis_size("comp")
    feat = lax.axis_size("feat")
    sample = samples[0]
    rows = sample.shape[0]
    features = sample.shape[1] * feat
    even = comp & (comp - 1) == 0

    blocks = {step: exchange(start_vectors, "comp", step) for step in range(2, comp, 2)} if even else gather(start_vectors)
    projected, vectors, sample = project(
        *(pltpu.with_memory_space_constraint(array, pltpu.HBM) for array in (start_vectors, sample))
    )
    if even and comp > 1:
        blocks[1] = exchange(vectors, "comp", 1)
    parts = terms(projected, "feat", 1)
    projected = sum(parts[1:], parts[0])
    if even:
        others = {step: exchange(projected, "comp", step) for step in range(1, comp, 2)}
    else:
        others = gather(projected)
    far = list(range(1, comp))

    def of(arrays, steps):
        return [arrays[step] for step in steps]

    partly = first_part(projected, sample, vectors, [], [], [], features)
    if even:
        for step in range(2, comp, 2):
            blocks[step], partly = lax.optimization_barrier((blocks[step], partly))
            vectors = blocks[step]
            blocks[step + 1] = [exchange(vectors[:, i:j], "comp", 1) for i, j in relay_pieces(vectors.shape[1])]
            others[step] = exchange(others[step + 1], "comp", 1)
    projected, partly = lax.optimization_barrier((projected, partly))
    if even and comp > 1:
        projected, blocks[1] = lax.optimization_barrier((projected, blocks[1]))
    weights = couple(projected, far, of(others, far), rows, features) if far else []
    updated, squares, wide = rest_part(partly, weights, [b if isinstance(b, list) else [b] for b in of(blocks, far)])
    return finish(updated, flipped_terms(squares, wide), features)


def solution(mesh):
    in_specs = (P(None, None, "feat"), P("comp", "feat"))
    out_specs = P("comp", "feat")
    return jax.shard_map(shards, mesh=mesh, in_specs=in_specs, out_specs=out_specs, check_vma=False)
```

```python
import functools

import jax
import jax.numpy as jnp
from jax import lax
from jax.experimental import pallas as pl
from jax.experimental.pallas import tpu as pltpu
from jax.sharding import PartitionSpec as P

step_rate = 0.1
epsilon = 1e-06
lanes = 128
in_vmem = pl.BlockSpec(memory_space=pltpu.VMEM)
anywhere = pl.BlockSpec(memory_space=pl.ANY)
params = pltpu.CompilerParams(vmem_limit_bytes=16 << 20)


def tile_of(columns, most):
    if columns % lanes:
        return columns
    units = columns // lanes
    return lanes * max(u for u in range(1, most + 1) if units % u == 0)


def halves(array):
    top = array.astype(jnp.bfloat16)
    return top, (array - top.astype(jnp.float32)).astype(jnp.bfloat16)


def product(left, right, transposed=False):
    dims = (((1,), (1 if transposed else 0,)), ((), ()))
    dot = functools.partial(lax.dot_general, dimension_numbers=dims, preferred_element_type=jnp.float32)
    left_top, left_rest = left if isinstance(left, tuple) else halves(left)
    right_top, right_rest = halves(right)
    rows = left_top.shape[0]
    both = dot(jnp.concatenate([left_top, left_rest], axis=0), right_top)
    return both[:rows] + (both[rows:] + dot(left_top, right_rest))


def scale_of(squares, features):
    return lax.rsqrt(squares / features + epsilon)


def loop(columns, most, body, init):
    tile = tile_of(columns, most)
    return lax.fori_loop(0, columns // tile, lambda i, c: body(i, pl.ds(pl.multiple_of(i * tile, tile), tile), c), init, unroll=True)


def project_kernel(x_hbm, s_hbm, out_ref, x_ref, s_ref, sems):
    per_group, columns = x_ref.shape
    rows = s_ref.shape[0]

    def copies(i, here):
        return (
            pltpu.make_async_copy(x_hbm.at[:, here], x_ref.at[:, here], sems.at[0, i]),
            pltpu.make_async_copy(s_hbm.at[:, here], s_ref.at[:, here], sems.at[1, i]),
        )

    def begin(i, here, carry):
        for copy in copies(i, here):
            copy.start()
        return carry

    def body(i, here, carry):
        for copy in copies(i, here):
            copy.wait()
        x = x_ref[:, here]
        projected, squares = carry
        projected += product(x, s_ref[:, here], transposed=True)
        return projected, squares + jnp.sum(x * x, axis=1, keepdims=True)

    loop(columns, 4, begin, 0)
    zeros = jnp.zeros((per_group, rows), jnp.float32), jnp.zeros((per_group, 1), jnp.float32)
    projected, squares = loop(columns, 4, body, zeros)
    out_ref[:, :rows] = projected
    out_ref[:, rows:] = jnp.broadcast_to(squares, (per_group, out_ref.shape[1] - rows))


def project(x, sample):
    per_group, columns = x.shape
    rows = sample.shape[0]
    width = -(-(rows + 1) // lanes) * lanes
    return pl.pallas_call(
        project_kernel,
        in_specs=[anywhere] * 2,
        out_specs=[in_vmem] * 3,
        out_shape=[
            jax.ShapeDtypeStruct((per_group, width), jnp.float32),
            jax.ShapeDtypeStruct(x.shape, jnp.float32),
            jax.ShapeDtypeStruct(sample.shape, jnp.float32),
        ],
        scratch_shapes=[pltpu.SemaphoreType.DMA((2, columns // tile_of(columns, 4)))],
        compiler_params=params,
        name="project",
    )(x, sample)


def images_of(p_ref, rows, features):
    scale = scale_of(p_ref[:, rows : rows + 1], features)
    return p_ref[:, :rows] * scale, scale


def owner(group, step, size):
    return (group + step) % size if size & (size - 1) else group ^ step


def couplings(images, steps, projected_refs, features):
    group, size = lax.axis_index("comp"), lax.axis_size("comp")
    rows = images.shape[1]
    others = []
    for step, p_ref in zip(steps, projected_refs):
        other, scale = images_of(p_ref, rows, features)
        others.append(other * (scale * jnp.where(owner(group, step, size) < group, -step_rate / (features * rows), 0.0)))
    return product(images, jnp.concatenate(others, axis=0), transposed=True)


def first_kernel(features, steps, p_ref, s_ref, x_ref, *refs):
    count = len(steps)
    projected_refs, x_refs, out_ref = refs[:count], refs[count : 2 * count], refs[2 * count]
    rows = s_ref.shape[0]
    images, scale = images_of(p_ref, rows, features)
    shared = product(images, images * scale, transposed=True)
    later = lax.broadcasted_iota(jnp.int32, shared.shape, 0)
    earlier = lax.broadcasted_iota(jnp.int32, shared.shape, 1)
    weights = [images * (step_rate / rows), jnp.where(earlier < later, shared * (-step_rate / (features * rows)), 0.0)]
    if count:
        weights.append(couplings(images, steps, projected_refs, features))
    weights = halves(jnp.concatenate(weights, axis=1))

    def body(i, here, carry):
        x = x_ref[:, here]
        others = [ref[:, here] for ref in x_refs]
        out_ref[:, here] = scale * x + product(weights, jnp.concatenate([s_ref[:, here], x, *others], axis=0))
        return carry

    loop(x_ref.shape[1], 7, body, 0)


def first_part(projected, sample, x, steps, others, blocks, features):
    return pl.pallas_call(
        functools.partial(first_kernel, features, steps),
        in_specs=[in_vmem] * (3 + 2 * len(steps)),
        out_specs=in_vmem,
        out_shape=jax.ShapeDtypeStruct(x.shape, jnp.float32),
        compiler_params=params,
        name="first_part",
    )(projected, sample, x, *others, *blocks)


def couple_kernel(features, rows, steps, p_ref, *refs):
    projected_refs, (top_ref, rest_ref) = refs[:-2], refs[-2:]
    top_ref[...], rest_ref[...] = halves(couplings(images_of(p_ref, rows, features)[0], steps, projected_refs, features))


def couple(projected, steps, others, rows, features):
    per_group = projected.shape[0]
    return pl.pallas_call(
        functools.partial(couple_kernel, features, rows, steps),
        in_specs=[in_vmem] * (1 + len(steps)),
        out_specs=[in_vmem] * 2,
        out_shape=[jax.ShapeDtypeStruct((per_group, per_group * len(steps)), jnp.bfloat16)] * 2,
        compiler_params=params,
        cost_estimate=pl.CostEstimate(flops=9000000000, bytes_accessed=4 * projected.size, transcendentals=0),
        name="couple",
    )(projected, *others)


def rest_kernel(count, t_ref, *refs):
    x_refs, (out_ref, squares_ref, wide_ref) = refs[-3 - count : -3], refs[-3:]
    per_group, columns = t_ref.shape
    if count:
        weights = refs[0][...], refs[1][...]

    def body(i, here, squares):
        updated = t_ref[:, here]
        if count:
            updated += product(weights, jnp.concatenate([ref[:, here] for ref in x_refs], axis=0))
        out_ref[:, here] = updated
        return squares + jnp.sum(updated * updated, axis=1, keepdims=True)

    squares = loop(columns, 7, body, jnp.zeros((per_group, 1), jnp.float32))
    spread = jnp.broadcast_to(squares, (per_group, per_group))
    row = jnp.sum(jnp.where(diagonal(per_group), spread, 0.0), axis=0, keepdims=True)
    squares_ref[...] = row
    wide_ref[...] = jnp.broadcast_to(row, wide_ref.shape)


def rest_part(partly, weights, blocks):
    return pl.pallas_call(
        functools.partial(rest_kernel, len(blocks)),
        in_specs=[in_vmem] * (1 + len(weights) + len(blocks)),
        out_specs=[in_vmem] * 3,
        out_shape=[
            jax.ShapeDtypeStruct(partly.shape, jnp.float32),
            jax.ShapeDtypeStruct((1, partly.shape[0]), jnp.float32),
            jax.ShapeDtypeStruct((8, partly.shape[0]), jnp.float32),
        ],
        compiler_params=params,
        name="rest_part",
    )(partly, *weights, *blocks)


def diagonal(count):
    down = lax.broadcasted_iota(jnp.int32, (count, count), 0)
    across = lax.broadcasted_iota(jnp.int32, (count, count), 1)
    return down == across


def finish_kernel(features, count, updated_ref, *refs):
    squares_refs, (out_ref, scaled, sems) = refs[:count], refs[count:]
    per_group, columns = updated_ref.shape
    squares = squares_refs[0][:1]
    for ref in squares_refs[1:]:
        squares += ref[:1]
    spread = jnp.broadcast_to(scale_of(squares, features), (per_group, per_group))
    scale = jnp.sum(jnp.where(diagonal(per_group), spread, 0.0), axis=1, keepdims=True)
    tile = tile_of(columns, 4)
    copies = []
    for i in range(columns // tile):
        here = pl.ds(i * tile, tile)
        scaled[:, here] = updated_ref[:, here] * scale
        copies.append(pltpu.make_async_copy(scaled.at[:, here], out_ref.at[:, here], sems.at[i]))
        copies[-1].start()
    for copy in copies:
        copy.wait()


def finish(updated, squares, features):
    count = len(squares)
    return pl.pallas_call(
        functools.partial(finish_kernel, features, count),
        in_specs=[in_vmem] * (1 + count),
        out_specs=anywhere,
        out_shape=jax.ShapeDtypeStruct(updated.shape, jnp.float32),
        scratch_shapes=[
            pltpu.VMEM(updated.shape, jnp.float32),
            pltpu.SemaphoreType.DMA((updated.shape[1] // tile_of(updated.shape[1], 4),)),
        ],
        compiler_params=params,
        name="finish",
    )(updated, *squares)


def exchange(array, axis, step):
    return lax.ppermute(array, axis, [(i, i ^ step) for i in range(lax.axis_size(axis))])


def terms(array, axis, together):
    size = lax.axis_size(axis)
    if size & (size - 1):
        return [lax.psum(array, axis)]
    parts, step = [array], 1
    while step < size:
        array = sum(parts[1:], parts[0])
        width = min(1 << together, size // step)
        parts = [array] + [exchange(array, axis, step * k) for k in range(1, width)]
        step *= width
    return parts


def flipped_terms(array, wide):
    comp, feat = lax.axis_size("comp"), lax.axis_size("feat")
    if comp % 2 or comp & (comp - 1) or feat & (feat - 1):
        return terms(array, "feat", 2)
    widths, step = [], 1
    while step < feat:
        widths.append(min(4, feat // step))
        step *= widths[-1]
    parts, step = [array], 1
    for stage, width in enumerate(widths):
        if stage:
            array = sum((part[:1] for part in parts[1:]), parts[0][:1])
            wide = jnp.broadcast_to(array, wide.shape)
        flip = int(stage + 1 < len(widths) or len(widths) % 2 == 0)
        parts = [] if flip else [array]
        for k in range(0 if flip else 1, width):
            pairs = [
                (i * feat + j, (i ^ flip) * feat + (j ^ (k * step))) for i in range(comp) for j in range(feat)
            ]
            parts.append(lax.ppermute(wide if k == width - 1 else array, ("comp", "feat"), pairs))
        step *= width
    return parts


def gather(own):
    size = lax.axis_size("comp")
    if size & (size - 1):
        arrays, group = lax.all_gather(own, "comp"), lax.axis_index("comp")
        return {step: arrays[owner(group, step, size)] for step in range(1, size)}
    return {step: exchange(own, "comp", step) for step in range(1, size)}


def shards(samples, start_vectors):
    comp = lax.axis_size("comp")
    feat = lax.axis_size("feat")
    sample = samples[0]
    rows = sample.shape[0]
    features = sample.shape[1] * feat
    even = comp & (comp - 1) == 0

    blocks = {step: exchange(start_vectors, "comp", step) for step in range(2, comp, 2)} if even else gather(start_vectors)
    projected, vectors, sample = project(
        *(pltpu.with_memory_space_constraint(array, pltpu.HBM) for array in (start_vectors, sample))
    )
    if even and comp > 1:
        blocks[1] = exchange(vectors, "comp", 1)
    parts = terms(projected, "feat", 1)
    projected = sum(parts[1:], parts[0])
    if even:
        others = {step: exchange(projected, "comp", step) for step in range(1, comp, 2)}
    else:
        others = gather(projected)
    near = [1][: comp - 1]
    far = list(range(2, comp))

    def of(arrays, steps):
        return [arrays[step] for step in steps]

    partly = first_part(projected, sample, vectors, near, of(others, near), of(blocks, near), features)
    if even:
        for step in range(2, comp, 2):
            blocks[step], others[1] = lax.optimization_barrier((blocks[step], others[1]))
            blocks[step + 1] = exchange(blocks[step], "comp", 1)
            others[step] = exchange(others[step + 1], "comp", 1)
    projected, partly = lax.optimization_barrier((projected, partly))
    weights = couple(projected, far, of(others, far), rows, features) if far else []
    updated, squares, wide = rest_part(partly, weights, of(blocks, far))
    return finish(updated, flipped_terms(squares, wide), features)


def solution(mesh):
    in_specs = (P(None, None, "feat"), P("comp", "feat"))
    out_specs = P("comp", "feat")
    return jax.shard_map(shards, mesh=mesh, in_specs=in_specs, out_specs=out_specs, check_vma=False)
```

```python
import functools

import jax
import jax.numpy as jnp
from jax import lax
from jax.experimental import pallas as pl
from jax.experimental.pallas import tpu as pltpu
from jax.sharding import PartitionSpec as P

step_rate = 0.1
epsilon = 1e-06
lanes = 128
block_rows = 16
in_vmem = pl.BlockSpec(memory_space=pltpu.VMEM)
anywhere = pl.BlockSpec(memory_space=pl.ANY)
params = pltpu.CompilerParams(vmem_limit_bytes=16 << 20)


def tile_of(columns, most):
    if columns % lanes:
        return columns
    units = columns // lanes
    return lanes * max(u for u in range(1, most + 1) if units % u == 0)


def halves(array):
    top = array.astype(jnp.bfloat16)
    return top, (array - top.astype(jnp.float32)).astype(jnp.bfloat16)


def product(left, right, transposed=False):
    dims = (((1,), (1 if transposed else 0,)), ((), ()))
    dot = functools.partial(lax.dot_general, dimension_numbers=dims, preferred_element_type=jnp.float32)
    left_top, left_rest = left if isinstance(left, tuple) else halves(left)
    right_top, right_rest = halves(right)
    rows = left_top.shape[0]
    both = dot(jnp.concatenate([left_top, left_rest], axis=0), right_top)
    return both[:rows] + (both[rows:] + dot(left_top, right_rest))


def scale_of(squares, features):
    return lax.rsqrt(squares / features + epsilon)


def loop(columns, most, body, init):
    tile = tile_of(columns, most)
    return lax.fori_loop(0, columns // tile, lambda i, c: body(i, pl.ds(pl.multiple_of(i * tile, tile), tile), c), init, unroll=True)


def project_kernel(x_hbm, s_hbm, out_ref, x_ref, s_ref, sems):
    per_group, columns = x_ref.shape
    rows = s_ref.shape[0]

    def copies(i, here):
        return (
            pltpu.make_async_copy(x_hbm.at[:, here], x_ref.at[:, here], sems.at[0, i]),
            pltpu.make_async_copy(s_hbm.at[:, here], s_ref.at[:, here], sems.at[1, i]),
        )

    def begin(i, here, carry):
        for copy in copies(i, here):
            copy.start()
        return carry

    def body(i, here, carry):
        for copy in copies(i, here):
            copy.wait()
        x = x_ref[:, here]
        projected, squares = carry
        projected += product(x, s_ref[:, here], transposed=True)
        return projected, squares + jnp.sum(x * x, axis=1, keepdims=True)

    loop(columns, 4, begin, 0)
    zeros = jnp.zeros((per_group, rows), jnp.float32), jnp.zeros((per_group, 1), jnp.float32)
    projected, squares = loop(columns, 4, body, zeros)
    out_ref[:, :rows] = projected
    out_ref[:, rows:] = jnp.broadcast_to(squares, (per_group, out_ref.shape[1] - rows))


def project(x, sample):
    per_group, columns = x.shape
    rows = sample.shape[0]
    width = -(-(rows + 1) // lanes) * lanes
    return pl.pallas_call(
        project_kernel,
        in_specs=[anywhere] * 2,
        out_specs=[in_vmem] * 3,
        out_shape=[
            jax.ShapeDtypeStruct((per_group, width), jnp.float32),
            jax.ShapeDtypeStruct(x.shape, jnp.float32),
            jax.ShapeDtypeStruct(sample.shape, jnp.float32),
        ],
        scratch_shapes=[pltpu.SemaphoreType.DMA((2, columns // tile_of(columns, 4)))],
        compiler_params=params,
        name="project",
    )(x, sample)


def images_of(p_ref, rows, features):
    scale = scale_of(p_ref[:, rows : rows + 1], features)
    return p_ref[:, :rows] * scale, scale


def owner(group, step, size):
    return (group + step) % size if size & (size - 1) else group ^ step


def couplings(images, steps, projected_refs, features):
    group, size = lax.axis_index("comp"), lax.axis_size("comp")
    rows = images.shape[1]
    others = []
    for step, p_ref in zip(steps, projected_refs):
        other, scale = images_of(p_ref, rows, features)
        others.append(other * (scale * jnp.where(owner(group, step, size) < group, -step_rate / (features * rows), 0.0)))
    return product(images, jnp.concatenate(others, axis=0), transposed=True)


def first_kernel(features, steps, p_ref, s_ref, x_ref, *refs):
    count = len(steps)
    projected_refs, x_refs, out_ref = refs[:count], refs[count : 2 * count], refs[2 * count]
    rows = s_ref.shape[0]
    images, scale = images_of(p_ref, rows, features)
    shared = product(images, images * scale, transposed=True)
    later = lax.broadcasted_iota(jnp.int32, shared.shape, 0)
    earlier = lax.broadcasted_iota(jnp.int32, shared.shape, 1)
    weights = [images * (step_rate / rows), jnp.where(earlier < later, shared * (-step_rate / (features * rows)), 0.0)]
    if count:
        weights.append(couplings(images, steps, projected_refs, features))
    weights = halves(jnp.concatenate(weights, axis=1))

    def body(i, here, carry):
        x = x_ref[:, here]
        others = [ref[:, here] for ref in x_refs]
        out_ref[:, here] = scale * x + product(weights, jnp.concatenate([s_ref[:, here], x, *others], axis=0))
        return carry

    loop(x_ref.shape[1], 2, body, 0)


def first_part(projected, sample, x, steps, others, blocks, features):
    return pl.pallas_call(
        functools.partial(first_kernel, features, steps),
        in_specs=[in_vmem] * (3 + 2 * len(steps)),
        out_specs=in_vmem,
        out_shape=jax.ShapeDtypeStruct(x.shape, jnp.float32),
        compiler_params=params,
        name="first_part",
    )(projected, sample, x, *others, *blocks)


def couple_kernel(features, rows, steps, p_ref, *refs):
    projected_refs, (top_ref, rest_ref) = refs[:-2], refs[-2:]
    top_ref[...], rest_ref[...] = halves(couplings(images_of(p_ref, rows, features)[0], steps, projected_refs, features))


def couple(projected, steps, others, rows, features):
    per_group = projected.shape[0]
    return pl.pallas_call(
        functools.partial(couple_kernel, features, rows, steps),
        in_specs=[in_vmem] * (1 + len(steps)),
        out_specs=[in_vmem] * 2,
        out_shape=[jax.ShapeDtypeStruct((per_group, per_group * len(steps)), jnp.bfloat16)] * 2,
        compiler_params=params,
        cost_estimate=pl.CostEstimate(flops=9000000000, bytes_accessed=4 * projected.size, transcendentals=0),
        name="couple",
    )(projected, *others)


def rest_kernel(count, t_ref, *refs):
    x_refs, (out_ref, squares_ref, wide_ref) = refs[-3 - count : -3], refs[-3:]
    per_group, columns = t_ref.shape
    if count:
        weights = refs[0][...], refs[1][...]

    def body(i, here, squares):
        updated = t_ref[:, here]
        if count:
            updated += product(weights, jnp.concatenate([ref[:, here] for ref in x_refs], axis=0))
        out_ref[:, here] = updated
        return squares + jnp.sum(updated * updated, axis=1, keepdims=True)

    squares = loop(columns, 2, body, jnp.zeros((per_group, 1), jnp.float32))
    spread = jnp.broadcast_to(squares, (per_group, per_group))
    row = jnp.sum(jnp.where(diagonal(per_group), spread, 0.0), axis=0, keepdims=True)
    squares_ref[...] = row
    wide_ref[...] = jnp.broadcast_to(row, wide_ref.shape)


def rest_part(partly, weights, blocks):
    return pl.pallas_call(
        functools.partial(rest_kernel, len(blocks)),
        in_specs=[in_vmem] * (1 + len(weights) + len(blocks)),
        out_specs=[in_vmem] * 3,
        out_shape=[
            jax.ShapeDtypeStruct(partly.shape, jnp.float32),
            jax.ShapeDtypeStruct((1, partly.shape[0]), jnp.float32),
            jax.ShapeDtypeStruct((8, partly.shape[0]), jnp.float32),
        ],
        compiler_params=params,
        name="rest_part",
    )(partly, *weights, *blocks)


def diagonal(count):
    down = lax.broadcasted_iota(jnp.int32, (count, count), 0)
    across = lax.broadcasted_iota(jnp.int32, (count, count), 1)
    return down == across


def finish_kernel(features, count, updated_ref, *refs):
    squares_refs, (out_ref, scaled, sems) = refs[:count], refs[count:]
    per_group, columns = updated_ref.shape
    squares = squares_refs[0][:1]
    for ref in squares_refs[1:]:
        squares += ref[:1]
    spread = jnp.broadcast_to(scale_of(squares, features), (per_group, per_group))
    scale = jnp.sum(jnp.where(diagonal(per_group), spread, 0.0), axis=1, keepdims=True)
    copies = []
    for i, first in enumerate(range(0, per_group, block_rows)):
        here = pl.ds(first, min(block_rows, per_group - first))
        scaled[here, :] = updated_ref[here, :] * scale[first : first + block_rows]
        copies.append(pltpu.make_async_copy(scaled.at[here, :], out_ref.at[here, :], sems.at[i]))
        copies[-1].start()
    for copy in copies:
        copy.wait()


def finish(updated, squares, features):
    count = len(squares)
    return pl.pallas_call(
        functools.partial(finish_kernel, features, count),
        in_specs=[in_vmem] * (1 + count),
        out_specs=anywhere,
        out_shape=jax.ShapeDtypeStruct(updated.shape, jnp.float32),
        scratch_shapes=[
            pltpu.VMEM(updated.shape, jnp.float32),
            pltpu.SemaphoreType.DMA((-(-updated.shape[0] // block_rows),)),
        ],
        compiler_params=params,
        name="finish",
    )(updated, *squares)


def exchange(array, axis, step):
    return lax.ppermute(array, axis, [(i, i ^ step) for i in range(lax.axis_size(axis))])


def terms(array, axis, together):
    size = lax.axis_size(axis)
    if size & (size - 1):
        return [lax.psum(array, axis)]
    parts, step = [array], 1
    while step < size:
        array = sum(parts[1:], parts[0])
        width = min(1 << together, size // step)
        parts = [array] + [exchange(array, axis, step * k) for k in range(1, width)]
        step *= width
    return parts


def flipped_terms(array, wide):
    comp, feat = lax.axis_size("comp"), lax.axis_size("feat")
    if comp % 2 or comp & (comp - 1) or feat & (feat - 1):
        return terms(array, "feat", 2)
    widths, step = [], 1
    while step < feat:
        widths.append(min(4, feat // step))
        step *= widths[-1]
    parts, step = [array], 1
    for stage, width in enumerate(widths):
        if stage:
            array = sum((part[:1] for part in parts[1:]), parts[0][:1])
            wide = jnp.broadcast_to(array, wide.shape)
        flip = int(stage + 1 < len(widths) or len(widths) % 2 == 0)
        parts = [] if flip else [array]
        for k in range(0 if flip else 1, width):
            pairs = [
                (i * feat + j, (i ^ flip) * feat + (j ^ (k * step))) for i in range(comp) for j in range(feat)
            ]
            parts.append(lax.ppermute(wide if k == width - 1 else array, ("comp", "feat"), pairs))
        step *= width
    return parts


def gather(own):
    size = lax.axis_size("comp")
    if size & (size - 1):
        arrays, group = lax.all_gather(own, "comp"), lax.axis_index("comp")
        return {step: arrays[owner(group, step, size)] for step in range(1, size)}
    return {step: exchange(own, "comp", step) for step in range(1, size)}


def shards(samples, start_vectors):
    comp = lax.axis_size("comp")
    feat = lax.axis_size("feat")
    sample = samples[0]
    rows = sample.shape[0]
    features = sample.shape[1] * feat
    even = comp & (comp - 1) == 0

    blocks = {step: exchange(start_vectors, "comp", step) for step in range(2, comp, 2)} if even else gather(start_vectors)
    projected, vectors, sample = project(
        *(pltpu.with_memory_space_constraint(array, pltpu.HBM) for array in (start_vectors, sample))
    )
    if even and comp > 1:
        blocks[1] = exchange(vectors, "comp", 1)
    parts = terms(projected, "feat", 1)
    projected = sum(parts[1:], parts[0])
    if even:
        others = {step: exchange(projected, "comp", step) for step in range(1, comp, 2)}
    else:
        others = gather(projected)
    near = [1][: comp - 1]
    far = list(range(2, comp))

    def of(arrays, steps):
        return [arrays[step] for step in steps]

    partly = first_part(projected, sample, vectors, near, of(others, near), of(blocks, near), features)
    if even:
        for step in range(2, comp, 2):
            blocks[step], others[1] = lax.optimization_barrier((blocks[step], others[1]))
            blocks[step + 1] = exchange(blocks[step], "comp", 1)
            others[step] = exchange(others[step + 1], "comp", 1)
    projected, partly = lax.optimization_barrier((projected, partly))
    weights = couple(projected, far, of(others, far), rows, features) if far else []
    updated, squares, wide = rest_part(partly, weights, of(blocks, far))
    return finish(updated, flipped_terms(squares, wide), features)


def solution(mesh):
    in_specs = (P(None, None, "feat"), P("comp", "feat"))
    out_specs = P("comp", "feat")
    return jax.shard_map(shards, mesh=mesh, in_specs=in_specs, out_specs=out_specs, check_vma=False)
```

```python
import functools

import jax
import jax.numpy as jnp
from jax import lax
from jax.experimental import pallas as pl
from jax.experimental.pallas import tpu as pltpu
from jax.sharding import PartitionSpec as P

step_rate = 0.1
epsilon = 1e-06
lanes = 128
block_rows = 8
in_vmem = pl.BlockSpec(memory_space=pltpu.VMEM)
anywhere = pl.BlockSpec(memory_space=pl.ANY)
params = pltpu.CompilerParams(vmem_limit_bytes=16 << 20)


def tile_of(columns, most):
    if columns % lanes:
        return columns
    units = columns // lanes
    return lanes * max(u for u in range(1, most + 1) if units % u == 0)


def halves(array):
    top = array.astype(jnp.bfloat16)
    return top, (array - top.astype(jnp.float32)).astype(jnp.bfloat16)


def product(left, right, transposed=False):
    dims = (((1,), (1 if transposed else 0,)), ((), ()))
    dot = functools.partial(lax.dot_general, dimension_numbers=dims, preferred_element_type=jnp.float32)
    left_top, left_rest = left if isinstance(left, tuple) else halves(left)
    right_top, right_rest = halves(right)
    rows = left_top.shape[0]
    both = dot(jnp.concatenate([left_top, left_rest], axis=0), right_top)
    return both[:rows] + (both[rows:] + dot(left_top, right_rest))


def scale_of(squares, features):
    return lax.rsqrt(squares / features + epsilon)


def loop(columns, most, body, init):
    tile = tile_of(columns, most)
    return lax.fori_loop(0, columns // tile, lambda i, c: body(i, pl.ds(pl.multiple_of(i * tile, tile), tile), c), init, unroll=True)


def project_kernel(x_hbm, s_hbm, out_ref, x_ref, s_ref, sems):
    per_group, columns = x_ref.shape
    rows = s_ref.shape[0]

    def copies(i, here):
        return (
            pltpu.make_async_copy(x_hbm.at[:, here], x_ref.at[:, here], sems.at[0, i]),
            pltpu.make_async_copy(s_hbm.at[:, here], s_ref.at[:, here], sems.at[1, i]),
        )

    def begin(i, here, carry):
        for copy in copies(i, here):
            copy.start()
        return carry

    def body(i, here, carry):
        for copy in copies(i, here):
            copy.wait()
        x = x_ref[:, here]
        projected, squares = carry
        projected += product(x, s_ref[:, here], transposed=True)
        return projected, squares + jnp.sum(x * x, axis=1, keepdims=True)

    loop(columns, 4, begin, 0)
    zeros = jnp.zeros((per_group, rows), jnp.float32), jnp.zeros((per_group, 1), jnp.float32)
    projected, squares = loop(columns, 4, body, zeros)
    out_ref[:, :rows] = projected
    out_ref[:, rows:] = jnp.broadcast_to(squares, (per_group, out_ref.shape[1] - rows))


def project(x, sample):
    per_group, columns = x.shape
    rows = sample.shape[0]
    width = -(-(rows + 1) // lanes) * lanes
    return pl.pallas_call(
        project_kernel,
        in_specs=[anywhere] * 2,
        out_specs=[in_vmem] * 3,
        out_shape=[
            jax.ShapeDtypeStruct((per_group, width), jnp.float32),
            jax.ShapeDtypeStruct(x.shape, jnp.float32),
            jax.ShapeDtypeStruct(sample.shape, jnp.float32),
        ],
        scratch_shapes=[pltpu.SemaphoreType.DMA((2, columns // tile_of(columns, 4)))],
        compiler_params=params,
        name="project",
    )(x, sample)


def images_of(p_ref, rows, features):
    scale = scale_of(p_ref[:, rows : rows + 1], features)
    return p_ref[:, :rows] * scale, scale


def owner(group, step, size):
    return (group + step) % size if size & (size - 1) else group ^ step


def couplings(images, steps, projected_refs, features):
    group, size = lax.axis_index("comp"), lax.axis_size("comp")
    rows = images.shape[1]
    others = []
    for step, p_ref in zip(steps, projected_refs):
        other, scale = images_of(p_ref, rows, features)
        others.append(other * (scale * jnp.where(owner(group, step, size) < group, -step_rate / (features * rows), 0.0)))
    return product(images, jnp.concatenate(others, axis=0), transposed=True)


def first_kernel(features, steps, p_ref, s_ref, x_ref, *refs):
    count = len(steps)
    projected_refs, x_refs, out_ref = refs[:count], refs[count : 2 * count], refs[2 * count]
    rows = s_ref.shape[0]
    images, scale = images_of(p_ref, rows, features)
    shared = product(images, images * scale, transposed=True)
    later = lax.broadcasted_iota(jnp.int32, shared.shape, 0)
    earlier = lax.broadcasted_iota(jnp.int32, shared.shape, 1)
    weights = [images * (step_rate / rows), jnp.where(earlier < later, shared * (-step_rate / (features * rows)), 0.0)]
    if count:
        weights.append(couplings(images, steps, projected_refs, features))
    weights = halves(jnp.concatenate(weights, axis=1))

    def body(i, here, carry):
        x = x_ref[:, here]
        others = [ref[:, here] for ref in x_refs]
        out_ref[:, here] = scale * x + product(weights, jnp.concatenate([s_ref[:, here], x, *others], axis=0))
        return carry

    loop(x_ref.shape[1], 4, body, 0)


def first_part(projected, sample, x, steps, others, blocks, features):
    return pl.pallas_call(
        functools.partial(first_kernel, features, steps),
        in_specs=[in_vmem] * (3 + 2 * len(steps)),
        out_specs=in_vmem,
        out_shape=jax.ShapeDtypeStruct(x.shape, jnp.float32),
        compiler_params=params,
        name="first_part",
    )(projected, sample, x, *others, *blocks)


def couple_kernel(features, rows, steps, p_ref, *refs):
    projected_refs, (top_ref, rest_ref) = refs[:-2], refs[-2:]
    top_ref[...], rest_ref[...] = halves(couplings(images_of(p_ref, rows, features)[0], steps, projected_refs, features))


def couple(projected, steps, others, rows, features):
    per_group = projected.shape[0]
    return pl.pallas_call(
        functools.partial(couple_kernel, features, rows, steps),
        in_specs=[in_vmem] * (1 + len(steps)),
        out_specs=[in_vmem] * 2,
        out_shape=[jax.ShapeDtypeStruct((per_group, per_group * len(steps)), jnp.bfloat16)] * 2,
        compiler_params=params,
        cost_estimate=pl.CostEstimate(flops=9000000000, bytes_accessed=4 * projected.size, transcendentals=0),
        name="couple",
    )(projected, *others)


def rest_kernel(count, t_ref, *refs):
    x_refs, (out_ref, squares_ref, wide_ref) = refs[-3 - count : -3], refs[-3:]
    per_group, columns = t_ref.shape
    if count:
        weights = refs[0][...], refs[1][...]

    def body(i, here, squares):
        updated = t_ref[:, here]
        if count:
            updated += product(weights, jnp.concatenate([ref[:, here] for ref in x_refs], axis=0))
        out_ref[:, here] = updated
        return squares + jnp.sum(updated * updated, axis=1, keepdims=True)

    squares = loop(columns, 4, body, jnp.zeros((per_group, 1), jnp.float32))
    spread = jnp.broadcast_to(squares, (per_group, per_group))
    row = jnp.sum(jnp.where(diagonal(per_group), spread, 0.0), axis=0, keepdims=True)
    squares_ref[...] = row
    wide_ref[...] = jnp.broadcast_to(row, wide_ref.shape)


def rest_part(partly, weights, blocks):
    return pl.pallas_call(
        functools.partial(rest_kernel, len(blocks)),
        in_specs=[in_vmem] * (1 + len(weights) + len(blocks)),
        out_specs=[in_vmem] * 3,
        out_shape=[
            jax.ShapeDtypeStruct(partly.shape, jnp.float32),
            jax.ShapeDtypeStruct((1, partly.shape[0]), jnp.float32),
            jax.ShapeDtypeStruct((8, partly.shape[0]), jnp.float32),
        ],
        compiler_params=params,
        name="rest_part",
    )(partly, *weights, *blocks)


def diagonal(count):
    down = lax.broadcasted_iota(jnp.int32, (count, count), 0)
    across = lax.broadcasted_iota(jnp.int32, (count, count), 1)
    return down == across


def finish_kernel(features, count, updated_ref, *refs):
    squares_refs, (out_ref, scaled, sems) = refs[:count], refs[count:]
    per_group, columns = updated_ref.shape
    squares = squares_refs[0][:1]
    for ref in squares_refs[1:]:
        squares += ref[:1]
    spread = jnp.broadcast_to(scale_of(squares, features), (per_group, per_group))
    scale = jnp.sum(jnp.where(diagonal(per_group), spread, 0.0), axis=1, keepdims=True)
    copies = []
    for i, first in enumerate(range(0, per_group, block_rows)):
        here = pl.ds(first, min(block_rows, per_group - first))
        scaled[here, :] = updated_ref[here, :] * scale[first : first + block_rows]
        copies.append(pltpu.make_async_copy(scaled.at[here, :], out_ref.at[here, :], sems.at[i]))
        copies[-1].start()
    for copy in copies:
        copy.wait()


def finish(updated, squares, features):
    count = len(squares)
    return pl.pallas_call(
        functools.partial(finish_kernel, features, count),
        in_specs=[in_vmem] * (1 + count),
        out_specs=anywhere,
        out_shape=jax.ShapeDtypeStruct(updated.shape, jnp.float32),
        scratch_shapes=[
            pltpu.VMEM(updated.shape, jnp.float32),
            pltpu.SemaphoreType.DMA((-(-updated.shape[0] // block_rows),)),
        ],
        compiler_params=params,
        name="finish",
    )(updated, *squares)


def exchange(array, axis, step):
    return lax.ppermute(array, axis, [(i, i ^ step) for i in range(lax.axis_size(axis))])


def terms(array, axis, together):
    size = lax.axis_size(axis)
    if size & (size - 1):
        return [lax.psum(array, axis)]
    parts, step = [array], 1
    while step < size:
        array = sum(parts[1:], parts[0])
        width = min(1 << together, size // step)
        parts = [array] + [exchange(array, axis, step * k) for k in range(1, width)]
        step *= width
    return parts


def flipped_terms(array, wide):
    comp, feat = lax.axis_size("comp"), lax.axis_size("feat")
    if comp % 2 or comp & (comp - 1) or feat & (feat - 1):
        return terms(array, "feat", 2)
    widths, step = [], 1
    while step < feat:
        widths.append(min(4, feat // step))
        step *= widths[-1]
    parts, step = [array], 1
    for stage, width in enumerate(widths):
        if stage:
            array = sum((part[:1] for part in parts[1:]), parts[0][:1])
            wide = jnp.broadcast_to(array, wide.shape)
        flip = int(stage + 1 < len(widths) or len(widths) % 2 == 0)
        parts = [] if flip else [array]
        for k in range(0 if flip else 1, width):
            pairs = [
                (i * feat + j, (i ^ flip) * feat + (j ^ (k * step))) for i in range(comp) for j in range(feat)
            ]
            parts.append(lax.ppermute(wide if k == width - 1 else array, ("comp", "feat"), pairs))
        step *= width
    return parts


def gather(own):
    size = lax.axis_size("comp")
    if size & (size - 1):
        arrays, group = lax.all_gather(own, "comp"), lax.axis_index("comp")
        return {step: arrays[owner(group, step, size)] for step in range(1, size)}
    return {step: exchange(own, "comp", step) for step in range(1, size)}


def shards(samples, start_vectors):
    comp = lax.axis_size("comp")
    feat = lax.axis_size("feat")
    sample = samples[0]
    rows = sample.shape[0]
    features = sample.shape[1] * feat
    even = comp & (comp - 1) == 0

    blocks = {step: exchange(start_vectors, "comp", step) for step in range(2, comp, 2)} if even else gather(start_vectors)
    projected, vectors, sample = project(
        *(pltpu.with_memory_space_constraint(array, pltpu.HBM) for array in (start_vectors, sample))
    )
    if even and comp > 1:
        blocks[1] = exchange(vectors, "comp", 1)
    parts = terms(projected, "feat", 1)
    projected = sum(parts[1:], parts[0])
    if even:
        others = {step: exchange(projected, "comp", step) for step in range(1, comp, 2)}
    else:
        others = gather(projected)
    near = [1][: comp - 1]
    far = list(range(2, comp))

    def of(arrays, steps):
        return [arrays[step] for step in steps]

    partly = first_part(projected, sample, vectors, near, of(others, near), of(blocks, near), features)
    if even:
        for step in range(2, comp, 2):
            blocks[step], others[1] = lax.optimization_barrier((blocks[step], others[1]))
            blocks[step + 1] = exchange(blocks[step], "comp", 1)
            others[step] = exchange(others[step + 1], "comp", 1)
    projected, partly = lax.optimization_barrier((projected, partly))
    weights = couple(projected, far, of(others, far), rows, features) if far else []
    updated, squares, wide = rest_part(partly, weights, of(blocks, far))
    return finish(updated, flipped_terms(squares, wide), features)


def solution(mesh):
    in_specs = (P(None, None, "feat"), P("comp", "feat"))
    out_specs = P("comp", "feat")
    return jax.shard_map(shards, mesh=mesh, in_specs=in_specs, out_specs=out_specs, check_vma=False)
```
